512 devices in a mesh: row: 16 (over z, core), col: 32 (over y, x).
Axes of the slice: x: 4, y: 8, z: 8, core: 2. Of those that a mesh axis runs over, the one named last changes fastest.
Arguments:
- joined_grad: bfloat16 [256, 1024, 384], P('row', 'col'), may hold values from -6 to 6
- join_weight: bfloat16 [1536, 384], replicated, may hold values from -0.15625 to 0.15625
- linear_first: bfloat16 [64, 384], replicated, may hold values from -0.75 to 0.75
- linear_second: bfloat16 [128, 384], replicated, may hold values from -0.5 to 0.5
- linear_third: bfloat16 [320, 384], replicated, may hold values from -0.3125 to 0.3125
- linear_fourth: bfloat16 [512, 384], replicated, may hold values from -0.25 to 0.25
- feature_second: bfloat16 [128, 512, 128], P('row', 'col'), may hold values from -6 to 6
- feature_third: bfloat16 [64, 256, 320], P('row', 'col'), may hold values from -6 to 6
- feature_fourth: bfloat16 [32, 128, 512], P('row', 'col'), may hold values from -6 to 6
- block_input: bfloat16 [256, 1024, 64], P('row', 'col'), may hold values from -36 to 36
- later_grad: bfloat16 [256, 1024, 64], P('row', 'col'), may hold values from -6 to 6
- norm_gain: float32 [64], replicated, may hold values from 0.1 to 1.9
- norm_shift: float32 [64], replicated, may hold values from -3 to 3
- expand_weight: bfloat16 [64, 256], replicated, may hold values from -0.75 to 0.75
- expand_bias: float32 [256], replicated, may hold values from -3 to 3
- depth_weight: float32 [9, 256], replicated, may hold values from -2 to 2
- depth_bias: float32 [256], replicated, may hold values from -3 to 3
- reduce_weight: bfloat16 [256, 64], replicated, may hold values from -0.375 to 0.375
- reduce_bias: float32 [64], replicated, may hold values from -3 to 3
Outputs:
- input_grad: bfloat16 [256, 1024, 64], P('row', 'col')
- second_grad: bfloat16 [128, 512, 128], P('row', 'col')
- third_grad: bfloat16 [64, 256, 320], P('row', 'col')
- fourth_grad: bfloat16 [32, 128, 512], P('row', 'col')
- linear_grads: float32 [393216], P(('row', 'col'))
- biases_grad: float32 [4, 384], replicated
- expand_grad: float32 [64, 256], replicated
- reduce_grad: float32 [256, 64], replicated
- depth_grad: float32 [9, 256], replicated
- hidden_grads: float32 [2, 256], replicated
- channel_grads: float32 [3, 64], replicated
The draws below stay inside these ranges and needn't reach their ends.
All inputs are finite; a program needn't handle non-finite values.
Results may differ from the reference program's by a relative error of at most 0.0083.
Values may be sent and summed in bfloat16 or wider, within the bound.
No kernel may reach another device: no remote copies, remote signals or barrier semaphores. Data moves between devices by JAX's collectives and lax.ppermute only.
A program may use at most 64 MiB of HBM per device.

```python
import math
import jax
import jax.numpy as jnp
from jax import lax

D1 = 64
D2 = 128
D3 = 320
D4 = 512
HID = 256
DEC = 384
H = 256
W = 1024


def draw_block_input(key, part):
    key = jax.random.fold_in(key, 11)
    key_values, key_channel, key_pixel = jax.random.split(key, 3)
    values = jnp.clip(jax.random.normal(key_values, (H, W, D1), jnp.float32), -6.0, 6.0)
    channel_scale = jnp.exp(jax.random.uniform(key_channel, (D1,), jnp.float32, math.log(0.3), math.log(3.0)))
    pixel_scale = jnp.exp(jax.random.uniform(key_pixel, (H, W, 1), jnp.float32, math.log(0.5), math.log(2.0)))
    return (values * channel_scale * pixel_scale).astype(jnp.bfloat16)


def block_levels(rng, shape, shards, smallest, largest):
    def one(axis_at, parts):
        heights = jax.random.uniform(jax.random.fold_in(jax.random.fold_in(rng, 6), axis_at), (parts,), jnp.float32, smallest / len(shards), largest / len(shards))
        return jnp.repeat(jnp.exp(heights), shape[axis_at] // parts).reshape((-1,) + (1,) * (len(shape) - axis_at - 1))

    loudness = one(*shards[0])
    for cut in shards[1:]:
        loudness = loudness * one(*cut)
    return loudness


def noise(key, shape, scale, reach, cuts=(), kind=jnp.bfloat16):
    loudness = block_levels(key, shape, cuts, -0.22, 0.18) if cuts else 1.0
    values = jax.random.normal(key, shape, jnp.float32) * scale * loudness
    return jnp.minimum(jnp.maximum(values, -reach), reach).astype(kind)


def setup_inputs(seed: int = 0) -> dict:
    arg_keys = jax.random.split(jax.random.key(seed), 20)
    return {
        "joined_grad": noise(arg_keys[0], (H, W, DEC), 1.0, 6.0, ((0, 16), (1, 32))),
        "join_weight": noise(arg_keys[1], (4 * DEC, DEC), (4 * DEC) ** -0.5, 0.15625),
        "linear_first": noise(arg_keys[2], (D1, DEC), D1 ** -0.5, 0.75),
        "linear_second": noise(arg_keys[3], (D2, DEC), D2 ** -0.5, 0.5),
        "linear_third": noise(arg_keys[4], (D3, DEC), D3 ** -0.5, 0.3125),
        "linear_fourth": noise(arg_keys[5], (D4, DEC), D4 ** -0.5, 0.25),
        "feature_second": noise(arg_keys[6], (H // 2, W // 2, D2), 1.0, 6.0, ((0, 16), (1, 32))),
        "feature_third": noise(arg_keys[7], (H // 4, W // 4, D3), 1.0, 6.0, ((0, 16), (1, 32))),
        "feature_fourth": noise(arg_keys[8], (H // 8, W // 8, D4), 1.0, 6.0, ((0, 16), (1, 32))),
        "block_input": draw_block_input(jax.random.fold_in(arg_keys[19], 71), 0),
        "later_grad": noise(arg_keys[10], (H, W, D1), 1.0, 6.0, ((0, 16), (1, 32))),
        "norm_gain": jnp.clip(1.0 + 0.18 * jax.random.normal(arg_keys[11], (D1,), jnp.float32), 0.1, 1.9),
        "norm_shift": noise(arg_keys[12], (D1,), 0.5, 3.0, (), jnp.float32),
        "expand_weight": noise(arg_keys[13], (D1, HID), D1 ** -0.5, 0.75),
        "expand_bias": noise(arg_keys[14], (HID,), 0.5, 3.0, (), jnp.float32),
        "depth_weight": noise(arg_keys[15], (9, HID), 9 ** -0.5, 2.0, (), jnp.float32),
        "depth_bias": noise(arg_keys[16], (HID,), 0.5, 3.0, (), jnp.float32),
        "reduce_weight": noise(arg_keys[17], (HID, D1), HID ** -0.5, 0.375),
        "reduce_bias": noise(arg_keys[18], (D1,), 0.5, 3.0, (), jnp.float32),
    }


norm_eps = 1e-06
inv_root_two = 0.7071067811865476
inv_root_tau = 0.3989422804014327

def interp_matrix(fine_count, coarse_count, factor):
    fine_pos = jnp.arange(fine_count).astype(jnp.float32)
    coordinate = jnp.maximum((fine_pos + 0.5) / factor - 0.5, 0.0)
    lower = jnp.floor(coordinate)
    weight = coordinate - lower
    upper = jnp.minimum(lower + 1.0, coarse_count - 1.0)
    coarse_pos = jnp.arange(coarse_count).astype(jnp.float32)
    return jnp.where(coarse_pos[None, :] == lower[:, None], 1.0 - weight[:, None], 0.0) + jnp.where(coarse_pos[None, :] == upper[:, None], weight[:, None], 0.0)

def contract_grid(grid, row_matrix, col_matrix):
    fine_rows = grid.shape[0]
    fine_cols = grid.shape[1]
    left_sum = jnp.dot(row_matrix.T.astype(jnp.bfloat16), grid.reshape(fine_rows, -1), preferred_element_type=jnp.float32)
    left_sum = left_sum.reshape(row_matrix.shape[1], fine_cols, grid.shape[2])
    return jnp.einsum('awc,wb->abc', left_sum, col_matrix, precision=lax.Precision.HIGHEST)

def layer_stats(source, gain, shift):
    values = source.astype(jnp.float32)
    center = lax.optimization_barrier(jnp.mean(values, -1, keepdims=True))
    spread = lax.optimization_barrier(jnp.mean(jnp.square(values - center), -1, keepdims=True))
    scaling = lax.rsqrt(spread + norm_eps)
    standard = (values - center) * scaling
    normed = (standard * gain + shift).astype(jnp.bfloat16)
    return (normed, standard, scaling)

def expand_rows(normed, weight, bias):
    shape = normed.shape
    result = jnp.dot(normed.reshape(-1, shape[-1]), weight, preferred_element_type=jnp.float32) + bias
    return result.astype(jnp.bfloat16).reshape(shape[0], shape[1], -1)

def gelu_parts(conv):
    cumulative = 0.5 * (1.0 + lax.erf(conv * inv_root_two))
    density = inv_root_tau * jnp.exp(-0.5 * conv * conv)
    return (conv * cumulative, cumulative + conv * density)

def reference(joined_grad, join_weight, linear_first, linear_second, linear_third, linear_fourth, feature_second, feature_third, feature_fourth, block_input, later_grad, norm_gain, norm_shift, expand_weight, expand_bias, depth_weight, depth_bias, reduce_weight, reduce_bias):
    normed, standard, scaling = layer_stats(block_input, norm_gain, norm_shift)
    hidden = expand_rows(normed, expand_weight, expand_bias)
    padded = jnp.pad(hidden, ((1, 1), (1, 1), (0, 0)))
    conv = jnp.zeros((H, W, HID), jnp.float32) + depth_bias
    for tap_index in range(9):
        offset_row = tap_index // 3
        offset_col = tap_index % 3
        conv = conv + depth_weight[tap_index] * padded[offset_row:offset_row + H, offset_col:offset_col + W]
    value, slope = gelu_parts(conv)
    activated = value.astype(jnp.bfloat16)
    reduced = jnp.dot(activated.reshape(-1, HID), reduce_weight, preferred_element_type=jnp.float32) + reduce_bias
    features = (block_input.reshape(-1, D1).astype(jnp.float32) + reduced).astype(jnp.bfloat16)
    pooled = [joined_grad]
    for scale_index in (1, 2, 3):
        factor = 2 ** scale_index
        row_matrix = interp_matrix(H, H // factor, factor)
        col_matrix = interp_matrix(W, W // factor, factor)
        pooled.append(contract_grid(joined_grad, row_matrix, col_matrix).astype(jnp.bfloat16))
    scale_base = 1.0 / math.sqrt(H * W)
    sources = (features, feature_second, feature_third, feature_fourth)
    projected = []
    weight_terms = []
    bias_terms = []
    for scale_index in range(4):
        block_weight = join_weight[scale_index * DEC:(scale_index + 1) * DEC]
        projection = jnp.dot(pooled[scale_index].reshape(-1, DEC), block_weight.T, preferred_element_type=jnp.float32).astype(jnp.bfloat16)
        factor_scale = 2 ** scale_index * scale_base
        source = sources[scale_index]
        source_flat = source.reshape(-1, source.shape[-1])
        weight_terms.append((jnp.dot(source_flat.T, projection, preferred_element_type=jnp.float32) * factor_scale).reshape(-1))
        bias_terms.append(lax.optimization_barrier(jnp.sum(projection, 0, dtype=jnp.float32)) * factor_scale)
        projected.append(projection)
    linear_grads = jnp.concatenate(weight_terms)
    biases_grad = jnp.stack(bias_terms)
    feature_grad = (jnp.dot(projected[0], linear_first.T, preferred_element_type=jnp.float32) + later_grad.reshape(-1, D1).astype(jnp.float32)).astype(jnp.bfloat16)
    second_grad = jnp.dot(projected[1], linear_second.T, preferred_element_type=jnp.float32).astype(jnp.bfloat16).reshape(H // 2, W // 2, D2)
    third_grad = jnp.dot(projected[2], linear_third.T, preferred_element_type=jnp.float32).astype(jnp.bfloat16).reshape(H // 4, W // 4, D3)
    fourth_grad = jnp.dot(projected[3], linear_fourth.T, preferred_element_type=jnp.float32).astype(jnp.bfloat16).reshape(H // 8, W // 8, D4)
    act_grad = jnp.dot(feature_grad, reduce_weight.T, preferred_element_type=jnp.float32).reshape(H, W, HID)
    pre_grad = (act_grad * slope).astype(jnp.bfloat16)
    reduce_grad = jnp.dot(activated.reshape(-1, HID).T, feature_grad, preferred_element_type=jnp.float32) * scale_base
    wide_grad = jnp.pad(pre_grad, ((1, 1), (1, 1), (0, 0)))
    depth_parts = []
    hidden_acc = jnp.zeros((H, W, HID), jnp.float32)
    for tap_index in range(9):
        offset_row = tap_index // 3
        offset_col = tap_index % 3
        window = padded[offset_row:offset_row + H, offset_col:offset_col + W]
        depth_parts.append(lax.optimization_barrier(jnp.sum(window.astype(jnp.float32) * pre_grad.astype(jnp.float32), (0, 1))) * scale_base)
        hidden_acc = hidden_acc + depth_weight[tap_index] * wide_grad[2 - offset_row:2 - offset_row + H, 2 - offset_col:2 - offset_col + W]
    depth_grad = jnp.stack(depth_parts)
    hidden_grad = hidden_acc.astype(jnp.bfloat16).reshape(-1, HID)
    expand_grad = jnp.dot(normed.reshape(-1, D1).T, hidden_grad, preferred_element_type=jnp.float32) * scale_base
    normed_grad = jnp.dot(hidden_grad, expand_weight.T, preferred_element_type=jnp.float32)
    standard_flat = standard.reshape(-1, D1)
    hidden_grads = jnp.stack([lax.optimization_barrier(jnp.sum(hidden_grad, 0, dtype=jnp.float32)) * scale_base, lax.optimization_barrier(jnp.sum(pre_grad.reshape(-1, HID), 0, dtype=jnp.float32)) * scale_base])
    channel_grads = jnp.stack([lax.optimization_barrier(jnp.sum(feature_grad, 0, dtype=jnp.float32)) * scale_base, lax.optimization_barrier(jnp.sum(normed_grad * standard_flat, 0)) * scale_base, lax.optimization_barrier(jnp.sum(normed_grad, 0)) * scale_base])
    scaled = normed_grad * norm_gain
    input_grad = (feature_grad.astype(jnp.float32) + scaling.reshape(-1, 1) * (scaled - lax.optimization_barrier(jnp.mean(scaled, -1, keepdims=True)) - standard_flat * lax.optimization_barrier(jnp.mean(scaled * standard_flat, -1, keepdims=True)))).astype(jnp.bfloat16).reshape(H, W, D1)
    return (input_grad, second_grad, third_grad, fourth_grad, linear_grads, biases_grad, expand_grad, reduce_grad, depth_grad, hidden_grads, channel_grads)
```

```python
import math

import jax
import jax.numpy as jnp
from jax import lax
from jax.sharding import PartitionSpec as P

D1 = 64
D2 = 128
D3 = 320
D4 = 512
HID = 256
DEC = 384
TH = 16
TW = 32


norm_eps = 1e-06
inv_root_two = 0.7071067811865476
inv_root_tau = 0.3989422804014327


def with_halo(shard, sides, width):
    for axis, dim in sides:
        devices, length = (lax.axis_size(axis), shard.shape[dim])
        up = [(i, (i + 1) % devices) for i in range(devices - 1)]
        down = [(j, i) for i, j in up]
        last = lax.slice_in_dim(shard, length - width, length, axis=dim)
        initial = lax.slice_in_dim(shard, 0, width, axis=dim)
        before = lax.ppermute(last, axis, up)
        after = lax.ppermute(initial, axis, down)
        shard = jnp.concatenate([before, shard, after], axis=dim)
    return shard


def interp_local(fine_start, fine_count, coarse_start, coarse_count, factor, coarse_total):
    fine_pos = (fine_start + jnp.arange(fine_count)).astype(jnp.float32)
    coordinate = jnp.maximum((fine_pos + 0.5) / factor - 0.5, 0.0)
    lower = jnp.floor(coordinate)
    weight = coordinate - lower
    upper = jnp.minimum(lower + 1.0, coarse_total - 1.0)
    coarse_pos = (coarse_start + jnp.arange(coarse_count)).astype(jnp.float32)
    return jnp.where(coarse_pos[None, :] == lower[:, None], 1.0 - weight[:, None], 0.0) + jnp.where(
        coarse_pos[None, :] == upper[:, None], weight[:, None], 0.0
    )


def contract_grid(grid, row_matrix, col_matrix):
    fine_rows = grid.shape[0]
    fine_cols = grid.shape[1]
    left_sum = jnp.dot(
        row_matrix.T.astype(jnp.bfloat16),
        grid.reshape(fine_rows, -1),
        preferred_element_type=jnp.float32,
    )
    left_sum = left_sum.reshape(row_matrix.shape[1], fine_cols, grid.shape[2])
    return jnp.einsum("awc,wb->abc", left_sum, col_matrix, precision=lax.Precision.HIGHEST)


def layer_stats(source, gain, shift):
    values = source.astype(jnp.float32)
    center = jnp.mean(values, -1, keepdims=True)
    spread = jnp.mean(jnp.square(values - center), -1, keepdims=True)
    scaling = lax.rsqrt(spread + norm_eps)
    standard = (values - center) * scaling
    normed = (standard * gain + shift).astype(jnp.bfloat16)
    return (normed, standard, scaling)


def expand_rows(normed, weight, bias):
    shape = normed.shape
    result = (
        jnp.dot(normed.reshape(-1, shape[-1]), weight, preferred_element_type=jnp.float32) + bias
    )
    return result.astype(jnp.bfloat16).reshape(shape[0], shape[1], -1)


def gelu_parts(conv):
    cumulative = 0.5 * (1.0 + lax.erf(conv * inv_root_two))
    density = inv_root_tau * jnp.exp(-0.5 * conv * conv)
    return (conv * cumulative, cumulative + conv * density)


def swap_cores(shard):
    devices = lax.axis_size("row")
    return lax.ppermute(shard, "row", [(i, i ^ 1) for i in range(devices)])


def sum_over_mesh(linear, small):
    rows = lax.axis_size("row")
    cols = lax.axis_size("col")
    chips = rows // 2
    core = lax.axis_index("row") % 2
    share = -(-small.size // (rows * 128)) * 128
    padded = jnp.pad(small, (0, rows * share - small.size)).reshape(chips, 2, share)
    both = jnp.concatenate([linear.reshape(chips, 2, -1), padded], axis=2)
    mine = lax.dynamic_index_in_dim(both, core, 1, False)
    other = lax.dynamic_index_in_dim(both, 1 - core, 1, False)
    summed = (mine + swap_cores(other)).reshape(chips, -1, 128)
    groups = [[2 * z + c for z in range(chips)] for c in range(2)]
    along_z = lax.all_to_all(summed, "row", 0, 0, tiled=True, axis_index_groups=groups)
    block = jnp.sum(along_z, 0).reshape(-1)
    lin_size = block.size - share
    out = jnp.concatenate(
        [
            block[:lin_size].reshape(cols, -1),
            jnp.broadcast_to(block[lin_size:], (cols, share)),
        ],
        axis=1,
    ).reshape(cols, -1, 128)
    along_cols = jnp.sum(lax.all_to_all(out, "col", 0, 0, tiled=True), 0).reshape(-1)
    lin_part = along_cols[: lin_size // cols]
    rest = jnp.broadcast_to(along_cols[lin_size // cols :].reshape(1, -1, 128), (rows, share // 128, 128))
    everything = lax.all_to_all(rest, "row", 0, 0, tiled=True).reshape(-1)
    return lin_part, everything[: small.size]


def local(
    joined_grad,
    join_weight,
    linear_first,
    linear_second,
    linear_third,
    linear_fourth,
    feature_second,
    feature_third,
    feature_fourth,
    block_input,
    later_grad,
    norm_gain,
    norm_shift,
    expand_weight,
    expand_bias,
    depth_weight,
    depth_bias,
    reduce_weight,
    reduce_bias,
):
    row_index = lax.axis_index("row")
    col_index = lax.axis_index("col")
    height = TH * lax.axis_size("row")
    width = TW * lax.axis_size("col")
    normed, standard, scaling = layer_stats(block_input, norm_gain, norm_shift)
    hidden = expand_rows(normed, expand_weight, expand_bias)
    padded = with_halo(hidden, (("row", 0), ("col", 1)), 1)
    conv = jnp.zeros((TH, TW, HID), jnp.float32) + depth_bias
    for tap_index in range(9):
        offset_row = tap_index // 3
        offset_col = tap_index % 3
        conv = (
            conv
            + depth_weight[tap_index]
            * padded[offset_row : offset_row + TH, offset_col : offset_col + TW]
        )
    value, slope = gelu_parts(conv)
    activated = value.astype(jnp.bfloat16)
    reduced = (
        jnp.dot(activated.reshape(-1, HID), reduce_weight, preferred_element_type=jnp.float32)
        + reduce_bias
    )
    features = (block_input.reshape(-1, D1).astype(jnp.float32) + reduced).astype(jnp.bfloat16)
    wide_cotangent = with_halo(joined_grad, (("row", 0), ("col", 1)), 4)
    pooled = [joined_grad]
    for scale_index in (1, 2, 3):
        factor = 2**scale_index
        coarse_rows = TH // factor
        coarse_cols = TW // factor
        row_matrix = interp_local(
            row_index * TH - 4,
            TH + 8,
            row_index * coarse_rows,
            coarse_rows,
            factor,
            height // factor,
        )
        col_matrix = interp_local(
            col_index * TW - 4,
            TW + 8,
            col_index * coarse_cols,
            coarse_cols,
            factor,
            width // factor,
        )
        pooled.append(contract_grid(wide_cotangent, row_matrix, col_matrix).astype(jnp.bfloat16))
    scale_base = 1.0 / math.sqrt(height * width)
    sources = (features, feature_second, feature_third, feature_fourth)
    projected = []
    weight_terms = []
    bias_terms = []
    for scale_index in range(4):
        block_weight = join_weight[scale_index * DEC : (scale_index + 1) * DEC]
        projection = jnp.dot(
            pooled[scale_index].reshape(-1, DEC), block_weight.T, preferred_element_type=jnp.float32
        ).astype(jnp.bfloat16)
        factor_scale = 2**scale_index * scale_base
        source = sources[scale_index]
        source_flat = source.reshape(-1, source.shape[-1])
        weight_terms.append(
            (
                jnp.dot(source_flat.T, projection, preferred_element_type=jnp.float32)
                * factor_scale
            ).reshape(-1)
        )
        bias_terms.append(jnp.sum(projection, 0, dtype=jnp.float32) * factor_scale)
        projected.append(projection)
    feature_grad = (
        jnp.dot(projected[0], linear_first.T, preferred_element_type=jnp.float32)
        + later_grad.reshape(-1, D1).astype(jnp.float32)
    ).astype(jnp.bfloat16)
    second_grad = (
        jnp.dot(projected[1], linear_second.T, preferred_element_type=jnp.float32)
        .astype(jnp.bfloat16)
        .reshape(TH // 2, TW // 2, D2)
    )
    third_grad = (
        jnp.dot(projected[2], linear_third.T, preferred_element_type=jnp.float32)
        .astype(jnp.bfloat16)
        .reshape(TH // 4, TW // 4, D3)
    )
    fourth_grad = (
        jnp.dot(projected[3], linear_fourth.T, preferred_element_type=jnp.float32)
        .astype(jnp.bfloat16)
        .reshape(TH // 8, TW // 8, D4)
    )
    act_grad = jnp.dot(feature_grad, reduce_weight.T, preferred_element_type=jnp.float32).reshape(
        TH, TW, HID
    )
    pre_grad = (act_grad * slope).astype(jnp.bfloat16)
    reduce_part = (
        jnp.dot(activated.reshape(-1, HID).T, feature_grad, preferred_element_type=jnp.float32)
        * scale_base
    )
    wide_grad = with_halo(pre_grad, (("row", 0), ("col", 1)), 1)
    depth_parts = []
    hidden_acc = jnp.zeros((TH, TW, HID), jnp.float32)
    for tap_index in range(9):
        offset_row = tap_index // 3
        offset_col = tap_index % 3
        window = padded[offset_row : offset_row + TH, offset_col : offset_col + TW]
        depth_parts.append(
            jnp.sum(window.astype(jnp.float32) * pre_grad.astype(jnp.float32), (0, 1)) * scale_base
        )
        hidden_acc = (
            hidden_acc
            + depth_weight[tap_index]
            * wide_grad[2 - offset_row : 2 - offset_row + TH, 2 - offset_col : 2 - offset_col + TW]
        )
    hidden_grad = hidden_acc.astype(jnp.bfloat16).reshape(-1, HID)
    expand_part = (
        jnp.dot(normed.reshape(-1, D1).T, hidden_grad, preferred_element_type=jnp.float32)
        * scale_base
    )
    normed_grad = jnp.dot(hidden_grad, expand_weight.T, preferred_element_type=jnp.float32)
    standard_flat = standard.reshape(-1, D1)
    hidden_part = jnp.stack(
        [
            jnp.sum(hidden_grad, 0, dtype=jnp.float32) * scale_base,
            jnp.sum(pre_grad.reshape(-1, HID), 0, dtype=jnp.float32) * scale_base,
        ]
    )
    channel_part = jnp.stack(
        [
            jnp.sum(feature_grad, 0, dtype=jnp.float32) * scale_base,
            jnp.sum(normed_grad * standard_flat, 0) * scale_base,
            jnp.sum(normed_grad, 0) * scale_base,
        ]
    )
    scaled = normed_grad * norm_gain
    input_grad = (
        (
            feature_grad.astype(jnp.float32)
            + scaling.reshape(-1, 1)
            * (
                scaled
                - jnp.mean(scaled, -1, keepdims=True)
                - standard_flat * jnp.mean(scaled * standard_flat, -1, keepdims=True)
            )
        )
        .astype(jnp.bfloat16)
        .reshape(TH, TW, D1)
    )
    parts = (
        jnp.stack(bias_terms),
        expand_part,
        reduce_part,
        jnp.stack(depth_parts),
        hidden_part,
        channel_part,
    )
    linear_grads, flat = sum_over_mesh(
        jnp.concatenate(weight_terms), jnp.concatenate([part.reshape(-1) for part in parts])
    )
    summed = []
    start = 0
    for part in parts:
        summed.append(flat[start : start + part.size].reshape(part.shape))
        start += part.size
    return (
        input_grad,
        second_grad,
        third_grad,
        fourth_grad,
        linear_grads,
        summed[0],
        summed[1],
        summed[2],
        summed[3],
        summed[4],
        summed[5],
    )


def solution(mesh):
    return jax.shard_map(
        local,
        mesh=mesh,
        in_specs=(
            P("row", "col", None),
            P(),
            P(),
            P(),
            P(),
            P(),
            P("row", "col", None),
            P("row", "col", None),
            P("row", "col", None),
            P("row", "col", None),
            P("row", "col", None),
            P(),
            P(),
            P(),
            P(),
            P(),
            P(),
            P(),
            P(),
        ),
        out_specs=(
            P("row", "col", None),
            P("row", "col", None),
            P("row", "col", None),
            P("row", "col", None),
            P(("row", "col")),
            P(),
            P(),
            P(),
            P(),
            P(),
            P(),
        ),
        check_vma=False,
    )
```

```python
import functools
import math

import jax
import jax.numpy as jnp
from jax import lax
from jax.experimental import pallas as pl
from jax.experimental.pallas import tpu as pltpu
from jax.sharding import PartitionSpec as P

D1 = 64
D2 = 128
D3 = 320
D4 = 512
HID = 256
DEC = 384
TH = 16
TW = 32

EDGE = 4
ROWS = TH + 2 * EDGE
PITCH = 48
GROUP = 2 * EDGE
COARSE = (128, 32, 8)
BLOCK = 192
SHARE = 24

norm_eps = 1e-06
inv_root_two = 0.7071067811865476
inv_root_tau = 0.3989422804014327


def nt(left, right):
    return lax.dot_general(left, right, (((1,), (1,)), ((), ())), preferred_element_type=jnp.float32)


def tn(left, right):
    return lax.dot_general(left, right, (((0,), (0,)), ((), ())), preferred_element_type=jnp.float32)


def nn(left, right):
    return jnp.dot(left, right, preferred_element_type=jnp.float32)


def place(position):
    row = jnp.floor((position + 0.5) * (1.0 / PITCH))
    col = position - PITCH * row
    return row - EDGE, jnp.where(col < 40.0, col, col - PITCH)


def pool_matrix(scale_index, row_index, col_index, height, width):
    factor = 2**scale_index
    coarse_rows, coarse_cols = TH // factor, TW // factor
    count = coarse_rows * coarse_cols
    position = lax.broadcasted_iota(jnp.int32, (1, ROWS * PITCH), 1).astype(jnp.float32)
    row, col = place(position)
    target = lax.broadcasted_iota(jnp.int32, (count, 1), 0).astype(jnp.float32)
    target_row = jnp.floor((target + 0.5) * (1.0 / coarse_cols))
    target_col = target - coarse_cols * target_row
    row0 = (row_index * TH).astype(jnp.float32)
    col0 = (col_index * TW).astype(jnp.float32)
    at_row = jnp.clip((row + row0 + 0.5) * (1.0 / factor) - 0.5, 0.0, height // factor - 1.0)
    at_col = jnp.clip((col + col0 + 0.5) * (1.0 / factor) - 0.5, 0.0, width // factor - 1.0)
    at_row = at_row - row0 * (1.0 / factor)
    at_col = at_col - col0 * (1.0 / factor)
    weight = jnp.maximum(1.0 - jnp.abs(at_row - target_row), 0.0) * jnp.maximum(
        1.0 - jnp.abs(at_col - target_col), 0.0
    )
    return weight.astype(jnp.bfloat16)


def tile_kernel(
    height,
    width,
    joined_ref,
    pair_ref,
    top_ref,
    bottom_ref,
    side_ref,
    join_ref,
    first_ref,
    second_ref,
    third_ref,
    fourth_ref,
    feature2_ref,
    feature3_ref,
    feature4_ref,
    gain_ref,
    shift_ref,
    expand_ref,
    expand_bias_ref,
    depth_ref,
    depth_bias_ref,
    reduce_ref,
    reduce_bias_ref,
    input_grad_ref,
    grad2_ref,
    grad3_ref,
    grad4_ref,
    mine_ref,
    other_ref,
    wide_ref,
    wide_pair_ref,
    hid_ref,
    hid_before_ref,
    hid_after_ref,
    slope_ref,
    act_ref,
    pre_ref,
    pre_before_ref,
    pre_after_ref,
    hgrad_ref,
    linear_ref,
    rest_ref,
):
    row_index = lax.axis_index("row")
    col_index = lax.axis_index("col")
    scale_base = 1.0 / math.sqrt(height * width)

    wide_ref[EDGE : EDGE + TH, 0:TW] = joined_ref[...]
    wide_ref[0:EDGE, 0:TW] = top_ref[:, :, 0:DEC]
    wide_ref[EDGE + TH :, 0:TW] = bottom_ref[:, :, 0:DEC]
    wide_ref[:, TW:] = side_ref[:, :, 0:DEC]
    wide_pair_ref[EDGE : EDGE + TH, 0:TW] = pair_ref[...]
    wide_pair_ref[0:EDGE, 0:TW] = top_ref[:, :, DEC:]
    wide_pair_ref[EDGE + TH :, 0:TW] = bottom_ref[:, :, DEC:]
    wide_pair_ref[:, TW:] = side_ref[:, :, DEC:]
    rest_ref[...] = jnp.zeros_like(rest_ref)

    def keep_row(row, value):
        for piece in range(value.shape[1] // 128):
            rest_ref[row + piece : row + piece + 1, :] = value[:, 128 * piece : 128 * piece + 128]

    matrix = jnp.concatenate(
        [pool_matrix(k, row_index, col_index, height, width) for k in (1, 2, 3)], axis=0
    )
    pooled = nn(matrix, wide_ref[...].reshape(ROWS * PITCH, DEC)).astype(jnp.bfloat16)
    start = 0
    base = D1
    for k, linear, feature, grad in (
        (1, second_ref, feature2_ref, grad2_ref),
        (2, third_ref, feature3_ref, grad3_ref),
        (3, fourth_ref, feature4_ref, grad4_ref),
    ):
        count = COARSE[k - 1]
        channels = linear.shape[0]
        projection = nt(pooled[start : start + count], join_ref[k * DEC : (k + 1) * DEC, :]).astype(
            jnp.bfloat16
        )
        grad[...] = nt(projection, linear[...]).astype(jnp.bfloat16)
        linear_ref[base : base + channels, :] = tn(feature[...], projection) * (2**k * scale_base)
        keep_row(
            3 * k,
            jnp.sum(projection.astype(jnp.float32), 0, keepdims=True) * (2**k * scale_base),
        )
        start += count
        base += channels

    values = wide_pair_ref[2:22, :, 0:D1].reshape(20 * PITCH, D1).astype(jnp.float32)
    center = jnp.mean(values, -1, keepdims=True)
    offset = values - center
    spread = jnp.mean(jnp.square(offset), -1, keepdims=True)
    scaling = lax.rsqrt(spread + norm_eps)
    standard = offset * scaling
    normed = (standard * gain_ref[...] + shift_ref[...]).astype(jnp.bfloat16)

    def inside(first, rows):
        position = lax.broadcasted_iota(jnp.int32, (rows * PITCH, 1), 0).astype(jnp.float32)
        row, col = place(position + first * PITCH)
        row = row + (row_index * TH).astype(jnp.float32)
        col = col + (col_index * TW).astype(jnp.float32)
        good = (row >= 0.0) & (row < height) & (col >= 0.0) & (col < width)
        return jnp.where(good, 1.0, 0.0)

    hidden = (nn(normed, expand_ref[...]) + expand_bias_ref[...]).astype(jnp.bfloat16)
    hid_ref[...] = (hidden.astype(jnp.float32) * inside(2, 20)).reshape(20, PITCH, HID)

    def shift_hidden(i, carry):
        row = hid_ref[i]
        hid_before_ref[i] = pltpu.roll(row, 1, 0)
        hid_after_ref[i] = pltpu.roll(row, PITCH - 1, 0)
        return carry

    lax.fori_loop(0, 20, shift_hidden, 0)
    hid_refs = (hid_before_ref, hid_ref, hid_after_ref)

    def conv_row(i, carry):
        conv = jnp.broadcast_to(depth_bias_ref[...], (PITCH, HID))
        for a in range(3):
            for b in range(3):
                conv = conv + depth_ref[3 * a + b : 3 * a + b + 1, :] * hid_refs[b][i + a]
        cumulative = 0.5 * (1.0 + lax.erf(conv * inv_root_two))
        density = inv_root_tau * jnp.exp(-0.5 * conv * conv)
        act_ref[i] = (conv * cumulative).astype(jnp.bfloat16)
        slope_ref[i] = cumulative + conv * density
        return carry

    lax.fori_loop(0, 18, conv_row, 0)

    def own(value, rows):
        first = (rows - TH) // 2
        channels = value.shape[-1]
        return value.reshape(rows, PITCH, channels)[first : first + TH, 0:TW].reshape(
            TH * TW, channels
        )

    projection = nt(wide_ref[3:21].reshape(18 * PITCH, DEC), join_ref[0:DEC, :]).astype(jnp.bfloat16)
    later = wide_pair_ref[3:21, :, D1:].reshape(18 * PITCH, D1).astype(jnp.float32)
    feature_grad = (nt(projection, first_ref[...]) + later).astype(jnp.bfloat16)
    act_grad = nt(feature_grad, reduce_ref[...])
    pre_grad = (act_grad * slope_ref[...].reshape(18 * PITCH, HID)).astype(jnp.bfloat16)
    pre_ref[...] = (pre_grad.astype(jnp.float32) * inside(3, 18)).reshape(18, PITCH, HID)

    activated = act_ref[1:17, 0:TW, :].reshape(TH * TW, HID)
    own_projection = own(projection, 18)
    own_grad = own(feature_grad, 18)
    own_block = pair_ref[:, :, 0:D1].reshape(TH * TW, D1).astype(jnp.float32)
    features = (own_block + (nn(activated, reduce_ref[...]) + reduce_bias_ref[...])).astype(
        jnp.bfloat16
    )
    linear_ref[0:D1, :] = tn(features, own_projection) * scale_base
    keep_row(0, jnp.sum(own_projection.astype(jnp.float32), 0, keepdims=True) * scale_base)
    reduce_part = tn(own_grad, activated) * scale_base

    def shift_pre(i, carry):
        row = pre_ref[i]
        pre_before_ref[i] = pltpu.roll(row, 1, 0)
        pre_after_ref[i] = pltpu.roll(row, PITCH - 1, 0)
        return carry

    lax.fori_loop(0, 18, shift_pre, 0)
    pre_refs = (pre_after_ref, pre_ref, pre_before_ref)

    def fold(value):
        return jnp.sum(value.reshape(TW // 8, 8, HID), 0)

    def grad_row(i, sums):
        total = jnp.zeros((TW, HID), jnp.float32)
        center_row = pre_ref[i + 1, 0:TW, :]
        taps = []
        for a in range(3):
            for b in range(3):
                tap = 3 * a + b
                total = total + depth_ref[tap : tap + 1, :] * pre_refs[b][i + 2 - a, 0:TW, :]
                taps.append(sums[tap] + fold(hid_refs[b][i + 1 + a, 0:TW, :] * center_row))
        rounded = total.astype(jnp.bfloat16)
        hgrad_ref[i] = rounded
        taps.append(sums[9] + fold(rounded.astype(jnp.float32)))
        taps.append(sums[10] + fold(center_row))
        return tuple(taps)

    sums = lax.fori_loop(0, TH, grad_row, (jnp.zeros((8, HID), jnp.float32),) * 11)
    for n in range(11):
        keep_row(12 + 2 * n, jnp.sum(sums[n], 0, keepdims=True) * scale_base)

    hidden_grad = hgrad_ref[...].reshape(TH * TW, HID)
    own_normed = own(normed, 20)
    own_standard = own(standard, 20)
    own_scaling = own(jnp.broadcast_to(scaling, (20 * PITCH, D1)), 20)
    expand_part = tn(own_normed, hidden_grad) * scale_base
    normed_grad = nt(hidden_grad, expand_ref[...])
    fgrad = own_grad.astype(jnp.float32)
    for n, value in enumerate((fgrad, normed_grad * own_standard, normed_grad)):
        rest_ref[34 + n : 35 + n, 0:D1] = jnp.sum(value, 0, keepdims=True) * scale_base
    scaled = normed_grad * gain_ref[...]
    input_grad = fgrad + own_scaling * (
        scaled
        - jnp.mean(scaled, -1, keepdims=True)
        - own_standard * jnp.mean(scaled * own_standard, -1, keepdims=True)
    )
    input_grad_ref[...] = input_grad.astype(jnp.bfloat16).reshape(TH, TW, D1)

    def block_rows(r):
        pieces = [linear_ref[64 * r : 64 * r + 64, 128 * j : 128 * j + 128] for j in range(3)]
        lanes = slice(0, 128) if r < 8 else slice(128, 256)
        first = 8 * (r % 8)
        pieces.append(expand_part[first : first + 8, lanes])
        pieces.append(reduce_part[first : first + 8, lanes])
        pieces.append(rest_ref[8 * r : 8 * r + 8, :])
        return pieces

    even_core = row_index % 2 == 0
    for z in range(8):
        at = 0
        for even, odd in zip(block_rows(2 * z), block_rows(2 * z + 1)):
            size = even.shape[0]
            mine_ref[z, at : at + size, :] = jnp.where(even_core, even, odd)
            other_ref[z, at : at + size, :] = jnp.where(even_core, odd, even)
            at += size


def tile_pass(height, width, *operands):
    sds = jax.ShapeDtypeStruct
    bf16, f32 = jnp.bfloat16, jnp.float32
    vmem = pltpu.VMEM
    return pl.pallas_call(
        functools.partial(tile_kernel, height, width),
        out_shape=(
            sds((TH, TW, D1), bf16),
            sds((COARSE[0], D2), bf16),
            sds((COARSE[1], D3), bf16),
            sds((COARSE[2], D4), bf16),
            sds((8, BLOCK + SHARE, 128), f32),
            sds((8, BLOCK + SHARE, 128), f32),
        ),
        in_specs=[pl.BlockSpec(memory_space=vmem)] * len(operands),
        out_specs=(pl.BlockSpec(memory_space=vmem),) * 6,
        scratch_shapes=[
            vmem((ROWS, PITCH, DEC), bf16),
            vmem((ROWS, PITCH, 2 * D1), bf16),
            vmem((20, PITCH, HID), f32),
            vmem((20, PITCH, HID), f32),
            vmem((20, PITCH, HID), f32),
            vmem((18, PITCH, HID), f32),
            vmem((18, PITCH, HID), bf16),
            vmem((18, PITCH, HID), f32),
            vmem((18, PITCH, HID), f32),
            vmem((18, PITCH, HID), f32),
            vmem((TH, TW, HID), bf16),
            vmem((D1 + D2 + D3 + D4, DEC), f32),
            vmem((128, 128), f32),
        ],
        compiler_params=pltpu.CompilerParams(vmem_limit_bytes=50 * 2**20),
        name="tile_pass",
    )(*operands)


def column_kernel(received_ref, out_ref, total_ref):
    total_ref[...] = jnp.sum(received_ref[...], 0)
    share = total_ref[BLOCK:, :]
    empty = jnp.zeros((2, 128), jnp.float32)
    for c in range(out_ref.shape[0]):
        for j in range(3):
            out_ref[c, 2 * j : 2 * j + 2, :] = total_ref[64 * j + 2 * c : 64 * j + 2 * c + 2, :]
        out_ref[c, 6:8, :] = empty
        out_ref[c, 8:, :] = share


def final_kernel(received_ref, linear_ref, out_ref):
    total = jnp.sum(received_ref[...], 0)
    for p in range(2):
        for j in range(3):
            linear_ref[3 * p + j : 3 * p + j + 1, :] = total[2 * j + p : 2 * j + p + 1, :]
    for r in range(out_ref.shape[0]):
        out_ref[r] = total[8:]


def small_kernel(all_ref, biases_ref, expand_ref, reduce_ref, depth_ref, hidden_ref, channel_ref, turn_ref):
    for r in range(16):
        lanes = slice(0, 128) if r < 8 else slice(128, 256)
        first = 8 * (r % 8)
        expand_ref[first : first + 8, lanes] = all_ref[r, 0:8, :]
        turn_ref[first : first + 8, lanes] = all_ref[r, 8:16, :]
    reduce_ref[...] = turn_ref[...].T

    def row(n):
        return all_ref[n // 8, 16 + n % 8 : 17 + n % 8, :]

    for k in range(4):
        for j in range(3):
            biases_ref[k : k + 1, 128 * j : 128 * j + 128] = row(3 * k + j)
    for t in range(9):
        for j in range(2):
            depth_ref[t : t + 1, 128 * j : 128 * j + 128] = row(12 + 2 * t + j)
    for t in range(2):
        for j in range(2):
            hidden_ref[t : t + 1, 128 * j : 128 * j + 128] = row(30 + 2 * t + j)
    for t in range(3):
        channel_ref[t : t + 1, :] = row(34 + t)[:, 0:D1]


def sum_over_mesh(mine, other):
    rows = lax.axis_size("row")
    cols = lax.axis_size("col")
    chips = rows // 2
    sds = jax.ShapeDtypeStruct
    f32 = jnp.float32
    received = lax.ppermute(other, "row", [(i, i ^ 1) for i in range(rows)])
    groups = [[2 * z + c for z in range(chips)] for c in range(2)]
    along_z = lax.all_to_all(mine + received, "row", 0, 0, tiled=True, axis_index_groups=groups)
    parts = pl.pallas_call(
        column_kernel,
        out_shape=sds((cols, 8 + SHARE, 128), f32),
        scratch_shapes=[pltpu.VMEM((BLOCK + SHARE, 128), f32)],
        name="column_parts",
    )(along_z)
    along_cols = lax.all_to_all(parts, "col", 0, 0, tiled=True)
    linear, share = pl.pallas_call(
        final_kernel,
        out_shape=(sds((6, 128), f32), sds((rows, SHARE, 128), f32)),
        name="final_sums",
    )(along_cols)
    everything = lax.all_to_all(share, "row", 0, 0, tiled=True)
    small = pl.pallas_call(
        small_kernel,
        out_shape=(
            sds((4, DEC), f32),
            sds((D1, HID), f32),
            sds((HID, D1), f32),
            sds((9, HID), f32),
            sds((2, HID), f32),
            sds((3, D1), f32),
        ),
        scratch_shapes=[pltpu.VMEM((D1, HID), f32)],
        name="small_sums",
    )(everything)
    return linear.reshape(-1), small


def swap_edges(before_edge, after_edge, axis):
    devices = lax.axis_size(axis)
    up = [(i, i + 1) for i in range(devices - 1)]
    down = [(j, i) for i, j in up]
    return lax.ppermute(after_edge, axis, up), lax.ppermute(before_edge, axis, down)


def local(
    joined_grad,
    join_weight,
    linear_first,
    linear_second,
    linear_third,
    linear_fourth,
    feature_second,
    feature_third,
    feature_fourth,
    block_input,
    later_grad,
    norm_gain,
    norm_shift,
    expand_weight,
    expand_bias,
    depth_weight,
    depth_bias,
    reduce_weight,
    reduce_bias,
):
    height = TH * lax.axis_size("row")
    width = TW * lax.axis_size("col")
    pair = jnp.concatenate([block_input, later_grad], axis=2)

    def lines(rows, cols):
        return jnp.concatenate([joined_grad[rows, cols], pair[rows, cols]], axis=2)

    everything = slice(None)
    top, bottom = swap_edges(
        lines(slice(0, EDGE), everything), lines(slice(TH - EDGE, TH), everything), "row"
    )

    def columns(cols):
        return jnp.concatenate([top[:, cols], lines(everything, cols), bottom[:, cols]], axis=0)

    left, right = swap_edges(columns(slice(0, EDGE)), columns(slice(TW - EDGE, TW)), "col")
    gap = jnp.zeros((ROWS, PITCH - TW - 2 * EDGE, left.shape[2]), left.dtype)
    side = jnp.concatenate([right, gap, left], axis=1)

    input_grad, grad2, grad3, grad4, mine, other = tile_pass(
        height,
        width,
        joined_grad,
        pair,
        top,
        bottom,
        side,
        join_weight,
        linear_first,
        linear_second,
        linear_third,
        linear_fourth,
        feature_second.reshape(-1, D2),
        feature_third.reshape(-1, D3),
        feature_fourth.reshape(-1, D4),
        norm_gain.reshape(1, -1),
        norm_shift.reshape(1, -1),
        expand_weight,
        expand_bias.reshape(1, -1),
        depth_weight,
        depth_bias.reshape(1, -1),
        reduce_weight,
        reduce_bias.reshape(1, -1),
    )
    linear_grads, small = sum_over_mesh(mine, other)
    return (
        input_grad,
        grad2.reshape(TH // 2, TW // 2, D2),
        grad3.reshape(TH // 4, TW // 4, D3),
        grad4.reshape(TH // 8, TW // 8, D4),
        linear_grads,
        *small,
    )


def solution(mesh):
    tiles = P("row", "col", None)
    return jax.shard_map(
        local,
        mesh=mesh,
        in_specs=(tiles,) + (P(),) * 5 + (tiles,) * 5 + (P(),) * 8,
        out_specs=(tiles,) * 4 + (P(("row", "col")),) + (P(),) * 6,
        check_vma=False,
    )
```

```python
import functools
import math

import jax
import jax.numpy as jnp
from jax import lax
from jax.experimental import pallas as pl
from jax.experimental.pallas import tpu as pltpu
from jax.sharding import PartitionSpec as P

D1 = 64
D2 = 128
D3 = 320
D4 = 512
HID = 256
DEC = 384
TH = 16
TW = 32

EDGE = 4
ROWS = TH + 2 * EDGE
PITCH = 48
GROUP = 2 * EDGE
COARSE = (128, 32, 8)
BLOCK = 192
SHARE = 24

norm_eps = 1e-06
inv_root_two = 0.7071067811865476
inv_root_tau = 0.3989422804014327


def nt(left, right):
    return lax.dot_general(left, right, (((1,), (1,)), ((), ())), preferred_element_type=jnp.float32)


def tn(left, right):
    return lax.dot_general(left, right, (((0,), (0,)), ((), ())), preferred_element_type=jnp.float32)


def nn(left, right):
    return jnp.dot(left, right, preferred_element_type=jnp.float32)


def place(position):
    row = jnp.floor((position + 0.5) * (1.0 / PITCH))
    col = position - PITCH * row
    return row - EDGE, jnp.where(col < 40.0, col, col - PITCH)


def pool_matrix(scale_index, row_index, col_index, height, width):
    factor = 2**scale_index
    coarse_rows, coarse_cols = TH // factor, TW // factor
    count = coarse_rows * coarse_cols
    position = lax.broadcasted_iota(jnp.int32, (1, ROWS * PITCH), 1).astype(jnp.float32)
    row, col = place(position)
    target = lax.broadcasted_iota(jnp.int32, (count, 1), 0).astype(jnp.float32)
    target_row = jnp.floor((target + 0.5) * (1.0 / coarse_cols))
    target_col = target - coarse_cols * target_row
    row0 = (row_index * TH).astype(jnp.float32)
    col0 = (col_index * TW).astype(jnp.float32)
    at_row = jnp.clip((row + row0 + 0.5) * (1.0 / factor) - 0.5, 0.0, height // factor - 1.0)
    at_col = jnp.clip((col + col0 + 0.5) * (1.0 / factor) - 0.5, 0.0, width // factor - 1.0)
    at_row = at_row - row0 * (1.0 / factor)
    at_col = at_col - col0 * (1.0 / factor)
    weight = jnp.maximum(1.0 - jnp.abs(at_row - target_row), 0.0) * jnp.maximum(
        1.0 - jnp.abs(at_col - target_col), 0.0
    )
    return weight.astype(jnp.bfloat16)


def tile_kernel(
    height,
    width,
    joined_ref,
    pair_ref,
    top_ref,
    bottom_ref,
    side_ref,
    join_ref,
    first_ref,
    second_ref,
    third_ref,
    fourth_ref,
    feature2_ref,
    feature3_ref,
    feature4_ref,
    gain_ref,
    shift_ref,
    expand_ref,
    expand_bias_ref,
    depth_ref,
    depth_bias_ref,
    reduce_ref,
    reduce_bias_ref,
    input_grad_ref,
    grad2_ref,
    grad3_ref,
    grad4_ref,
    mine_ref,
    other_ref,
    wide_ref,
    wide_pair_ref,
    hid_ref,
    hid_before_ref,
    hid_after_ref,
    slope_ref,
    act_ref,
    pre_ref,
    pre_before_ref,
    pre_after_ref,
    hgrad_ref,
    linear_ref,
    rest_ref,
):
    row_index = lax.axis_index("row")
    col_index = lax.axis_index("col")
    scale_base = 1.0 / math.sqrt(height * width)

    wide_ref[EDGE : EDGE + TH, 0:TW] = joined_ref[...]
    wide_ref[0:EDGE, 0:TW] = top_ref[:, :, 0:DEC]
    wide_ref[EDGE + TH :, 0:TW] = bottom_ref[:, :, 0:DEC]
    wide_ref[:, TW:] = side_ref[:, :, 0:DEC]
    wide_pair_ref[EDGE : EDGE + TH, 0:TW] = pair_ref[...]
    wide_pair_ref[0:EDGE, 0:TW] = top_ref[:, :, DEC:]
    wide_pair_ref[EDGE + TH :, 0:TW] = bottom_ref[:, :, DEC:]
    wide_pair_ref[:, TW:] = side_ref[:, :, DEC:]
    rest_ref[...] = jnp.zeros_like(rest_ref)

    def keep_row(row, value):
        for piece in range(value.shape[1] // 128):
            rest_ref[row + piece : row + piece + 1, :] = value[:, 128 * piece : 128 * piece + 128]

    matrix = jnp.concatenate(
        [pool_matrix(k, row_index, col_index, height, width) for k in (1, 2, 3)], axis=0
    )
    pooled = nn(matrix, wide_ref[...].reshape(ROWS * PITCH, DEC)).astype(jnp.bfloat16)
    start = 0
    base = D1
    for k, linear, feature, grad in (
        (1, second_ref, feature2_ref, grad2_ref),
        (2, third_ref, feature3_ref, grad3_ref),
        (3, fourth_ref, feature4_ref, grad4_ref),
    ):
        count = COARSE[k - 1]
        channels = linear.shape[0]
        projection = nt(pooled[start : start + count], join_ref[k * DEC : (k + 1) * DEC, :]).astype(
            jnp.bfloat16
        )
        grad[...] = nt(projection, linear[...]).astype(jnp.bfloat16)
        linear_ref[base : base + channels, :] = tn(feature[...], projection) * (2**k * scale_base)
        keep_row(
            3 * k,
            jnp.sum(projection.astype(jnp.float32), 0, keepdims=True) * (2**k * scale_base),
        )
        start += count
        base += channels

    values = wide_pair_ref[2:22, :, 0:D1].reshape(20 * PITCH, D1).astype(jnp.float32)
    center = jnp.mean(values, -1, keepdims=True)
    offset = values - center
    spread = jnp.mean(jnp.square(offset), -1, keepdims=True)
    scaling = lax.rsqrt(spread + norm_eps)
    standard = offset * scaling
    normed = (standard * gain_ref[...] + shift_ref[...]).astype(jnp.bfloat16)

    def inside(first, rows):
        position = lax.broadcasted_iota(jnp.int32, (rows * PITCH, 1), 0).astype(jnp.float32)
        row, col = place(position + first * PITCH)
        row = row + (row_index * TH).astype(jnp.float32)
        col = col + (col_index * TW).astype(jnp.float32)
        good = (row >= 0.0) & (row < height) & (col >= 0.0) & (col < width)
        return jnp.where(good, 1.0, 0.0)

    hidden = (nn(normed, expand_ref[...]) + expand_bias_ref[...]).astype(jnp.bfloat16)
    hid_ref[...] = (hidden.astype(jnp.float32) * inside(2, 20)).reshape(20, PITCH, HID)

    def shift_hidden(i, carry):
        row = hid_ref[i]
        hid_before_ref[i] = pltpu.roll(row, 1, 0)
        hid_after_ref[i] = pltpu.roll(row, PITCH - 1, 0)
        return carry

    lax.fori_loop(0, 20, shift_hidden, 0)
    hid_refs = (hid_before_ref, hid_ref, hid_after_ref)

    def conv_row(i, carry):
        conv = jnp.broadcast_to(depth_bias_ref[...], (PITCH, HID))
        for a in range(3):
            for b in range(3):
                conv = conv + depth_ref[3 * a + b : 3 * a + b + 1, :] * hid_refs[b][i + a]
        cumulative = 0.5 * (1.0 + lax.erf(conv * inv_root_two))
        density = inv_root_tau * jnp.exp(-0.5 * conv * conv)
        act_ref[i] = (conv * cumulative).astype(jnp.bfloat16)
        slope_ref[i] = cumulative + conv * density
        return carry

    lax.fori_loop(0, 18, conv_row, 0)

    def own(value, rows):
        first = (rows - TH) // 2
        channels = value.shape[-1]
        return value.reshape(rows, PITCH, channels)[first : first + TH, 0:TW].reshape(
            TH * TW, channels
        )

    projection = nt(wide_ref[3:21].reshape(18 * PITCH, DEC), join_ref[0:DEC, :]).astype(jnp.bfloat16)
    later = wide_pair_ref[3:21, :, D1:].reshape(18 * PITCH, D1).astype(jnp.float32)
    feature_grad = (nt(projection, first_ref[...]) + later).astype(jnp.bfloat16)
    act_grad = nn(feature_grad, reduce_ref[...])
    pre_grad = (act_grad * slope_ref[...].reshape(18 * PITCH, HID)).astype(jnp.bfloat16)
    pre_ref[...] = (pre_grad.astype(jnp.float32) * inside(3, 18)).reshape(18, PITCH, HID)

    activated = act_ref[1:17, 0:TW, :].reshape(TH * TW, HID)
    own_projection = own(projection, 18)
    own_grad = own(feature_grad, 18)
    own_block = pair_ref[:, :, 0:D1].reshape(TH * TW, D1).astype(jnp.float32)
    features = (own_block + (nt(activated, reduce_ref[...]) + reduce_bias_ref[...])).astype(
        jnp.bfloat16
    )
    linear_ref[0:D1, :] = tn(features, own_projection) * scale_base
    keep_row(0, jnp.sum(own_projection.astype(jnp.float32), 0, keepdims=True) * scale_base)
    reduce_part = tn(own_grad, activated) * scale_base

    def shift_pre(i, carry):
        row = pre_ref[i]
        pre_before_ref[i] = pltpu.roll(row, 1, 0)
        pre_after_ref[i] = pltpu.roll(row, PITCH - 1, 0)
        return carry

    lax.fori_loop(0, 18, shift_pre, 0)
    pre_refs = (pre_after_ref, pre_ref, pre_before_ref)

    def fold(value):
        return jnp.sum(value.reshape(TW // 8, 8, HID), 0)

    def grad_row(i, sums):
        total = jnp.zeros((TW, HID), jnp.float32)
        center_row = pre_ref[i + 1, 0:TW, :]
        taps = []
        for a in range(3):
            for b in range(3):
                tap = 3 * a + b
                total = total + depth_ref[tap : tap + 1, :] * pre_refs[b][i + 2 - a, 0:TW, :]
                taps.append(sums[tap] + fold(hid_refs[b][i + 1 + a, 0:TW, :] * center_row))
        rounded = total.astype(jnp.bfloat16)
        hgrad_ref[i] = rounded
        taps.append(sums[9] + fold(rounded.astype(jnp.float32)))
        taps.append(sums[10] + fold(center_row))
        return tuple(taps)

    sums = lax.fori_loop(0, TH, grad_row, (jnp.zeros((8, HID), jnp.float32),) * 11)
    for n in range(11):
        keep_row(12 + 2 * n, jnp.sum(sums[n], 0, keepdims=True) * scale_base)

    hidden_grad = hgrad_ref[...].reshape(TH * TW, HID)
    own_normed = own(normed, 20)
    own_standard = own(standard, 20)
    own_scaling = own(jnp.broadcast_to(scaling, (20 * PITCH, D1)), 20)
    expand_part = tn(own_normed, hidden_grad) * scale_base
    normed_grad = nt(hidden_grad, expand_ref[...])
    fgrad = own_grad.astype(jnp.float32)
    for n, value in enumerate((fgrad, normed_grad * own_standard, normed_grad)):
        rest_ref[34 + n : 35 + n, 0:D1] = jnp.sum(value, 0, keepdims=True) * scale_base
    scaled = normed_grad * gain_ref[...]
    input_grad = fgrad + own_scaling * (
        scaled
        - jnp.mean(scaled, -1, keepdims=True)
        - own_standard * jnp.mean(scaled * own_standard, -1, keepdims=True)
    )
    input_grad_ref[...] = input_grad.astype(jnp.bfloat16).reshape(TH, TW, D1)

    def block_rows(r):
        pieces = [linear_ref[64 * r : 64 * r + 64, 128 * j : 128 * j + 128] for j in range(3)]
        lanes = slice(0, 128) if r < 8 else slice(128, 256)
        first = 8 * (r % 8)
        pieces.append(expand_part[first : first + 8, lanes])
        pieces.append(reduce_part[first : first + 8, lanes])
        pieces.append(rest_ref[8 * r : 8 * r + 8, :])
        return pieces

    even_core = row_index % 2 == 0
    for z in range(8):
        at = 0
        for even, odd in zip(block_rows(2 * z), block_rows(2 * z + 1)):
            size = even.shape[0]
            mine_ref[z, at : at + size, :] = jnp.where(even_core, even, odd)
            other_ref[z, at : at + size, :] = jnp.where(even_core, odd, even)
            at += size


def tile_pass(height, width, *operands):
    sds = jax.ShapeDtypeStruct
    bf16, f32 = jnp.bfloat16, jnp.float32
    vmem = pltpu.VMEM
    return pl.pallas_call(
        functools.partial(tile_kernel, height, width),
        out_shape=(
            sds((TH, TW, D1), bf16),
            sds((COARSE[0], D2), bf16),
            sds((COARSE[1], D3), bf16),
            sds((COARSE[2], D4), bf16),
            sds((8, BLOCK + SHARE, 128), f32),
            sds((8, BLOCK + SHARE, 128), f32),
        ),
        in_specs=[pl.BlockSpec(memory_space=vmem)] * len(operands),
        out_specs=(pl.BlockSpec(memory_space=vmem),) * 6,
        scratch_shapes=[
            vmem((ROWS, PITCH, DEC), bf16),
            vmem((ROWS, PITCH, 2 * D1), bf16),
            vmem((20, PITCH, HID), f32),
            vmem((20, PITCH, HID), f32),
            vmem((20, PITCH, HID), f32),
            vmem((18, PITCH, HID), f32),
            vmem((18, PITCH, HID), bf16),
            vmem((18, PITCH, HID), f32),
            vmem((18, PITCH, HID), f32),
            vmem((18, PITCH, HID), f32),
            vmem((TH, TW, HID), bf16),
            vmem((D1 + D2 + D3 + D4, DEC), f32),
            vmem((128, 128), f32),
        ],
        compiler_params=pltpu.CompilerParams(vmem_limit_bytes=50 * 2**20),
        name="tile_pass",
    )(*operands)


def column_kernel(received_ref, out_ref, total_ref):
    total_ref[...] = jnp.sum(received_ref[:, 0:BLOCK, :].astype(jnp.float32), 0)
    share = jnp.sum(received_ref[:, BLOCK:, :].astype(jnp.float32), 0)
    share = share[0:SHARE] + share[SHARE:]
    empty = jnp.zeros((2, 128), jnp.float32)
    for c in range(out_ref.shape[0]):
        for j in range(3):
            out_ref[c, 2 * j : 2 * j + 2, :] = total_ref[64 * j + 2 * c : 64 * j + 2 * c + 2, :]
        out_ref[c, 6:8, :] = empty
        out_ref[c, 8:, :] = share


def final_kernel(received_ref, linear_ref, out_ref):
    total = jnp.sum(received_ref[...], 0)
    for p in range(2):
        for j in range(3):
            linear_ref[3 * p + j : 3 * p + j + 1, :] = total[2 * j + p : 2 * j + p + 1, :]
    for r in range(out_ref.shape[0]):
        out_ref[r] = total[8:]


def small_kernel(all_ref, biases_ref, expand_ref, reduce_ref, depth_ref, hidden_ref, channel_ref):
    for r in range(16):
        lanes = slice(0, 128) if r < 8 else slice(128, 256)
        first = 8 * (r % 8)
        expand_ref[first : first + 8, lanes] = all_ref[r, 0:8, :]
        reduce_ref[first : first + 8, lanes] = all_ref[r, 8:16, :]

    def row(n):
        return all_ref[n // 8, 16 + n % 8 : 17 + n % 8, :]

    for k in range(4):
        for j in range(3):
            biases_ref[k : k + 1, 128 * j : 128 * j + 128] = row(3 * k + j)
    for t in range(9):
        for j in range(2):
            depth_ref[t : t + 1, 128 * j : 128 * j + 128] = row(12 + 2 * t + j)
    for t in range(2):
        for j in range(2):
            hidden_ref[t : t + 1, 128 * j : 128 * j + 128] = row(30 + 2 * t + j)
    for t in range(3):
        channel_ref[t : t + 1, :] = row(34 + t)[:, 0:D1]


def in_vmem(kernel, name, out_shape, *operands, scratch=()):
    vmem = pl.BlockSpec(memory_space=pltpu.VMEM)
    return pl.pallas_call(
        kernel,
        out_shape=out_shape,
        in_specs=[vmem] * len(operands),
        out_specs=jax.tree.map(lambda _: vmem, out_shape),
        scratch_shapes=scratch,
        compiler_params=pltpu.CompilerParams(vmem_limit_bytes=16 * 2**20),
        name=name,
    )(*operands)


def chip_kernel(mine_ref, received_ref, out_ref):
    total = mine_ref[:, 0:BLOCK, :] + received_ref[:, 0:BLOCK, :]
    out_ref[:, 0:BLOCK, :] = total.astype(jnp.bfloat16)
    share = mine_ref[:, BLOCK:, :] + received_ref[:, BLOCK:, :]
    high = share.astype(jnp.bfloat16).astype(jnp.float32)
    out_ref[:, BLOCK:, :] = jnp.concatenate([high, share - high], axis=1).astype(jnp.bfloat16)


def sum_over_mesh(mine, other):
    rows = lax.axis_size("row")
    cols = lax.axis_size("col")
    chips = rows // 2
    sds = jax.ShapeDtypeStruct
    f32 = jnp.float32
    received = lax.ppermute(other, "row", [(i, i ^ 1) for i in range(rows)])
    groups = [[2 * z + c for z in range(chips)] for c in range(2)]
    chip = in_vmem(
        chip_kernel,
        "chip_sums",
        sds((chips, BLOCK + 2 * SHARE, 128), jnp.bfloat16),
        mine,
        received,
    )
    along_z = lax.all_to_all(chip, "row", 0, 0, tiled=True, axis_index_groups=groups)
    parts = in_vmem(
        column_kernel,
        "column_parts",
        sds((cols, 8 + SHARE, 128), f32),
        along_z,
        scratch=[pltpu.VMEM((BLOCK, 128), f32)],
    )
    along_cols = lax.all_to_all(parts, "col", 0, 0, tiled=True)
    linear, share = in_vmem(
        final_kernel, "final_sums", (sds((6, 128), f32), sds((rows, SHARE, 128), f32)), along_cols
    )
    everything = lax.all_to_all(share, "row", 0, 0, tiled=True)
    biases, expand, reduce, depth, hidden, channel = in_vmem(
        small_kernel,
        "small_sums",
        (
            sds((4, DEC), f32),
            sds((D1, HID), f32),
            sds((D1, HID), f32),
            sds((9, HID), f32),
            sds((2, HID), f32),
            sds((3, D1), f32),
        ),
        everything,
    )
    return linear.reshape(-1), (biases, expand, reduce.T, depth, hidden, channel)


def swap_edges(first_edge, last_edge, axis):
    devices = lax.axis_size(axis)
    even = lax.axis_index(axis) % 2 == 0
    near = [(i, i ^ 1) for i in range(devices)]
    far = [(i, i + 1) for i in range(1, devices - 1, 2)]
    far = far + [(j, i) for i, j in far]
    from_far = lax.ppermute(jnp.where(even, first_edge, last_edge), axis, far)
    from_near = lax.ppermute(jnp.where(even, last_edge, first_edge), axis, near)
    return jnp.where(even, from_far, from_near), jnp.where(even, from_near, from_far)


def local(
    joined_grad,
    join_weight,
    linear_first,
    linear_second,
    linear_third,
    linear_fourth,
    feature_second,
    feature_third,
    feature_fourth,
    block_input,
    later_grad,
    norm_gain,
    norm_shift,
    expand_weight,
    expand_bias,
    depth_weight,
    depth_bias,
    reduce_weight,
    reduce_bias,
):
    height = TH * lax.axis_size("row")
    width = TW * lax.axis_size("col")
    pair = jnp.concatenate([block_input, later_grad], axis=2)

    def lines(rows, cols):
        return jnp.concatenate([joined_grad[rows, cols], pair[rows, cols]], axis=2)

    everything = slice(None)
    top, bottom = swap_edges(
        lines(slice(0, EDGE), everything), lines(slice(TH - EDGE, TH), everything), "row"
    )

    def columns(cols):
        return jnp.concatenate([top[:, cols], lines(everything, cols), bottom[:, cols]], axis=0)

    left, right = swap_edges(columns(slice(0, EDGE)), columns(slice(TW - EDGE, TW)), "col")
    gap = jnp.zeros((ROWS, PITCH - TW - 2 * EDGE, left.shape[2]), left.dtype)
    side = jnp.concatenate([right, gap, left], axis=1)

    input_grad, grad2, grad3, grad4, mine, other = tile_pass(
        height,
        width,
        joined_grad,
        pair,
        top,
        bottom,
        side,
        join_weight,
        linear_first,
        linear_second,
        linear_third,
        linear_fourth,
        feature_second.reshape(-1, D2),
        feature_third.reshape(-1, D3),
        feature_fourth.reshape(-1, D4),
        norm_gain.reshape(1, -1),
        norm_shift.reshape(1, -1),
        expand_weight,
        expand_bias.reshape(1, -1),
        depth_weight,
        depth_bias.reshape(1, -1),
        reduce_weight.T,
        reduce_bias.reshape(1, -1),
    )
    linear_grads, small = sum_over_mesh(mine, other)
    return (
        input_grad,
        grad2.reshape(TH // 2, TW // 2, D2),
        grad3.reshape(TH // 4, TW // 4, D3),
        grad4.reshape(TH // 8, TW // 8, D4),
        linear_grads,
        *small,
    )


def solution(mesh):
    tiles = P("row", "col", None)
    return jax.shard_map(
        local,
        mesh=mesh,
        in_specs=(tiles,) + (P(),) * 5 + (tiles,) * 5 + (P(),) * 8,
        out_specs=(tiles,) * 4 + (P(("row", "col")),) + (P(),) * 6,
        check_vma=False,
    )
```

```python
import functools
import math

import jax
import jax.numpy as jnp
from jax import lax
from jax.experimental import pallas as pl
from jax.experimental.pallas import tpu as pltpu
from jax.sharding import PartitionSpec as P

D1 = 64
D2 = 128
D3 = 320
D4 = 512
HID = 256
DEC = 384
TH = 16
TW = 32

EDGE = 4
ROWS = TH + 2 * EDGE
PITCH = 48
USED = 40
COARSE = (128, 32, 8)

XS = 4
NEAR = 16
LINEAR_ROWS = 96
PART_ROWS = LINEAR_ROWS + 16

norm_eps = 1e-06
inv_root_two = 0.7071067811865476
inv_root_tau = 0.3989422804014327


def nt(left, right):
    return lax.dot_general(left, right, (((1,), (1,)), ((), ())), preferred_element_type=jnp.float32)


def tn(left, right):
    return lax.dot_general(left, right, (((0,), (0,)), ((), ())), preferred_element_type=jnp.float32)


def nn(left, right):
    return jnp.dot(left, right, preferred_element_type=jnp.float32)


def rest_row(n):
    return 8 * (n // 4) + 4 * (n // 2 % 2) + n % 2


def place(position, pitch):
    row = jnp.floor((position + 0.5) * (1.0 / pitch))
    col = position - pitch * row
    return row - EDGE, jnp.where(col < TW + EDGE, col, col - USED)


def regroup(channels_last):
    source = lax.broadcasted_iota(jnp.int32, (128, 128), 0)
    target = lax.broadcasted_iota(jnp.int32, (128, 128), 1)
    wanted = (
        (target & 64)
        + 8 * (target & 6)
        + ((target & 32) >> 2)
        + ((target & 24) >> 2)
        + (target & 1)
    )
    moves = jnp.where(source == wanted, 1.0, 0.0).astype(jnp.bfloat16)
    pieces = []
    for first in range(0, channels_last.shape[1], 128):
        piece = channels_last[:, first : first + 128]
        size = piece.shape[1]
        pieces.append(nn(piece, moves[0:size, 0:size]))
    return jnp.concatenate(pieces, axis=1).astype(jnp.bfloat16)


def pool_matrix(scale_index, row_index, col_index, height, width):
    factor = 2**scale_index
    coarse_rows, coarse_cols = TH // factor, TW // factor
    count = coarse_rows * coarse_cols
    position = lax.broadcasted_iota(jnp.int32, (1, ROWS * PITCH), 1).astype(jnp.float32)
    row, col = place(position, PITCH)
    target = lax.broadcasted_iota(jnp.int32, (count, 1), 0).astype(jnp.float32)
    target_row = jnp.floor((target + 0.5) * (1.0 / coarse_cols))
    target_col = target - coarse_cols * target_row
    row0 = (row_index * TH).astype(jnp.float32)
    col0 = (col_index * TW).astype(jnp.float32)
    at_row = jnp.clip((row + row0 + 0.5) * (1.0 / factor) - 0.5, 0.0, height // factor - 1.0)
    at_col = jnp.clip((col + col0 + 0.5) * (1.0 / factor) - 0.5, 0.0, width // factor - 1.0)
    at_row = at_row - row0 * (1.0 / factor)
    at_col = at_col - col0 * (1.0 / factor)
    weight = jnp.maximum(1.0 - jnp.abs(at_row - target_row), 0.0) * jnp.maximum(
        1.0 - jnp.abs(at_col - target_col), 0.0
    )
    return weight.astype(jnp.bfloat16)


def tile_kernel(
    height,
    width,
    joined_ref,
    block_ref,
    later_ref,
    top_ref,
    bottom_ref,
    side_ref,
    join_ref,
    first_ref,
    second_ref,
    third_ref,
    fourth_ref,
    feature2_ref,
    feature3_ref,
    feature4_ref,
    gain_ref,
    shift_ref,
    expand_ref,
    expand_bias_ref,
    depth_ref,
    depth_bias_ref,
    reduce_ref,
    reduce_bias_ref,
    input_grad_ref,
    grad2_ref,
    grad3_ref,
    grad4_ref,
    mine_ref,
    other_ref,
    wide_ref,
    wide_pair_ref,
    hid_ref,
    hid_before_ref,
    hid_after_ref,
    slope_ref,
    act_ref,
    pre_ref,
    pre_before_ref,
    pre_after_ref,
    hgrad_ref,
    linear_ref,
    rest_ref,
):
    row_index = lax.axis_index("row")
    col_index = lax.axis_index("col")
    scale_base = 1.0 / math.sqrt(height * width)

    wide_ref[EDGE : EDGE + TH, 0:TW] = joined_ref[...]
    wide_ref[0:EDGE, 0:TW] = top_ref[:, :, 0:DEC]
    wide_ref[EDGE + TH :, 0:TW] = bottom_ref[:, :, 0:DEC]
    wide_ref[:, TW:] = side_ref[:, :, 0:DEC]
    wide_pair_ref[EDGE : EDGE + TH, 0:TW, 0:D1] = block_ref[...]
    wide_pair_ref[EDGE : EDGE + TH, 0:TW, D1:] = later_ref[...]
    wide_pair_ref[0:EDGE, 0:TW] = top_ref[:, :, DEC:]
    wide_pair_ref[EDGE + TH :, 0:TW] = bottom_ref[:, :, DEC:]
    wide_pair_ref[:, TW:] = side_ref[:, :, DEC:]
    rest_ref[...] = jnp.zeros_like(rest_ref)

    def keep_row(row, value):
        for piece in range(value.shape[1] // 128):
            at = rest_row(row + piece)
            rest_ref[at : at + 1, :] = value[:, 128 * piece : 128 * piece + 128]

    matrix = jnp.concatenate(
        [pool_matrix(k, row_index, col_index, height, width) for k in (1, 2, 3)], axis=0
    )
    pooled = nn(matrix, wide_ref[...].reshape(ROWS * PITCH, DEC)).astype(jnp.bfloat16)
    start = 0
    base = D1
    for k, linear, feature, grad in (
        (1, second_ref, feature2_ref, grad2_ref),
        (2, third_ref, feature3_ref, grad3_ref),
        (3, fourth_ref, feature4_ref, grad4_ref),
    ):
        count = COARSE[k - 1]
        channels = linear.shape[0]
        projection = nt(pooled[start : start + count], join_ref[k * DEC : (k + 1) * DEC, :]).astype(
            jnp.bfloat16
        )
        grad[...] = nt(projection, linear[...]).astype(jnp.bfloat16)
        linear_ref[base : base + channels, :] = tn(regroup(feature[...]), projection) * (2**k * scale_base)
        keep_row(
            3 * k,
            jnp.sum(projection.astype(jnp.float32), 0, keepdims=True) * (2**k * scale_base),
        )
        start += count
        base += channels

    values = wide_pair_ref[2:22, :, 0:D1].astype(jnp.float32)
    values = values[:, 0:USED].reshape(20 * USED, D1)
    center = jnp.mean(values, -1, keepdims=True)
    offset = values - center
    spread = jnp.mean(jnp.square(offset), -1, keepdims=True)
    scaling = lax.rsqrt(spread + norm_eps)
    standard = offset * scaling
    normed = (standard * gain_ref[...] + shift_ref[...]).astype(jnp.bfloat16)

    def inside(first, rows):
        position = lax.broadcasted_iota(jnp.int32, (rows * USED, 1), 0).astype(jnp.float32)
        row, col = place(position + first * USED, USED)
        row = row + (row_index * TH).astype(jnp.float32)
        col = col + (col_index * TW).astype(jnp.float32)
        good = (row >= 0.0) & (row < height) & (col >= 0.0) & (col < width)
        return jnp.where(good, 1.0, 0.0)

    hidden = (nn(normed, expand_ref[...]) + expand_bias_ref[...]).astype(jnp.bfloat16)
    hid_ref[...] = (hidden.astype(jnp.float32) * inside(2, 20)).reshape(20, USED, HID)

    def shift_hidden(i, carry):
        row = hid_ref[i]
        hid_before_ref[i] = pltpu.roll(row, 1, 0)
        hid_after_ref[i] = pltpu.roll(row, USED - 1, 0)
        return carry

    lax.fori_loop(0, 20, shift_hidden, 0)
    hid_refs = (hid_before_ref, hid_ref, hid_after_ref)

    def conv_row(i, carry):
        conv = jnp.broadcast_to(depth_bias_ref[...], (USED, HID))
        for a in range(3):
            for b in range(3):
                conv = conv + depth_ref[3 * a + b : 3 * a + b + 1, :] * hid_refs[b][i + a]
        cumulative = 0.5 * (1.0 + lax.erf(conv * inv_root_two))
        density = inv_root_tau * jnp.exp(-0.5 * conv * conv)
        act_ref[i] = (conv * cumulative)[0:TW].astype(jnp.bfloat16)
        slope_ref[i] = cumulative + conv * density
        return carry

    lax.fori_loop(0, 18, conv_row, 0)

    def own(value, rows, pitch):
        first = (rows - TH) // 2
        channels = value.shape[-1]
        return value.reshape(rows, pitch, channels)[first : first + TH, 0:TW].reshape(
            TH * TW, channels
        )

    projection = nt(wide_ref[3:21].reshape(18 * PITCH, DEC), join_ref[0:DEC, :]).astype(jnp.bfloat16)
    later = wide_pair_ref[3:21, :, D1:].reshape(18 * PITCH, D1).astype(jnp.float32)
    feature_grad = (nt(projection, first_ref[...]) + later).astype(jnp.bfloat16)
    act_grad = nn(feature_grad, reduce_ref[...])
    act_grad = act_grad.reshape(18, PITCH, HID)[:, 0:USED]
    pre_grad = (act_grad * slope_ref[...]).astype(jnp.bfloat16).astype(jnp.float32)
    pre_ref[...] = pre_grad * inside(3, 18).reshape(18, USED, 1)

    activated = act_ref[1:17].reshape(TH * TW, HID)
    own_projection = own(projection, 18, PITCH)
    own_grad = own(feature_grad, 18, PITCH)
    own_block = block_ref[...].reshape(TH * TW, D1).astype(jnp.float32)
    features = (own_block + (nt(activated, reduce_ref[...]) + reduce_bias_ref[...])).astype(
        jnp.bfloat16
    )
    linear_ref[0:D1, :] = tn(regroup(features), own_projection) * scale_base
    keep_row(0, jnp.sum(own_projection.astype(jnp.float32), 0, keepdims=True) * scale_base)
    reduce_part = tn(own_grad, activated) * scale_base

    def shift_pre(i, carry):
        row = pre_ref[i]
        pre_before_ref[i] = pltpu.roll(row, 1, 0)
        pre_after_ref[i] = pltpu.roll(row, USED - 1, 0)
        return carry

    lax.fori_loop(0, 18, shift_pre, 0)
    pre_refs = (pre_after_ref, pre_ref, pre_before_ref)

    def fold(value):
        return jnp.sum(value.reshape(TW // 8, 8, HID), 0)

    def grad_row(i, sums):
        total = jnp.zeros((TW, HID), jnp.float32)
        center_row = pre_ref[i + 1, 0:TW, :]
        taps = []
        for a in range(3):
            for b in range(3):
                tap = 3 * a + b
                total = total + depth_ref[tap : tap + 1, :] * pre_refs[b][i + 2 - a, 0:TW, :]
                taps.append(sums[tap] + fold(hid_refs[b][i + 1 + a, 0:TW, :] * center_row))
        rounded = total.astype(jnp.bfloat16)
        hgrad_ref[i] = rounded
        taps.append(sums[9] + fold(rounded.astype(jnp.float32)))
        taps.append(sums[10] + fold(center_row))
        return tuple(taps)

    sums = lax.fori_loop(0, TH, grad_row, (jnp.zeros((8, HID), jnp.float32),) * 11)
    for n in range(11):
        keep_row(12 + 2 * n, jnp.sum(sums[n], 0, keepdims=True) * scale_base)

    hidden_grad = hgrad_ref[...].reshape(TH * TW, HID)
    own_normed = own(normed.astype(jnp.float32), 20, USED).astype(jnp.bfloat16)
    own_standard = own(standard, 20, USED)
    own_scaling = own(jnp.broadcast_to(scaling, (20 * USED, D1)), 20, USED)
    expand_part = tn(own_normed, hidden_grad) * scale_base
    normed_grad = nt(hidden_grad, expand_ref[...])
    fgrad = own_grad.astype(jnp.float32)
    for n, value in enumerate((fgrad, normed_grad * own_standard, normed_grad)):
        at = rest_row(34 + n)
        rest_ref[at : at + 1, 0:D1] = jnp.sum(value, 0, keepdims=True) * scale_base
    scaled = normed_grad * gain_ref[...]
    input_grad = fgrad + own_scaling * (
        scaled
        - jnp.mean(scaled, -1, keepdims=True)
        - own_standard * jnp.mean(scaled * own_standard, -1, keepdims=True)
    )
    input_grad_ref[...] = input_grad.astype(jnp.bfloat16).reshape(TH, TW, D1)

    even_core = row_index % 2 == 0

    def keep(part, at, even, odd):
        mine_ref[part, at : at + 8, :] = jnp.where(even_core, even, odd)
        other_ref[part, at : at + 8, :] = jnp.where(even_core, odd, even)

    upper = lax.broadcasted_iota(jnp.int32, (8, 128), 0) < 4
    for part in range(NEAR):
        zl, within = part // 8, 8 * (part % 8)
        at = 0
        for zh in range(4):
            first = 128 * (2 * zh + zl) + within
            for j in range(3):
                lanes = slice(128 * j, 128 * j + 128)
                keep(
                    part,
                    at,
                    linear_ref[first : first + 8, lanes],
                    linear_ref[first + 64 : first + 72, lanes],
                )
                at += 8
        lanes = slice(0, 128) if part < 8 else slice(128, 256)
        expand = expand_part[within : within + 8, lanes]
        reduce = reduce_part[within : within + 8, lanes]
        keep(
            part,
            at,
            jnp.where(upper, expand, pltpu.roll(reduce, 4, 0)),
            jnp.where(upper, pltpu.roll(expand, 4, 0), reduce),
        )
        rest = rest_ref[8 * part : 8 * part + 8, :]
        keep(part, at + 8, rest, pltpu.roll(rest, 4, 0))


def border_kernel(
    joined_ref, block_ref, later_ref, far_ref, near_ref, joined_buf, block_buf, later_buf, sems
):
    copies = []
    for n, (source, target) in enumerate(
        ((joined_ref, joined_buf), (block_ref, block_buf), (later_ref, later_buf))
    ):
        for last in range(2):
            rows = slice(TH - EDGE, TH) if last else slice(0, EDGE)
            copy = pltpu.make_async_copy(source.at[rows], target.at[last], sems.at[2 * n + last])
            copy.start()
            copies.append(copy)
    for copy in copies:
        copy.wait()
    even = lax.axis_index("row") % 2 == 0
    for buf, lanes in (
        (joined_buf, slice(0, DEC)),
        (block_buf, slice(DEC, DEC + D1)),
        (later_buf, slice(DEC + D1, DEC + 2 * D1)),
    ):
        first = buf[0].astype(jnp.float32)
        last = buf[1].astype(jnp.float32)
        far_ref[:, :, lanes] = jnp.where(even, first, last).astype(jnp.bfloat16)
        near_ref[:, :, lanes] = jnp.where(even, last, first).astype(jnp.bfloat16)


def row_borders(joined, block, later):
    vmem = pl.BlockSpec(memory_space=pltpu.VMEM)
    out = jax.ShapeDtypeStruct((EDGE, TW, DEC + 2 * D1), jnp.bfloat16)
    return pl.pallas_call(
        border_kernel,
        out_shape=(out, out),
        in_specs=[pl.BlockSpec(memory_space=pltpu.HBM)] * 3,
        out_specs=(vmem, vmem),
        scratch_shapes=[pltpu.VMEM((2, EDGE) + a.shape[1:], a.dtype) for a in (joined, block, later)]
        + [pltpu.SemaphoreType.DMA((6,))],
        compiler_params=pltpu.CompilerParams(vmem_limit_bytes=56 * 2**20),
        name="row_borders",
    )(joined, block, later)


def tile_pass(height, width, *operands):
    sds = jax.ShapeDtypeStruct
    bf16, f32 = jnp.bfloat16, jnp.float32
    vmem = pltpu.VMEM
    return pl.pallas_call(
        functools.partial(tile_kernel, height, width),
        out_shape=(
            sds((TH, TW, D1), bf16),
            sds((COARSE[0], D2), bf16),
            sds((COARSE[1], D3), bf16),
            sds((COARSE[2], D4), bf16),
            sds((NEAR, PART_ROWS, 128), f32),
            sds((NEAR, PART_ROWS, 128), f32),
        ),
        in_specs=[pl.BlockSpec(memory_space=vmem)] * len(operands),
        out_specs=(pl.BlockSpec(memory_space=vmem),) * 6,
        scratch_shapes=[
            vmem((ROWS, PITCH, DEC), bf16),
            vmem((ROWS, PITCH, 2 * D1), bf16),
            vmem((20, USED, HID), f32),
            vmem((20, USED, HID), f32),
            vmem((20, USED, HID), f32),
            vmem((18, USED, HID), f32),
            vmem((18, TW, HID), bf16),
            vmem((18, USED, HID), f32),
            vmem((18, USED, HID), f32),
            vmem((18, USED, HID), f32),
            vmem((TH, TW, HID), bf16),
            vmem((D1 + D2 + D3 + D4, DEC), f32),
            vmem((128, 128), f32),
        ],
        compiler_params=pltpu.CompilerParams(vmem_limit_bytes=50 * 2**20),
        name="tile_pass",
    )(*operands)


def near_kernel(received_ref, out_ref):
    total = jnp.sum(received_ref[...].astype(jnp.float32), 0)
    share = total[LINEAR_ROWS : LINEAR_ROWS + 8]
    rest = total[LINEAR_ROWS + 8 :]
    rest = pltpu.roll(rest + pltpu.roll(rest, 4, 0), 6, 0)
    row = lax.broadcasted_iota(jnp.int32, (8, 128), 0)
    for zh in range(4):
        pieces = [total[24 * zh + 8 * j : 24 * zh + 8 * j + 8] for j in range(3)]
        for yh in range(4):
            part = rest
            for j in range(3):
                shift = (2 * j - 2 * yh) % 8
                moved = pltpu.roll(pieces[j], shift, 0) if shift else pieces[j]
                part = jnp.where((row >= 2 * j) & (row < 2 * j + 2), moved, part)
            out_ref[4 * zh + yh, 0:8, :] = part
            out_ref[4 * zh + yh, 8:16, :] = share


def final_kernel(received_ref, linear_ref, out_ref):
    total = jnp.sum(received_ref[...], 0)
    for p in range(2):
        for j in range(3):
            linear_ref[3 * p + j : 3 * p + j + 1, :] = total[2 * j + p : 2 * j + p + 1, :]
    rest = pltpu.roll(total[0:8], 2, 0)
    for n in range(out_ref.shape[0]):
        out_ref[n, 0:8, :] = total[8:16]
        out_ref[n, 8:16, :] = rest


def small_kernel(all_ref, biases_ref, expand_ref, reduce_ref, depth_ref, hidden_ref, channel_ref):
    upper = lax.broadcasted_iota(jnp.int32, (8, 128), 0) < 4
    for part in range(NEAR):
        lanes = slice(0, 128) if part < 8 else slice(128, 256)
        rows = slice(8 * (part % 8), 8 * (part % 8) + 8)
        even, odd = all_ref[2 * part, 0:8, :], all_ref[2 * part + 1, 0:8, :]
        expand_ref[rows, lanes] = jnp.where(upper, even, pltpu.roll(odd, 4, 0))
        reduce_ref[rows, lanes] = jnp.where(upper, pltpu.roll(even, 4, 0), odd)

    def row(n):
        return all_ref[n // 2, 8 + n % 2 : 9 + n % 2, :]

    for k in range(4):
        for j in range(3):
            biases_ref[k : k + 1, 128 * j : 128 * j + 128] = row(3 * k + j)
    for t in range(9):
        for j in range(2):
            depth_ref[t : t + 1, 128 * j : 128 * j + 128] = row(12 + 2 * t + j)
    for t in range(2):
        for j in range(2):
            hidden_ref[t : t + 1, 128 * j : 128 * j + 128] = row(30 + 2 * t + j)
    for t in range(3):
        channel_ref[t : t + 1, :] = row(34 + t)[:, 0:D1]


def in_vmem(kernel, name, out_shape, *operands, scratch=()):
    vmem = pl.BlockSpec(memory_space=pltpu.VMEM)
    return pl.pallas_call(
        kernel,
        out_shape=out_shape,
        in_specs=[vmem] * len(operands),
        out_specs=jax.tree.map(lambda _: vmem, out_shape),
        scratch_shapes=scratch,
        compiler_params=pltpu.CompilerParams(vmem_limit_bytes=16 * 2**20),
        name=name,
    )(*operands)


def chip_kernel(mine_ref, received_ref, out_ref):
    plain = LINEAR_ROWS + 8
    total = mine_ref[:, 0:plain, :] + received_ref[:, 0:plain, :]
    rest = mine_ref[:, plain:, :] + received_ref[:, plain:, :]
    high = rest.astype(jnp.bfloat16).astype(jnp.float32)
    row = lax.broadcasted_iota(jnp.int32, rest.shape, 1)
    low = jnp.where(row < 2, rest - high, 0.0)
    both = jnp.where(row < 2, high, pltpu.roll(low, 4, 1))
    out_ref[...] = jnp.concatenate([total, both], axis=1).astype(jnp.bfloat16)


def device_groups(chips, cols):
    half_z, half_y = range(chips // 2), range(cols // XS // 2)
    two, xs = range(2), range(XS)

    def device(zh, zl, core, yh, yl, x):
        return (2 * (2 * zh + zl) + core) * cols + XS * (2 * yh + yl) + x

    near = [
        [device(zh, zl, core, yh, yl, x) for zl in two for yl in two for x in xs]
        for core in two
        for zh in half_z
        for yh in half_y
    ]
    far = [
        [device(zh, zl, core, yh, yl, x) for zh in half_z for yh in half_y]
        for core in two
        for zl in two
        for yl in two
        for x in xs
    ]
    both = [
        [device(zh, zl, core, yh, yl, x) for zl in two for yl in two for x in xs for core in two]
        for zh in half_z
        for yh in half_y
    ]
    return near, far, both


def sum_over_mesh(mine, other):
    rows = lax.axis_size("row")
    cols = lax.axis_size("col")
    sds = jax.ShapeDtypeStruct
    f32 = jnp.float32
    near, far, both = device_groups(rows // 2, cols)

    def exchange(parts, groups):
        return lax.all_to_all(parts, ("row", "col"), 0, 0, tiled=True, axis_index_groups=groups)

    received = lax.ppermute(other, "row", [(i, i ^ 1) for i in range(rows)])
    chip = in_vmem(chip_kernel, "chip_sums", sds(mine.shape, jnp.bfloat16), mine, received)
    parts = in_vmem(near_kernel, "near_sums", sds((16, 16, 128), f32), exchange(chip, near))
    linear, share = in_vmem(
        final_kernel,
        "final_sums",
        (sds((6, 128), f32), sds((2 * NEAR, 16, 128), f32)),
        exchange(parts, far),
    )
    everything = exchange(share, both)
    biases, expand, reduce, depth, hidden, channel = in_vmem(
        small_kernel,
        "small_sums",
        (
            sds((4, DEC), f32),
            sds((D1, HID), f32),
            sds((D1, HID), f32),
            sds((9, HID), f32),
            sds((2, HID), f32),
            sds((3, D1), f32),
        ),
        everything,
    )
    return linear.reshape(-1), (biases, expand, reduce.T, depth, hidden, channel)


def swap_edges(to_far, to_near, axis):
    devices = lax.axis_size(axis)
    even = lax.axis_index(axis) % 2 == 0
    near = [(i, i ^ 1) for i in range(devices)]
    far = [(i, i + 1) for i in range(1, devices - 1, 2)]
    far = far + [(j, i) for i, j in far]
    from_far = lax.ppermute(to_far, axis, far)
    from_near = lax.ppermute(to_near, axis, near)
    return jnp.where(even, from_far, from_near), jnp.where(even, from_near, from_far)


def local(
    joined_grad,
    join_weight,
    linear_first,
    linear_second,
    linear_third,
    linear_fourth,
    feature_second,
    feature_third,
    feature_fourth,
    block_input,
    later_grad,
    norm_gain,
    norm_shift,
    expand_weight,
    expand_bias,
    depth_weight,
    depth_bias,
    reduce_weight,
    reduce_bias,
):
    height = TH * lax.axis_size("row")
    width = TW * lax.axis_size("col")
    top, bottom = swap_edges(*row_borders(joined_grad, block_input, later_grad), "row")

    def columns(cols):
        own = jnp.concatenate(
            [array[:, cols] for array in (joined_grad, block_input, later_grad)], axis=2
        )
        return jnp.concatenate([top[:, cols], own, bottom[:, cols]], axis=0)

    first, last = columns(slice(0, EDGE)), columns(slice(TW - EDGE, TW))
    even = lax.axis_index("col") % 2 == 0
    left, right = swap_edges(jnp.where(even, first, last), jnp.where(even, last, first), "col")
    gap = jnp.zeros((ROWS, PITCH - TW - 2 * EDGE, left.shape[2]), left.dtype)
    side = jnp.concatenate([right, left, gap], axis=1)

    input_grad, grad2, grad3, grad4, mine, other = tile_pass(
        height,
        width,
        joined_grad,
        block_input,
        later_grad,
        top,
        bottom,
        side,
        join_weight,
        linear_first,
        linear_second,
        linear_third,
        linear_fourth,
        feature_second.reshape(-1, D2),
        feature_third.reshape(-1, D3),
        feature_fourth.reshape(-1, D4),
        norm_gain.reshape(1, -1),
        norm_shift.reshape(1, -1),
        expand_weight,
        expand_bias.reshape(1, -1),
        depth_weight,
        depth_bias.reshape(1, -1),
        reduce_weight.T,
        reduce_bias.reshape(1, -1),
    )
    linear_grads, small = sum_over_mesh(mine, other)
    return (
        input_grad,
        grad2.reshape(TH // 2, TW // 2, D2),
        grad3.reshape(TH // 4, TW // 4, D3),
        grad4.reshape(TH // 8, TW // 8, D4),
        linear_grads,
        *small,
    )


def solution(mesh):
    tiles = P("row", "col", None)
    return jax.shard_map(
        local,
        mesh=mesh,
        in_specs=(tiles,) + (P(),) * 5 + (tiles,) * 5 + (P(),) * 8,
        out_specs=(tiles,) * 4 + (P(("row", "col")),) + (P(),) * 6,
        check_vma=False,
    )
```

```python
import functools
import math

import jax
import jax.numpy as jnp
from jax import lax
from jax.experimental import pallas as pl
from jax.experimental.pallas import tpu as pltpu
from jax.sharding import PartitionSpec as P

D1 = 64
D2 = 128
D3 = 320
D4 = 512
HID = 256
DEC = 384
TH = 16
TW = 32

EDGE = 4
ROWS = TH + 2 * EDGE
PITCH = 48
USED = 40
COARSE = (128, 32, 8)

XS = 4
NEAR = 16
LINEAR_ROWS = 96
PART_ROWS = LINEAR_ROWS + 16

norm_eps = 1e-06
inv_root_two = 0.7071067811865476
inv_root_tau = 0.3989422804014327


def nt(left, right):
    return lax.dot_general(left, right, (((1,), (1,)), ((), ())), preferred_element_type=jnp.float32)


def tn(left, right):
    return lax.dot_general(left, right, (((0,), (0,)), ((), ())), preferred_element_type=jnp.float32)


def nn(left, right):
    return jnp.dot(left, right, preferred_element_type=jnp.float32)


def rest_row(n):
    return 8 * (n // 4) + 4 * (n // 2 % 2) + n % 2


def place(position, pitch):
    row = jnp.floor((position + 0.5) * (1.0 / pitch))
    col = position - pitch * row
    if pitch < TW:
        col = jnp.where(col < EDGE, col + TW, col - 2 * EDGE)
    elif pitch > TW:
        col = jnp.where(col < TW + EDGE, col, col - USED)
    return row - EDGE, col


def count_up(shape, axis):
    return lax.broadcasted_iota(jnp.int32, shape, axis).astype(jnp.float32)


def inside(first, rows, pitch, height, width):
    row, col = place(count_up((rows * pitch, 1), 0) + first * pitch, pitch)
    row = row + (lax.axis_index("row") * TH).astype(jnp.float32)
    col = col + (lax.axis_index("col") * TW).astype(jnp.float32)
    good = (row >= 0.0) & (row < height) & (col >= 0.0) & (col < width)
    return jnp.where(good, 1.0, 0.0)


def normalize(values, gain, shift):
    center = jnp.mean(values, -1, keepdims=True)
    offset = values - center
    spread = jnp.mean(jnp.square(offset), -1, keepdims=True)
    scaling = lax.rsqrt(spread + norm_eps)
    standard = offset * scaling
    return (standard * gain + shift).astype(jnp.bfloat16), standard, scaling


def expand(normed, weight, bias):
    return (nn(normed, weight) + bias).astype(jnp.bfloat16).astype(jnp.float32)


def regroup(channels_last):
    source = lax.broadcasted_iota(jnp.int32, (128, 128), 0)
    target = lax.broadcasted_iota(jnp.int32, (128, 128), 1)
    wanted = (
        (target & 64)
        + 8 * (target & 6)
        + ((target & 32) >> 2)
        + ((target & 24) >> 2)
        + (target & 1)
    )
    moves = jnp.where(source == wanted, 1.0, 0.0).astype(jnp.bfloat16)
    pieces = []
    for first in range(0, channels_last.shape[1], 128):
        piece = channels_last[:, first : first + 128]
        size = piece.shape[1]
        pieces.append(nn(piece, moves[0:size, 0:size]))
    return jnp.concatenate(pieces, axis=1).astype(jnp.bfloat16)


def split_rest(rest):
    axis = rest.ndim - 2
    row = lax.broadcasted_iota(jnp.int32, rest.shape, axis)
    high = rest.astype(jnp.bfloat16).astype(jnp.float32)
    low = jnp.where(row < 2, rest - high, 0.0)
    return jnp.where(row < 2, high, pltpu.roll(low, 4, axis))


def join_rest(rest):
    return rest + pltpu.roll(rest, 4, rest.ndim - 2)


def pool_matrix(scale_index, pitch, row_index, col_index, height, width):
    factor = 2**scale_index
    coarse_rows, coarse_cols = TH // factor, TW // factor
    count = coarse_rows * coarse_cols
    row, col = place(count_up((1, ROWS * pitch), 1), pitch)
    target = count_up((count, 1), 0)
    target_row = jnp.floor((target + 0.5) * (1.0 / coarse_cols))
    target_col = target - coarse_cols * target_row
    row0 = (row_index * TH).astype(jnp.float32)
    col0 = (col_index * TW).astype(jnp.float32)
    at_row = jnp.clip((row + row0 + 0.5) * (1.0 / factor) - 0.5, 0.0, height // factor - 1.0)
    at_col = jnp.clip((col + col0 + 0.5) * (1.0 / factor) - 0.5, 0.0, width // factor - 1.0)
    at_row = at_row - row0 * (1.0 / factor)
    at_col = at_col - col0 * (1.0 / factor)
    weight = jnp.maximum(1.0 - jnp.abs(at_row - target_row), 0.0) * jnp.maximum(
        1.0 - jnp.abs(at_col - target_col), 0.0
    )
    return weight.astype(jnp.bfloat16)


def own_kernel(
    height,
    width,
    joined_ref,
    block_ref,
    top_ref,
    bottom_ref,
    join_ref,
    gain_ref,
    shift_ref,
    expand_ref,
    expand_bias_ref,
    feature2_ref,
    feature3_ref,
    feature4_ref,
    pooled_ref,
    side_matrix_ref,
    projection_ref,
    hidden_ref,
    normed_ref,
    standard_ref,
    scaling_ref,
    grouped2_ref,
    grouped3_ref,
    grouped4_ref,
    wide_ref,
):
    row_index = lax.axis_index("row")
    col_index = lax.axis_index("col")
    wide_ref[EDGE : EDGE + TH] = joined_ref[...]
    wide_ref[0:EDGE] = top_ref[:, :, 0:DEC]
    wide_ref[EDGE + TH :] = bottom_ref[:, :, 0:DEC]

    def matrix(pitch):
        return jnp.concatenate(
            [pool_matrix(k, pitch, row_index, col_index, height, width) for k in (1, 2, 3)], axis=0
        )

    pooled_ref[...] = nn(matrix(TW), wide_ref[...].reshape(ROWS * TW, DEC))
    side_matrix_ref[...] = matrix(PITCH - TW)
    projection_ref[...] = (
        nt(wide_ref[3:21].reshape(18 * TW, DEC), join_ref[0:DEC, :])
        .astype(jnp.bfloat16)
        .reshape(18, TW, DEC)
    )

    values = jnp.concatenate(
        [top_ref[2:4, :, DEC : DEC + D1], block_ref[...], bottom_ref[0:2, :, DEC : DEC + D1]], axis=0
    )
    normed, standard, scaling = normalize(
        values.reshape(20 * TW, D1).astype(jnp.float32), gain_ref[...], shift_ref[...]
    )
    hidden = expand(normed, expand_ref[...], expand_bias_ref[...])
    hidden_ref[...] = (hidden * inside(2, 20, TW, height, width)).reshape(20, TW, HID)
    own = slice(2 * TW, 18 * TW)
    normed_ref[...] = normed[own]
    standard_ref[...] = standard[own]
    scaling_ref[...] = jnp.broadcast_to(scaling[own], (TH * TW, D1))
    grouped2_ref[...] = regroup(feature2_ref[...])
    grouped3_ref[...] = regroup(feature3_ref[...])
    grouped4_ref[...] = regroup(feature4_ref[...])


def own_pass(height, width, *operands):
    sds = jax.ShapeDtypeStruct
    bf16, f32 = jnp.bfloat16, jnp.float32
    pixels = TH * TW
    return in_vmem(
        functools.partial(own_kernel, height, width),
        "own_pass",
        (
            sds((sum(COARSE), DEC), f32),
            sds((sum(COARSE), ROWS * (PITCH - TW)), bf16),
            sds((18, TW, DEC), bf16),
            sds((20, TW, HID), f32),
            sds((pixels, D1), bf16),
            sds((pixels, D1), f32),
            sds((pixels, D1), f32),
            sds((COARSE[0], D2), bf16),
            sds((COARSE[1], D3), bf16),
            sds((COARSE[2], D4), bf16),
        ),
        *operands,
        scratch=[pltpu.VMEM((ROWS, TW, DEC), bf16)],
    )


def tile_kernel(
    height,
    width,
    pooled_ref,
    side_matrix_ref,
    own_projection_ref,
    own_hidden_ref,
    normed_ref,
    standard_ref,
    scaling_ref,
    feature2_ref,
    feature3_ref,
    feature4_ref,
    block_ref,
    later_ref,
    top_ref,
    bottom_ref,
    side_ref,
    join_ref,
    first_ref,
    second_ref,
    third_ref,
    fourth_ref,
    gain_ref,
    shift_ref,
    expand_ref,
    expand_bias_ref,
    depth_ref,
    depth_bias_ref,
    reduce_ref,
    reduce_bias_ref,
    input_grad_ref,
    grad2_ref,
    grad3_ref,
    grad4_ref,
    mine_ref,
    other_ref,
    projection_ref,
    wide_later_ref,
    hid_ref,
    slope_ref,
    act_ref,
    pre_ref,
    hgrad_ref,
    linear_ref,
    rest_ref,
):
    row_index = lax.axis_index("row")
    scale_base = 1.0 / math.sqrt(height * width)

    later_lanes = slice(DEC + D1, DEC + 2 * D1)
    wide_later_ref[1 : 1 + TH, 0:TW] = later_ref[...]
    wide_later_ref[0:1, 0:TW] = top_ref[EDGE - 1 :, :, later_lanes]
    wide_later_ref[1 + TH :, 0:TW] = bottom_ref[0:1, :, later_lanes]
    wide_later_ref[:, TW:] = side_ref[3:21, :, later_lanes]
    rest_ref[...] = jnp.zeros_like(rest_ref)

    def keep_row(row, value):
        for piece in range(value.shape[1] // 128):
            at = rest_row(row + piece)
            rest_ref[at : at + 1, :] = value[:, 128 * piece : 128 * piece + 128]

    side_joined = side_ref[:, :, 0:DEC].reshape(ROWS * (PITCH - TW), DEC)
    pooled = (pooled_ref[...] + nn(side_matrix_ref[...], side_joined)).astype(jnp.bfloat16)
    start = 0
    base = D1
    for k, linear, feature, grad in (
        (1, second_ref, feature2_ref, grad2_ref),
        (2, third_ref, feature3_ref, grad3_ref),
        (3, fourth_ref, feature4_ref, grad4_ref),
    ):
        count = COARSE[k - 1]
        channels = linear.shape[0]
        projection = nt(pooled[start : start + count], join_ref[k * DEC : (k + 1) * DEC, :]).astype(
            jnp.bfloat16
        )
        grad[...] = nt(projection, linear[...]).astype(jnp.bfloat16)
        linear_ref[base : base + channels, :] = tn(feature[...], projection) * (2**k * scale_base)
        keep_row(
            3 * k,
            jnp.sum(projection.astype(jnp.float32), 0, keepdims=True) * (2**k * scale_base),
        )
        start += count
        base += channels

    values = side_ref[2:22, :, DEC : DEC + D1].astype(jnp.float32)[:, 0 : 2 * EDGE]
    normed, _, _ = normalize(values.reshape(20 * 2 * EDGE, D1), gain_ref[...], shift_ref[...])
    hidden = expand(normed, expand_ref[...], expand_bias_ref[...])
    hid_ref[:, 0:TW] = own_hidden_ref[...]
    hid_ref[:, TW:] = (hidden * inside(2, 20, 2 * EDGE, height, width)).reshape(20, 2 * EDGE, HID)

    def across(before, same, after):
        return pltpu.roll(before, 1, 0) + same + pltpu.roll(after, USED - 1, 0)

    def conv_row(i, carry):
        rows = [hid_ref[i + a] for a in range(3)]
        sums = [
            sum(depth_ref[3 * a + b : 3 * a + b + 1, :] * rows[a] for a in range(3))
            for b in range(3)
        ]
        conv = across(*sums) + depth_bias_ref[...]
        cumulative = 0.5 * (1.0 + lax.erf(conv * inv_root_two))
        density = inv_root_tau * jnp.exp(-0.5 * conv * conv)
        act_ref[i] = (conv * cumulative)[0:TW].astype(jnp.bfloat16)
        slope_ref[i] = cumulative + conv * density
        return carry

    lax.fori_loop(0, 18, conv_row, 0)

    def own(value, rows, pitch):
        first = (rows - TH) // 2
        channels = value.shape[-1]
        return value.reshape(rows, pitch, channels)[first : first + TH, 0:TW].reshape(
            TH * TW, channels
        )

    side_projection = nt(
        side_ref[3:21, :, 0:DEC].reshape(18 * (PITCH - TW), DEC), join_ref[0:DEC, :]
    ).astype(jnp.bfloat16)
    projection_ref[:, 0:TW] = own_projection_ref[...]
    projection_ref[:, TW:] = side_projection.reshape(18, PITCH - TW, DEC)
    projection = projection_ref[...].reshape(18 * PITCH, DEC)
    later = wide_later_ref[...].reshape(18 * PITCH, D1).astype(jnp.float32)
    feature_grad = (nt(projection, first_ref[...]) + later).astype(jnp.bfloat16)
    act_grad = nn(feature_grad, reduce_ref[...])
    act_grad = act_grad.reshape(18, PITCH, HID)[:, 0:USED]
    pre_grad = (act_grad * slope_ref[...]).astype(jnp.bfloat16).astype(jnp.float32)
    pre_ref[...] = pre_grad * inside(3, 18, USED, height, width).reshape(18, USED, 1)

    activated = act_ref[1:17].reshape(TH * TW, HID)
    own_projection = own_projection_ref[1 : 1 + TH].reshape(TH * TW, DEC)
    own_grad = own(feature_grad, 18, PITCH)
    own_block = block_ref[...].reshape(TH * TW, D1).astype(jnp.float32)
    features = (own_block + (nt(activated, reduce_ref[...]) + reduce_bias_ref[...])).astype(
        jnp.bfloat16
    )
    linear_ref[0:D1, :] = tn(regroup(features), own_projection) * scale_base
    keep_row(0, jnp.sum(own_projection.astype(jnp.float32), 0, keepdims=True) * scale_base)
    reduce_part = tn(own_grad, activated) * scale_base

    def fold(value):
        return jnp.sum(value.reshape(-1, 8, HID), 0)

    def grad_row(i, sums):
        center_row = pre_ref[i + 1, 0:TW, :]
        own_row = jnp.concatenate([center_row, jnp.zeros((USED - TW, HID), jnp.float32)], axis=0)
        rows = [pre_ref[i + 2 - a] for a in range(3)]
        sums_b = [
            sum(depth_ref[3 * a + b : 3 * a + b + 1, :] * rows[a] for a in range(3))
            for b in range(3)
        ]
        total = across(sums_b[2], sums_b[1], sums_b[0])[0:TW]
        moved = [pltpu.roll(own_row, USED - 1, 0), own_row, pltpu.roll(own_row, 1, 0)]
        taps = []
        for a in range(3):
            hid_row = hid_ref[i + 1 + a]
            for b in range(3):
                taps.append(sums[3 * a + b] + fold(hid_row * moved[b]))
        rounded = total.astype(jnp.bfloat16)
        hgrad_ref[i] = rounded
        taps.append(sums[9] + fold(rounded.astype(jnp.float32)))
        taps.append(sums[10] + fold(center_row))
        return tuple(taps)

    sums = lax.fori_loop(0, TH, grad_row, (jnp.zeros((8, HID), jnp.float32),) * 11)
    for n in range(11):
        keep_row(12 + 2 * n, jnp.sum(sums[n], 0, keepdims=True) * scale_base)

    hidden_grad = hgrad_ref[...].reshape(TH * TW, HID)
    own_standard = standard_ref[...]
    expand_part = tn(normed_ref[...], hidden_grad) * scale_base
    normed_grad = nt(hidden_grad, expand_ref[...])
    fgrad = own_grad.astype(jnp.float32)
    for n, value in enumerate((fgrad, normed_grad * own_standard, normed_grad)):
        at = rest_row(34 + n)
        rest_ref[at : at + 1, 0:D1] = jnp.sum(value, 0, keepdims=True) * scale_base
    scaled = normed_grad * gain_ref[...]
    input_grad = fgrad + scaling_ref[...] * (
        scaled
        - jnp.mean(scaled, -1, keepdims=True)
        - own_standard * jnp.mean(scaled * own_standard, -1, keepdims=True)
    )
    input_grad_ref[...] = input_grad.astype(jnp.bfloat16).reshape(TH, TW, D1)

    even_core = row_index % 2 == 0

    def keep(part, pairs):
        for n in range(0, len(pairs), 2):
            mine = [jnp.where(even_core, even, odd) for even, odd in pairs[n : n + 2]]
            other = [jnp.where(even_core, odd, even) for even, odd in pairs[n : n + 2]]
            if n + 2 == len(pairs):
                other[1] = split_rest(other[1])
            at = slice(8 * n, 8 * n + 16)
            mine_ref[part, at, :] = jnp.concatenate(mine, axis=0)
            other_ref[part, at, :] = jnp.concatenate(other, axis=0).astype(jnp.bfloat16)

    upper = lax.broadcasted_iota(jnp.int32, (8, 128), 0) < 4
    for part in range(NEAR):
        zl, within = part // 8, 8 * (part % 8)
        pairs = []
        for zh in range(4):
            first = 128 * (2 * zh + zl) + within
            for j in range(3):
                lanes = slice(128 * j, 128 * j + 128)
                pairs.append(
                    (
                        linear_ref[first : first + 8, lanes],
                        linear_ref[first + 64 : first + 72, lanes],
                    )
                )
        lanes = slice(0, 128) if part < 8 else slice(128, 256)
        expands = expand_part[within : within + 8, lanes]
        reduces = reduce_part[within : within + 8, lanes]
        pairs.append(
            (
                jnp.where(upper, expands, pltpu.roll(reduces, 4, 0)),
                jnp.where(upper, pltpu.roll(expands, 4, 0), reduces),
            )
        )
        rest = rest_ref[8 * part : 8 * part + 8, :]
        pairs.append((rest, pltpu.roll(rest, 4, 0)))
        keep(part, pairs)


def row_kernel(
    joined_ref, block_ref, later_ref, far_ref, near_ref, joined_buf, block_buf, later_buf, sems
):
    copies = []
    for n, (source, target) in enumerate(
        ((joined_ref, joined_buf), (block_ref, block_buf), (later_ref, later_buf))
    ):
        for last in range(2):
            rows = slice(TH - EDGE, TH) if last else slice(0, EDGE)
            copy = pltpu.make_async_copy(source.at[rows], target.at[last], sems.at[2 * n + last])
            copy.start()
            copies.append(copy)
    for copy in copies:
        copy.wait()
    even = lax.axis_index("row") % 2 == 0
    for buf, lanes in (
        (joined_buf, slice(0, DEC)),
        (block_buf, slice(DEC, DEC + D1)),
        (later_buf, slice(DEC + D1, DEC + 2 * D1)),
    ):
        first = buf[0].astype(jnp.float32)
        last = buf[1].astype(jnp.float32)
        far_ref[:, :, lanes] = jnp.where(even, first, last).astype(jnp.bfloat16)
        near_ref[:, :, lanes] = jnp.where(even, last, first).astype(jnp.bfloat16)


def row_borders(joined, block, later):
    vmem = pl.BlockSpec(memory_space=pltpu.VMEM)
    out = jax.ShapeDtypeStruct((EDGE, TW, DEC + 2 * D1), jnp.bfloat16)
    return pl.pallas_call(
        row_kernel,
        out_shape=(out, out),
        in_specs=[pl.BlockSpec(memory_space=pltpu.HBM)] * 3,
        out_specs=(vmem, vmem),
        scratch_shapes=[pltpu.VMEM((2, EDGE) + a.shape[1:], a.dtype) for a in (joined, block, later)]
        + [pltpu.SemaphoreType.DMA((6,))],
        compiler_params=pltpu.CompilerParams(vmem_limit_bytes=56 * 2**20),
        name="row_borders",
    )(joined, block, later)


def column_kernel(joined_ref, block_ref, later_ref, top_ref, bottom_ref, far_ref, near_ref):
    even = lax.axis_index("col") % 2 == 0
    own_rows = slice(EDGE, EDGE + TH)
    for ref, rows, lanes in (
        (joined_ref, own_rows, slice(0, DEC)),
        (block_ref, own_rows, slice(DEC, DEC + D1)),
        (later_ref, own_rows, slice(DEC + D1, DEC + 2 * D1)),
        (top_ref, slice(0, EDGE), slice(0, DEC + 2 * D1)),
        (bottom_ref, slice(EDGE + TH, ROWS), slice(0, DEC + 2 * D1)),
    ):
        first = ref[:, 0:16].astype(jnp.float32)[:, 0:EDGE]
        last = ref[:, TW - 16 : TW].astype(jnp.float32)[:, 16 - EDGE : 16]
        far_ref[rows, :, lanes] = jnp.where(even, first, last).astype(jnp.bfloat16)
        near_ref[rows, :, lanes] = jnp.where(even, last, first).astype(jnp.bfloat16)


def tile_pass(height, width, *operands):
    sds = jax.ShapeDtypeStruct
    bf16, f32 = jnp.bfloat16, jnp.float32
    vmem = pltpu.VMEM
    return pl.pallas_call(
        functools.partial(tile_kernel, height, width),
        out_shape=(
            sds((TH, TW, D1), bf16),
            sds((COARSE[0], D2), bf16),
            sds((COARSE[1], D3), bf16),
            sds((COARSE[2], D4), bf16),
            sds((NEAR, PART_ROWS, 128), f32),
            sds((NEAR, PART_ROWS, 128), bf16),
        ),
        in_specs=[pl.BlockSpec(memory_space=vmem)] * len(operands),
        out_specs=(pl.BlockSpec(memory_space=vmem),) * 6,
        scratch_shapes=[
            vmem((18, PITCH, DEC), bf16),
            vmem((18, PITCH, D1), bf16),
            vmem((20, USED, HID), f32),
            vmem((18, USED, HID), f32),
            vmem((18, TW, HID), bf16),
            vmem((18, USED, HID), f32),
            vmem((TH, TW, HID), bf16),
            vmem((D1 + D2 + D3 + D4, DEC), f32),
            vmem((128, 128), f32),
        ],
        compiler_params=pltpu.CompilerParams(vmem_limit_bytes=28 * 2**20),
        name="tile_pass",
    )(*operands)


def near_kernel(received_ref, out_ref):
    total = jnp.sum(received_ref[...].astype(jnp.float32), 0)
    share = total[LINEAR_ROWS : LINEAR_ROWS + 8]
    rest = total[LINEAR_ROWS + 8 :]
    rest = pltpu.roll(join_rest(rest), 6, 0)
    row = lax.broadcasted_iota(jnp.int32, (8, 128), 0)
    for zh in range(4):
        pieces = [total[24 * zh + 8 * j : 24 * zh + 8 * j + 8] for j in range(3)]
        for yh in range(4):
            part = rest
            for j in range(3):
                shift = (2 * j - 2 * yh) % 8
                moved = pltpu.roll(pieces[j], shift, 0) if shift else pieces[j]
                part = jnp.where((row >= 2 * j) & (row < 2 * j + 2), moved, part)
            out_ref[4 * zh + yh, 0:8, :] = part
            out_ref[4 * zh + yh, 8:16, :] = share


def final_kernel(received_ref, linear_ref, out_ref):
    total = jnp.sum(received_ref[...], 0)
    for p in range(2):
        for j in range(3):
            linear_ref[3 * p + j : 3 * p + j + 1, :] = total[2 * j + p : 2 * j + p + 1, :]
    for n in range(out_ref.shape[0]):
        for i in range(4):
            out_ref[n, i] = total[8 + 2 * i : 10 + 2 * i]
        out_ref[n, 4] = total[6:8]


def small_kernel(all_ref, biases_ref, expand_ref, reduce_ref, depth_ref, hidden_ref, channel_ref):
    for share in range(2 * NEAR):
        lanes = slice(0, 128) if share < NEAR else slice(128, 256)
        first = 4 * (share % NEAR)
        for i in range(2):
            rows = slice(first + 2 * i, first + 2 * i + 2)
            expand_ref[rows, lanes] = all_ref[share, i]
            reduce_ref[rows, lanes] = all_ref[share, 2 + i]

    def row(n):
        return all_ref[n // 2, 4, n % 2 : n % 2 + 1, :]

    for k in range(4):
        for j in range(3):
            biases_ref[k : k + 1, 128 * j : 128 * j + 128] = row(3 * k + j)
    for t in range(9):
        for j in range(2):
            depth_ref[t : t + 1, 128 * j : 128 * j + 128] = row(12 + 2 * t + j)
    for t in range(2):
        for j in range(2):
            hidden_ref[t : t + 1, 128 * j : 128 * j + 128] = row(30 + 2 * t + j)
    for t in range(3):
        channel_ref[t : t + 1, :] = row(34 + t)[:, 0:D1]


def in_vmem(kernel, name, out_shape, *operands, scratch=()):
    vmem = pl.BlockSpec(memory_space=pltpu.VMEM)
    return pl.pallas_call(
        kernel,
        out_shape=out_shape,
        in_specs=[vmem] * len(operands),
        out_specs=jax.tree.map(lambda _: vmem, out_shape),
        scratch_shapes=scratch,
        compiler_params=pltpu.CompilerParams(vmem_limit_bytes=16 * 2**20),
        name=name,
    )(*operands)


def chip_kernel(mine_ref, received_ref, out_ref):
    plain = LINEAR_ROWS + 8
    received = received_ref[...].astype(jnp.float32)
    total = mine_ref[:, 0:plain, :] + received[:, 0:plain]
    rest = split_rest(mine_ref[:, plain:, :] + join_rest(received[:, plain:]))
    out_ref[...] = jnp.concatenate([total, rest], axis=1).astype(jnp.bfloat16)


def device_groups(chips, cols):
    half_z, half_y = range(chips // 2), range(cols // XS // 2)
    two, xs = range(2), range(XS)

    def device(zh, zl, core, yh, yl, x):
        return (2 * (2 * zh + zl) + core) * cols + XS * (2 * yh + yl) + x

    near = [
        [device(zh, zl, core, yh, yl, x) for zl in two for yl in two for x in xs]
        for core in two
        for zh in half_z
        for yh in half_y
    ]
    far = [
        [device(zh, zl, core, yh, yl, x) for zh in half_z for yh in half_y]
        for core in two
        for zl in two
        for yl in two
        for x in xs
    ]
    both = [
        [device(zh, zl, core, yh, yl, x) for zl in two for yl in two for x in xs for core in two]
        for zh in half_z
        for yh in half_y
    ]
    return near, far, both


def sum_over_mesh(mine, other):
    rows = lax.axis_size("row")
    cols = lax.axis_size("col")
    sds = jax.ShapeDtypeStruct
    f32 = jnp.float32
    near, far, both = device_groups(rows // 2, cols)

    def exchange(parts, groups):
        return lax.all_to_all(parts, ("row", "col"), 0, 0, tiled=True, axis_index_groups=groups)

    received = lax.ppermute(other, "row", [(i, i ^ 1) for i in range(rows)])
    chip = in_vmem(chip_kernel, "chip_sums", sds(other.shape, other.dtype), mine, received)
    parts = in_vmem(near_kernel, "near_sums", sds((16, 16, 128), f32), exchange(chip, near))
    linear, share = in_vmem(
        final_kernel,
        "final_sums",
        (sds((6, 128), f32), sds((2 * NEAR, 5, 2, 128), f32)),
        exchange(parts, far),
    )
    everything = exchange(share, both)
    biases, expand, reduce, depth, hidden, channel = in_vmem(
        small_kernel,
        "small_sums",
        (
            sds((4, DEC), f32),
            sds((D1, HID), f32),
            sds((D1, HID), f32),
            sds((9, HID), f32),
            sds((2, HID), f32),
            sds((3, D1), f32),
        ),
        everything,
    )
    return linear.reshape(-1), (biases, expand, reduce.T, depth, hidden, channel)


def swap_edges(to_far, to_near, axis):
    devices = lax.axis_size(axis)
    even = lax.axis_index(axis) % 2 == 0
    near = [(i, i ^ 1) for i in range(devices)]
    far = [(i, i + 1) for i in range(1, devices - 1, 2)]
    far = far + [(j, i) for i, j in far]
    from_far = lax.ppermute(to_far, axis, far)
    from_near = lax.ppermute(to_near, axis, near)
    return jnp.where(even, from_far, from_near), jnp.where(even, from_near, from_far)


def local(
    joined_grad,
    join_weight,
    linear_first,
    linear_second,
    linear_third,
    linear_fourth,
    feature_second,
    feature_third,
    feature_fourth,
    block_input,
    later_grad,
    norm_gain,
    norm_shift,
    expand_weight,
    expand_bias,
    depth_weight,
    depth_bias,
    reduce_weight,
    reduce_bias,
):
    height = TH * lax.axis_size("row")
    width = TW * lax.axis_size("col")
    top, bottom = swap_edges(*row_borders(joined_grad, block_input, later_grad), "row")
    column = jax.ShapeDtypeStruct((ROWS, EDGE, DEC + 2 * D1), jnp.bfloat16)
    left, right = swap_edges(
        *in_vmem(
            column_kernel,
            "column_borders",
            (column, column),
            joined_grad,
            block_input,
            later_grad,
            top,
            bottom,
        ),
        "col",
    )
    early = own_pass(
        height,
        width,
        joined_grad,
        block_input,
        top,
        bottom,
        join_weight,
        norm_gain.reshape(1, -1),
        norm_shift.reshape(1, -1),
        expand_weight,
        expand_bias.reshape(1, -1),
        feature_second.reshape(-1, D2),
        feature_third.reshape(-1, D3),
        feature_fourth.reshape(-1, D4),
    )
    gap = jnp.zeros((ROWS, PITCH - TW - 2 * EDGE, left.shape[2]), left.dtype)
    side = jnp.concatenate([right, left, gap], axis=1)

    input_grad, grad2, grad3, grad4, mine, other = tile_pass(
        height,
        width,
        *early,
        block_input,
        later_grad,
        top,
        bottom,
        side,
        join_weight,
        linear_first,
        linear_second,
        linear_third,
        linear_fourth,
        norm_gain.reshape(1, -1),
        norm_shift.reshape(1, -1),
        expand_weight,
        expand_bias.reshape(1, -1),
        depth_weight,
        depth_bias.reshape(1, -1),
        reduce_weight.T,
        reduce_bias.reshape(1, -1),
    )
    linear_grads, small = sum_over_mesh(mine, other)
    return (
        input_grad,
        grad2.reshape(TH // 2, TW // 2, D2),
        grad3.reshape(TH // 4, TW // 4, D3),
        grad4.reshape(TH // 8, TW // 8, D4),
        linear_grads,
        *small,
    )


def solution(mesh):
    tiles = P("row", "col", None)
    return jax.shard_map(
        local,
        mesh=mesh,
        in_specs=(tiles,) + (P(),) * 5 + (tiles,) * 5 + (P(),) * 8,
        out_specs=(tiles,) * 4 + (P(("row", "col")),) + (P(),) * 6,
        check_vma=False,
    )
```

```python
import functools
import math

import jax
import jax.numpy as jnp
from jax import lax
from jax.experimental import pallas as pl
from jax.experimental.pallas import tpu as pltpu
from jax.sharding import PartitionSpec as P

D1 = 64
D2 = 128
D3 = 320
D4 = 512
HID = 256
DEC = 384
TH = 16
TW = 32

EDGE = 4
ROWS = TH + 2 * EDGE
PITCH = 48
USED = 40
COARSE = (128, 32, 8)

XS = 4
NEAR = 16
LINEAR_ROWS = 96
PART_ROWS = LINEAR_ROWS + 16

norm_eps = 1e-06
inv_root_two = 0.7071067811865476
inv_root_tau = 0.3989422804014327


def nt(left, right):
    return lax.dot_general(left, right, (((1,), (1,)), ((), ())), preferred_element_type=jnp.float32)


def tn(left, right):
    return lax.dot_general(left, right, (((0,), (0,)), ((), ())), preferred_element_type=jnp.float32)


def nn(left, right):
    return jnp.dot(left, right, preferred_element_type=jnp.float32)


def rest_row(n):
    return 8 * (n // 4) + 4 * (n // 2 % 2) + n % 2


def place(position, pitch):
    row = jnp.floor((position + 0.5) * (1.0 / pitch))
    col = position - pitch * row
    if pitch < TW:
        col = jnp.where(col < EDGE, col + TW, col - 2 * EDGE)
    elif pitch > TW:
        col = jnp.where(col < TW + EDGE, col, col - USED)
    return row - EDGE, col


def count_up(shape, axis):
    return lax.broadcasted_iota(jnp.int32, shape, axis).astype(jnp.float32)


def inside(first, rows, pitch, height, width):
    row, col = place(count_up((rows * pitch, 1), 0) + first * pitch, pitch)
    row = row + (lax.axis_index("row") * TH).astype(jnp.float32)
    col = col + (lax.axis_index("col") * TW).astype(jnp.float32)
    good = (row >= 0.0) & (row < height) & (col >= 0.0) & (col < width)
    return jnp.where(good, 1.0, 0.0)


def normalize(values, gain, shift):
    center = jnp.mean(values, -1, keepdims=True)
    offset = values - center
    spread = jnp.mean(jnp.square(offset), -1, keepdims=True)
    scaling = lax.rsqrt(spread + norm_eps)
    standard = offset * scaling
    return (standard * gain + shift).astype(jnp.bfloat16), standard, scaling


def expand(normed, weight, bias):
    return (nn(normed, weight) + bias).astype(jnp.bfloat16).astype(jnp.float32)


def regroup(channels_last):
    source = lax.broadcasted_iota(jnp.int32, (128, 128), 0)
    target = lax.broadcasted_iota(jnp.int32, (128, 128), 1)
    wanted = (
        (target & 64)
        + 8 * (target & 6)
        + ((target & 32) >> 2)
        + ((target & 24) >> 2)
        + (target & 1)
    )
    moves = jnp.where(source == wanted, 1.0, 0.0).astype(jnp.bfloat16)
    pieces = []
    for first in range(0, channels_last.shape[1], 128):
        piece = channels_last[:, first : first + 128]
        size = piece.shape[1]
        pieces.append(nn(piece, moves[0:size, 0:size]))
    return jnp.concatenate(pieces, axis=1).astype(jnp.bfloat16)


def split_rest(rest):
    axis = rest.ndim - 2
    row = lax.broadcasted_iota(jnp.int32, rest.shape, axis)
    high = rest.astype(jnp.bfloat16).astype(jnp.float32)
    low = jnp.where(row < 2, rest - high, 0.0)
    return jnp.where(row < 2, high, pltpu.roll(low, 4, axis))


def join_rest(rest):
    return rest + pltpu.roll(rest, 4, rest.ndim - 2)


def pool_matrix(scale_index, pitch, row_index, col_index, height, width):
    factor = 2**scale_index
    coarse_rows, coarse_cols = TH // factor, TW // factor
    count = coarse_rows * coarse_cols
    row, col = place(count_up((1, ROWS * pitch), 1), pitch)
    target = count_up((count, 1), 0)
    target_row = jnp.floor((target + 0.5) * (1.0 / coarse_cols))
    target_col = target - coarse_cols * target_row
    row0 = (row_index * TH).astype(jnp.float32)
    col0 = (col_index * TW).astype(jnp.float32)
    at_row = jnp.clip((row + row0 + 0.5) * (1.0 / factor) - 0.5, 0.0, height // factor - 1.0)
    at_col = jnp.clip((col + col0 + 0.5) * (1.0 / factor) - 0.5, 0.0, width // factor - 1.0)
    at_row = at_row - row0 * (1.0 / factor)
    at_col = at_col - col0 * (1.0 / factor)
    weight = jnp.maximum(1.0 - jnp.abs(at_row - target_row), 0.0) * jnp.maximum(
        1.0 - jnp.abs(at_col - target_col), 0.0
    )
    return weight.astype(jnp.bfloat16)


def add_later(projection, linear, later):
    later = later.reshape(-1, D1).astype(jnp.float32)
    return (nt(projection, linear) + later).astype(jnp.bfloat16)


def own_kernel(
    height,
    width,
    joined_ref,
    block_ref,
    later_ref,
    top_ref,
    bottom_ref,
    join_ref,
    first_ref,
    reduce_ref,
    gain_ref,
    shift_ref,
    expand_ref,
    expand_bias_ref,
    feature2_ref,
    feature3_ref,
    feature4_ref,
    pooled_ref,
    side_matrix_ref,
    projection_ref,
    grad_ref,
    act_grad_ref,
    hidden_ref,
    normed_ref,
    standard_ref,
    scaling_ref,
    grouped2_ref,
    grouped3_ref,
    grouped4_ref,
    wide_ref,
):
    row_index = lax.axis_index("row")
    col_index = lax.axis_index("col")
    wide_ref[EDGE : EDGE + TH] = joined_ref[...]
    wide_ref[0:EDGE] = top_ref[:, :, 0:DEC]
    wide_ref[EDGE + TH :] = bottom_ref[:, :, 0:DEC]

    def matrix(pitch):
        return jnp.concatenate(
            [pool_matrix(k, pitch, row_index, col_index, height, width) for k in (1, 2, 3)], axis=0
        )

    pooled_ref[...] = nn(matrix(TW), wide_ref[...].reshape(ROWS * TW, DEC))
    side_matrix_ref[...] = matrix(PITCH - TW)
    projection = nt(wide_ref[3:21].reshape(18 * TW, DEC), join_ref[0:DEC, :]).astype(jnp.bfloat16)
    projection_ref[...] = projection[TW : 17 * TW]
    lanes = slice(DEC + D1, DEC + 2 * D1)
    later = jnp.concatenate(
        [top_ref[3:4, :, lanes], later_ref[...], bottom_ref[0:1, :, lanes]], axis=0
    )
    feature_grad = add_later(projection, first_ref[...], later)
    grad_ref[...] = feature_grad[TW : 17 * TW]
    act_grad_ref[...] = nn(feature_grad, reduce_ref[...]).reshape(18, TW, HID)

    values = jnp.concatenate(
        [top_ref[2:4, :, DEC : DEC + D1], block_ref[...], bottom_ref[0:2, :, DEC : DEC + D1]], axis=0
    )
    normed, standard, scaling = normalize(
        values.reshape(20 * TW, D1).astype(jnp.float32), gain_ref[...], shift_ref[...]
    )
    hidden = expand(normed, expand_ref[...], expand_bias_ref[...])
    hidden_ref[...] = (hidden * inside(2, 20, TW, height, width)).reshape(20, TW, HID)
    own = slice(2 * TW, 18 * TW)
    normed_ref[...] = normed[own]
    standard_ref[...] = standard[own]
    scaling_ref[...] = jnp.broadcast_to(scaling[own], (TH * TW, D1))
    grouped2_ref[...] = regroup(feature2_ref[...])
    grouped3_ref[...] = regroup(feature3_ref[...])
    grouped4_ref[...] = regroup(feature4_ref[...])


def own_pass(height, width, *operands):
    sds = jax.ShapeDtypeStruct
    bf16, f32 = jnp.bfloat16, jnp.float32
    pixels = TH * TW
    return in_vmem(
        functools.partial(own_kernel, height, width),
        "own_pass",
        (
            sds((sum(COARSE), DEC), f32),
            sds((sum(COARSE), ROWS * (PITCH - TW)), bf16),
            sds((pixels, DEC), bf16),
            sds((pixels, D1), bf16),
            sds((18, TW, HID), f32),
            sds((20, TW, HID), f32),
            sds((pixels, D1), bf16),
            sds((pixels, D1), f32),
            sds((pixels, D1), f32),
            sds((COARSE[0], D2), bf16),
            sds((COARSE[1], D3), bf16),
            sds((COARSE[2], D4), bf16),
        ),
        *operands,
        scratch=[pltpu.VMEM((ROWS, TW, DEC), bf16)],
    )


def tile_kernel(
    height,
    width,
    pooled_ref,
    side_matrix_ref,
    own_projection_ref,
    own_grad_ref,
    own_act_grad_ref,
    own_hidden_ref,
    normed_ref,
    standard_ref,
    scaling_ref,
    feature2_ref,
    feature3_ref,
    feature4_ref,
    block_ref,
    side_ref,
    join_ref,
    first_ref,
    second_ref,
    third_ref,
    fourth_ref,
    gain_ref,
    shift_ref,
    expand_ref,
    expand_bias_ref,
    depth_ref,
    depth_bias_ref,
    reduce_ref,
    reduce_bias_ref,
    input_grad_ref,
    grad2_ref,
    grad3_ref,
    grad4_ref,
    mine_ref,
    other_ref,
    hid_ref,
    slope_ref,
    act_ref,
    pre_ref,
    hgrad_ref,
    linear_ref,
    rest_ref,
):
    row_index = lax.axis_index("row")
    scale_base = 1.0 / math.sqrt(height * width)

    rest_ref[...] = jnp.zeros_like(rest_ref)

    def keep_row(row, value):
        for piece in range(value.shape[1] // 128):
            at = rest_row(row + piece)
            rest_ref[at : at + 1, :] = value[:, 128 * piece : 128 * piece + 128]

    side_joined = side_ref[:, :, 0:DEC].reshape(ROWS * (PITCH - TW), DEC)
    pooled = (pooled_ref[...] + nn(side_matrix_ref[...], side_joined)).astype(jnp.bfloat16)
    start = 0
    base = D1
    for k, linear, feature, grad in (
        (1, second_ref, feature2_ref, grad2_ref),
        (2, third_ref, feature3_ref, grad3_ref),
        (3, fourth_ref, feature4_ref, grad4_ref),
    ):
        count = COARSE[k - 1]
        channels = linear.shape[0]
        projection = nt(pooled[start : start + count], join_ref[k * DEC : (k + 1) * DEC, :]).astype(
            jnp.bfloat16
        )
        grad[...] = nt(projection, linear[...]).astype(jnp.bfloat16)
        linear_ref[base : base + channels, :] = tn(feature[...], projection) * (2**k * scale_base)
        keep_row(
            3 * k,
            jnp.sum(projection.astype(jnp.float32), 0, keepdims=True) * (2**k * scale_base),
        )
        start += count
        base += channels

    values = side_ref[2:22, :, DEC : DEC + D1].astype(jnp.float32)[:, 0 : 2 * EDGE]
    normed, _, _ = normalize(values.reshape(20 * 2 * EDGE, D1), gain_ref[...], shift_ref[...])
    hidden = expand(normed, expand_ref[...], expand_bias_ref[...])
    hid_ref[:, 0:TW] = own_hidden_ref[...]
    hid_ref[:, TW:] = (hidden * inside(2, 20, 2 * EDGE, height, width)).reshape(20, 2 * EDGE, HID)

    def across(before, same, after):
        return pltpu.roll(before, 1, 0) + same + pltpu.roll(after, USED - 1, 0)

    def conv_row(i, carry):
        rows = [hid_ref[i + a] for a in range(3)]
        sums = [
            sum(depth_ref[3 * a + b : 3 * a + b + 1, :] * rows[a] for a in range(3))
            for b in range(3)
        ]
        conv = across(*sums) + depth_bias_ref[...]
        cumulative = 0.5 * (1.0 + lax.erf(conv * inv_root_two))
        density = inv_root_tau * jnp.exp(-0.5 * conv * conv)
        act_ref[i] = (conv * cumulative)[0:TW].astype(jnp.bfloat16)
        slope_ref[i] = cumulative + conv * density
        return carry

    lax.fori_loop(0, 18, conv_row, 0)

    beside = slice(0, 2 * EDGE)
    projection = nt(
        side_ref[3:21, :, 0:DEC].reshape(18 * (PITCH - TW), DEC), join_ref[0:DEC, :]
    ).astype(jnp.bfloat16)
    feature_grad = add_later(
        projection, first_ref[...], side_ref[3:21, :, DEC + D1 : DEC + 2 * D1]
    )
    act_grad = nn(feature_grad, reduce_ref[...]).reshape(18, PITCH - TW, HID)[:, beside]
    grid = inside(3, 18, USED, height, width).reshape(18, USED, 1)
    for cols, part in ((slice(0, TW), own_act_grad_ref[...]), (slice(TW, USED), act_grad)):
        pre_grad = (part * slope_ref[:, cols, :]).astype(jnp.bfloat16).astype(jnp.float32)
        pre_ref[:, cols, :] = pre_grad * grid[:, cols]

    activated = act_ref[1:17].reshape(TH * TW, HID)
    own_projection = own_projection_ref[...]
    own_grad = own_grad_ref[...]
    own_block = block_ref[...].reshape(TH * TW, D1).astype(jnp.float32)
    features = (own_block + (nt(activated, reduce_ref[...]) + reduce_bias_ref[...])).astype(
        jnp.bfloat16
    )
    linear_ref[0:D1, :] = tn(regroup(features), own_projection) * scale_base
    keep_row(0, jnp.sum(own_projection.astype(jnp.float32), 0, keepdims=True) * scale_base)
    reduce_part = tn(own_grad, activated) * scale_base

    def fold(value):
        return jnp.sum(value.reshape(-1, 8, HID), 0)

    def grad_row(i, sums):
        center_row = pre_ref[i + 1, 0:TW, :]
        own_row = jnp.concatenate([center_row, jnp.zeros((USED - TW, HID), jnp.float32)], axis=0)
        rows = [pre_ref[i + 2 - a] for a in range(3)]
        sums_b = [
            sum(depth_ref[3 * a + b : 3 * a + b + 1, :] * rows[a] for a in range(3))
            for b in range(3)
        ]
        total = across(sums_b[2], sums_b[1], sums_b[0])[0:TW]
        moved = [pltpu.roll(own_row, USED - 1, 0), own_row, pltpu.roll(own_row, 1, 0)]
        taps = []
        for a in range(3):
            hid_row = hid_ref[i + 1 + a]
            for b in range(3):
                taps.append(sums[3 * a + b] + fold(hid_row * moved[b]))
        rounded = total.astype(jnp.bfloat16)
        hgrad_ref[i] = rounded
        taps.append(sums[9] + fold(rounded.astype(jnp.float32)))
        taps.append(sums[10] + fold(center_row))
        return tuple(taps)

    sums = lax.fori_loop(0, TH, grad_row, (jnp.zeros((8, HID), jnp.float32),) * 11)
    for n in range(11):
        keep_row(12 + 2 * n, jnp.sum(sums[n], 0, keepdims=True) * scale_base)

    hidden_grad = hgrad_ref[...].reshape(TH * TW, HID)
    own_standard = standard_ref[...]
    expand_part = tn(normed_ref[...], hidden_grad) * scale_base
    normed_grad = nt(hidden_grad, expand_ref[...])
    fgrad = own_grad.astype(jnp.float32)
    for n, value in enumerate((fgrad, normed_grad * own_standard, normed_grad)):
        at = rest_row(34 + n)
        rest_ref[at : at + 1, 0:D1] = jnp.sum(value, 0, keepdims=True) * scale_base
    scaled = normed_grad * gain_ref[...]
    input_grad = fgrad + scaling_ref[...] * (
        scaled
        - jnp.mean(scaled, -1, keepdims=True)
        - own_standard * jnp.mean(scaled * own_standard, -1, keepdims=True)
    )
    input_grad_ref[...] = input_grad.astype(jnp.bfloat16).reshape(TH, TW, D1)

    even_core = row_index % 2 == 0

    def keep(part, pairs):
        for n in range(0, len(pairs), 2):
            mine = [jnp.where(even_core, even, odd) for even, odd in pairs[n : n + 2]]
            other = [jnp.where(even_core, odd, even) for even, odd in pairs[n : n + 2]]
            if n + 2 == len(pairs):
                other[1] = split_rest(other[1])
            at = slice(8 * n, 8 * n + 16)
            mine_ref[part, at, :] = jnp.concatenate(mine, axis=0)
            other_ref[part, at, :] = jnp.concatenate(other, axis=0).astype(jnp.bfloat16)

    upper = lax.broadcasted_iota(jnp.int32, (8, 128), 0) < 4
    for part in range(NEAR):
        zl, within = part // 8, 8 * (part % 8)
        pairs = []
        for zh in range(4):
            first = 128 * (2 * zh + zl) + within
            for j in range(3):
                lanes = slice(128 * j, 128 * j + 128)
                pairs.append(
                    (
                        linear_ref[first : first + 8, lanes],
                        linear_ref[first + 64 : first + 72, lanes],
                    )
                )
        lanes = slice(0, 128) if part < 8 else slice(128, 256)
        expands = expand_part[within : within + 8, lanes]
        reduces = reduce_part[within : within + 8, lanes]
        pairs.append(
            (
                jnp.where(upper, expands, pltpu.roll(reduces, 4, 0)),
                jnp.where(upper, pltpu.roll(expands, 4, 0), reduces),
            )
        )
        rest = rest_ref[8 * part : 8 * part + 8, :]
        pairs.append((rest, pltpu.roll(rest, 4, 0)))
        keep(part, pairs)


def row_kernel(
    joined_ref, block_ref, later_ref, far_ref, near_ref, joined_buf, block_buf, later_buf, sems
):
    copies = []
    for n, (source, target) in enumerate(
        ((joined_ref, joined_buf), (block_ref, block_buf), (later_ref, later_buf))
    ):
        for last in range(2):
            rows = slice(TH - EDGE, TH) if last else slice(0, EDGE)
            copy = pltpu.make_async_copy(source.at[rows], target.at[last], sems.at[2 * n + last])
            copy.start()
            copies.append(copy)
    for copy in copies:
        copy.wait()
    even = lax.axis_index("row") % 2 == 0
    for buf, lanes in (
        (joined_buf, slice(0, DEC)),
        (block_buf, slice(DEC, DEC + D1)),
        (later_buf, slice(DEC + D1, DEC + 2 * D1)),
    ):
        first = buf[0].astype(jnp.float32)
        last = buf[1].astype(jnp.float32)
        far_ref[:, :, lanes] = jnp.where(even, first, last).astype(jnp.bfloat16)
        near_ref[:, :, lanes] = jnp.where(even, last, first).astype(jnp.bfloat16)


def row_borders(joined, block, later):
    vmem = pl.BlockSpec(memory_space=pltpu.VMEM)
    out = jax.ShapeDtypeStruct((EDGE, TW, DEC + 2 * D1), jnp.bfloat16)
    return pl.pallas_call(
        row_kernel,
        out_shape=(out, out),
        in_specs=[pl.BlockSpec(memory_space=pltpu.HBM)] * 3,
        out_specs=(vmem, vmem),
        scratch_shapes=[pltpu.VMEM((2, EDGE) + a.shape[1:], a.dtype) for a in (joined, block, later)]
        + [pltpu.SemaphoreType.DMA((6,))],
        compiler_params=pltpu.CompilerParams(vmem_limit_bytes=56 * 2**20),
        name="row_borders",
    )(joined, block, later)


def column_kernel(joined_ref, block_ref, later_ref, top_ref, bottom_ref, far_ref, near_ref):
    even = lax.axis_index("col") % 2 == 0
    own_rows = slice(EDGE, EDGE + TH)
    for ref, rows, lanes in (
        (joined_ref, own_rows, slice(0, DEC)),
        (block_ref, own_rows, slice(DEC, DEC + D1)),
        (later_ref, own_rows, slice(DEC + D1, DEC + 2 * D1)),
        (top_ref, slice(0, EDGE), slice(0, DEC + 2 * D1)),
        (bottom_ref, slice(EDGE + TH, ROWS), slice(0, DEC + 2 * D1)),
    ):
        first = ref[:, 0:16].astype(jnp.float32)[:, 0:EDGE]
        last = ref[:, TW - 16 : TW].astype(jnp.float32)[:, 16 - EDGE : 16]
        far_ref[rows, :, lanes] = jnp.where(even, first, last).astype(jnp.bfloat16)
        near_ref[rows, :, lanes] = jnp.where(even, last, first).astype(jnp.bfloat16)


def tile_pass(height, width, *operands):
    sds = jax.ShapeDtypeStruct
    bf16, f32 = jnp.bfloat16, jnp.float32
    vmem = pltpu.VMEM
    return pl.pallas_call(
        functools.partial(tile_kernel, height, width),
        out_shape=(
            sds((TH, TW, D1), bf16),
            sds((COARSE[0], D2), bf16),
            sds((COARSE[1], D3), bf16),
            sds((COARSE[2], D4), bf16),
            sds((NEAR, PART_ROWS, 128), f32),
            sds((NEAR, PART_ROWS, 128), bf16),
        ),
        in_specs=[pl.BlockSpec(memory_space=vmem)] * len(operands),
        out_specs=(pl.BlockSpec(memory_space=vmem),) * 6,
        scratch_shapes=[
            vmem((20, USED, HID), f32),
            vmem((18, USED, HID), f32),
            vmem((18, TW, HID), bf16),
            vmem((18, USED, HID), f32),
            vmem((TH, TW, HID), bf16),
            vmem((D1 + D2 + D3 + D4, DEC), f32),
            vmem((128, 128), f32),
        ],
        compiler_params=pltpu.CompilerParams(vmem_limit_bytes=28 * 2**20),
        name="tile_pass",
    )(*operands)


def near_kernel(received_ref, out_ref):
    total = jnp.sum(received_ref[...].astype(jnp.float32), 0)
    share = total[LINEAR_ROWS : LINEAR_ROWS + 8]
    rest = total[LINEAR_ROWS + 8 :]
    rest = pltpu.roll(join_rest(rest), 6, 0)
    row = lax.broadcasted_iota(jnp.int32, (8, 128), 0)
    for zh in range(4):
        pieces = [total[24 * zh + 8 * j : 24 * zh + 8 * j + 8] for j in range(3)]
        for yh in range(4):
            part = rest
            for j in range(3):
                shift = (2 * j - 2 * yh) % 8
                moved = pltpu.roll(pieces[j], shift, 0) if shift else pieces[j]
                part = jnp.where((row >= 2 * j) & (row < 2 * j + 2), moved, part)
            out_ref[4 * zh + yh, 0:8, :] = part
            out_ref[4 * zh + yh, 8:16, :] = share


def final_kernel(received_ref, out_ref):
    total = jnp.sum(received_ref[...], 0)
    for n in range(out_ref.shape[0]):
        for i in range(4):
            out_ref[n, i] = total[8 + 2 * i : 10 + 2 * i]
        out_ref[n, 4] = total[6:8]


def result_kernel(
    all_ref,
    received_ref,
    input_grad,
    grad2,
    grad3,
    grad4,
    input_out,
    out2,
    out3,
    out4,
    linear_ref,
    biases_ref,
    expand_ref,
    reduce_ref,
    depth_ref,
    hidden_ref,
    channel_ref,
):
    input_out[...] = input_grad[...]
    out2[...] = grad2[...]
    out3[...] = grad3[...]
    last = grad4[...].astype(jnp.float32)
    for i in range(out4.shape[0]):
        out4[i] = last[4 * i : 4 * i + 4].astype(jnp.bfloat16)
    total = jnp.sum(received_ref[:, 0:8, :], 0)
    for p in range(2):
        for j in range(3):
            linear_ref[3 * p + j : 3 * p + j + 1, :] = total[2 * j + p : 2 * j + p + 1, :]

    for share in range(2 * NEAR):
        lanes = slice(0, 128) if share < NEAR else slice(128, 256)
        first = 4 * (share % NEAR)
        for i in range(2):
            rows = slice(first + 2 * i, first + 2 * i + 2)
            expand_ref[rows, lanes] = all_ref[share, i]
            reduce_ref[rows, lanes] = all_ref[share, 2 + i]

    def row(n):
        return all_ref[n // 2, 4, n % 2 : n % 2 + 1, :]

    for k in range(4):
        for j in range(3):
            biases_ref[k : k + 1, 128 * j : 128 * j + 128] = row(3 * k + j)
    for t in range(9):
        for j in range(2):
            depth_ref[t : t + 1, 128 * j : 128 * j + 128] = row(12 + 2 * t + j)
    for t in range(2):
        for j in range(2):
            hidden_ref[t : t + 1, 128 * j : 128 * j + 128] = row(30 + 2 * t + j)
    for t in range(3):
        channel_ref[t : t + 1, :] = row(34 + t)[:, 0:D1]


def in_vmem(kernel, name, out_shape, *operands, scratch=()):
    vmem = pl.BlockSpec(memory_space=pltpu.VMEM)
    return pl.pallas_call(
        kernel,
        out_shape=out_shape,
        in_specs=[vmem] * len(operands),
        out_specs=jax.tree.map(lambda _: vmem, out_shape),
        scratch_shapes=scratch,
        compiler_params=pltpu.CompilerParams(vmem_limit_bytes=16 * 2**20),
        name=name,
    )(*operands)


def chip_kernel(mine_ref, received_ref, out_ref):
    plain = LINEAR_ROWS + 8
    received = received_ref[...].astype(jnp.float32)
    total = mine_ref[:, 0:plain, :] + received[:, 0:plain]
    rest = split_rest(mine_ref[:, plain:, :] + join_rest(received[:, plain:]))
    out_ref[...] = jnp.concatenate([total, rest], axis=1).astype(jnp.bfloat16)


def device_groups(chips, cols):
    half_z, half_y = range(chips // 2), range(cols // XS // 2)
    two, xs = range(2), range(XS)

    def device(zh, zl, core, yh, yl, x):
        return (2 * (2 * zh + zl) + core) * cols + XS * (2 * yh + yl) + x

    near = [
        [device(zh, zl, core, yh, yl, x) for zl in two for yl in two for x in xs]
        for core in two
        for zh in half_z
        for yh in half_y
    ]
    far = [
        [device(zh, zl, core, yh, yl, x) for zh in half_z for yh in half_y]
        for core in two
        for zl in two
        for yl in two
        for x in xs
    ]
    both = [
        [device(zh, zl, core, yh, yl, x) for zl in two for yl in two for x in xs for core in two]
        for zh in half_z
        for yh in half_y
    ]
    return near, far, both


def sum_over_mesh(mine, other, grads):
    rows = lax.axis_size("row")
    cols = lax.axis_size("col")
    sds = jax.ShapeDtypeStruct
    f32 = jnp.float32
    near, far, both = device_groups(rows // 2, cols)

    def exchange(parts, groups):
        return lax.all_to_all(parts, ("row", "col"), 0, 0, tiled=True, axis_index_groups=groups)

    received = lax.ppermute(other, "row", [(i, i ^ 1) for i in range(rows)])
    chip = in_vmem(chip_kernel, "chip_sums", sds(other.shape, other.dtype), mine, received)
    parts = in_vmem(near_kernel, "near_sums", sds((16, 16, 128), f32), exchange(chip, near))
    received = exchange(parts, far)
    share = in_vmem(final_kernel, "final_sums", sds((2 * NEAR, 5, 2, 128), f32), received)
    everything = exchange(share, both)
    *tiles, linear, biases, expand, reduce, depth, hidden, channel = in_vmem(
        result_kernel,
        "results",
        (
            *(sds(grad.shape, grad.dtype) for grad in grads[:3]),
            sds((TH // 8, TW // 8, D4), jnp.bfloat16),
            sds((6, 128), f32),
            sds((4, DEC), f32),
            sds((D1, HID), f32),
            sds((D1, HID), f32),
            sds((9, HID), f32),
            sds((2, HID), f32),
            sds((3, D1), f32),
        ),
        everything,
        received,
        *grads,
    )
    return tiles, (linear.reshape(-1), biases, expand, reduce.T, depth, hidden, channel)


def swap_edges(to_far, to_near, axis):
    devices = lax.axis_size(axis)
    even = lax.axis_index(axis) % 2 == 0
    near = [(i, i ^ 1) for i in range(devices)]
    far = [(i, i + 1) for i in range(1, devices - 1, 2)]
    far = far + [(j, i) for i, j in far]
    from_far = lax.ppermute(to_far, axis, far)
    from_near = lax.ppermute(to_near, axis, near)
    return jnp.where(even, from_far, from_near), jnp.where(even, from_near, from_far)


def local(
    joined_grad,
    join_weight,
    linear_first,
    linear_second,
    linear_third,
    linear_fourth,
    feature_second,
    feature_third,
    feature_fourth,
    block_input,
    later_grad,
    norm_gain,
    norm_shift,
    expand_weight,
    expand_bias,
    depth_weight,
    depth_bias,
    reduce_weight,
    reduce_bias,
):
    height = TH * lax.axis_size("row")
    width = TW * lax.axis_size("col")
    top, bottom = swap_edges(*row_borders(joined_grad, block_input, later_grad), "row")
    column = jax.ShapeDtypeStruct((ROWS, EDGE, DEC + 2 * D1), jnp.bfloat16)
    left, right = swap_edges(
        *in_vmem(
            column_kernel,
            "column_borders",
            (column, column),
            joined_grad,
            block_input,
            later_grad,
            top,
            bottom,
        ),
        "col",
    )
    early = own_pass(
        height,
        width,
        joined_grad,
        block_input,
        later_grad,
        top,
        bottom,
        join_weight,
        linear_first,
        reduce_weight.T,
        norm_gain.reshape(1, -1),
        norm_shift.reshape(1, -1),
        expand_weight,
        expand_bias.reshape(1, -1),
        feature_second.reshape(-1, D2),
        feature_third.reshape(-1, D3),
        feature_fourth.reshape(-1, D4),
    )
    gap = jnp.zeros((ROWS, PITCH - TW - 2 * EDGE, left.shape[2]), left.dtype)
    side = jnp.concatenate([right, left, gap], axis=1)

    input_grad, grad2, grad3, grad4, mine, other = tile_pass(
        height,
        width,
        *early,
        block_input,
        side,
        join_weight,
        linear_first,
        linear_second,
        linear_third,
        linear_fourth,
        norm_gain.reshape(1, -1),
        norm_shift.reshape(1, -1),
        expand_weight,
        expand_bias.reshape(1, -1),
        depth_weight,
        depth_bias.reshape(1, -1),
        reduce_weight.T,
        reduce_bias.reshape(1, -1),
    )
    tiles, sums = sum_over_mesh(mine, other, (input_grad, grad2, grad3, grad4))
    input_grad, grad2, grad3, grad4 = tiles
    return (
        input_grad,
        grad2.reshape(TH // 2, TW // 2, D2),
        grad3.reshape(TH // 4, TW // 4, D3),
        grad4,
        *sums,
    )


def solution(mesh):
    tiles = P("row", "col", None)
    return jax.shard_map(
        local,
        mesh=mesh,
        in_specs=(tiles,) + (P(),) * 5 + (tiles,) * 5 + (P(),) * 8,
        out_specs=(tiles,) * 4 + (P(("row", "col")),) + (P(),) * 6,
        check_vma=False,
    )
```

```python
import functools
import math

import jax
import jax.numpy as jnp
from jax import lax
from jax.experimental import pallas as pl
from jax.experimental.pallas import tpu as pltpu
from jax.sharding import PartitionSpec as P

D1 = 64
D2 = 128
D3 = 320
D4 = 512
HID = 256
DEC = 384
TH = 16
TW = 32

EDGE = 4
ROWS = TH + 2 * EDGE
PITCH = 48
USED = 40
COARSE = (128, 32, 8)

XS = 4
NEAR = 16
LINEAR_ROWS = 96
PART_ROWS = LINEAR_ROWS + 16

norm_eps = 1e-06
inv_root_two = 0.7071067811865476
inv_root_tau = 0.3989422804014327


def nt(left, right):
    return lax.dot_general(left, right, (((1,), (1,)), ((), ())), preferred_element_type=jnp.float32)


def tn(left, right):
    return lax.dot_general(left, right, (((0,), (0,)), ((), ())), preferred_element_type=jnp.float32)


def add3(terms):
    return terms[0] + terms[1] + terms[2]


def nn(left, right):
    return jnp.dot(left, right, preferred_element_type=jnp.float32)


def rest_row(n):
    return 8 * (n // 4) + 4 * (n // 2 % 2) + n % 2


def place(position, pitch):
    row = jnp.floor((position + 0.5) * (1.0 / pitch))
    col = position - pitch * row
    if pitch < TW:
        col = jnp.where(col < EDGE, col + TW, col - 2 * EDGE)
    elif pitch > TW:
        col = jnp.where(col < TW + EDGE, col, col - USED)
    return row - EDGE, col


def count_up(shape, axis):
    return lax.broadcasted_iota(jnp.int32, shape, axis).astype(jnp.float32)


def rows_inside(halo, height):
    row_index = lax.axis_index("row")
    above = jnp.where(row_index > 0, 1.0, 0.0)
    below = jnp.where(row_index < height // TH - 1, 1.0, 0.0)
    return [above] * halo + [None] * TH + [below] * halo


def sides_inside(width):
    col_index = lax.axis_index("col")
    before = jnp.where(col_index > 0, 1.0, 0.0)
    after = jnp.where(col_index < width // TW - 1, 1.0, 0.0)
    right = lax.broadcasted_iota(jnp.int32, (2 * EDGE, HID), 0) < EDGE
    return jnp.where(right, after, before)


def normalize(values, gain, shift):
    center = jnp.mean(values, -1, keepdims=True)
    offset = values - center
    spread = jnp.mean(jnp.square(offset), -1, keepdims=True)
    scaling = lax.rsqrt(spread + norm_eps)
    standard = offset * scaling
    return (standard * gain + shift).astype(jnp.bfloat16), standard, scaling


def expand(normed, weight, bias):
    return (nn(normed, weight) + bias).astype(jnp.bfloat16).astype(jnp.float32)


def regroup(channels_last):
    source = lax.broadcasted_iota(jnp.int32, (128, 128), 0)
    target = lax.broadcasted_iota(jnp.int32, (128, 128), 1)
    wanted = (
        (target & 64)
        + 8 * (target & 6)
        + ((target & 32) >> 2)
        + ((target & 24) >> 2)
        + (target & 1)
    )
    moves = jnp.where(source == wanted, 1.0, 0.0).astype(jnp.bfloat16)
    pieces = []
    for first in range(0, channels_last.shape[1], 128):
        piece = channels_last[:, first : first + 128]
        size = piece.shape[1]
        pieces.append(nn(piece, moves[0:size, 0:size]))
    return jnp.concatenate(pieces, axis=1).astype(jnp.bfloat16)


def split_rest(rest):
    axis = rest.ndim - 2
    row = lax.broadcasted_iota(jnp.int32, rest.shape, axis)
    high = rest.astype(jnp.bfloat16).astype(jnp.float32)
    low = jnp.where(row < 2, rest - high, 0.0)
    return jnp.where(row < 2, high, pltpu.roll(low, 4, axis))


def join_rest(rest):
    return rest + pltpu.roll(rest, 4, rest.ndim - 2)


def pool_matrix(scale_index, pitch, row_index, col_index, height, width):
    factor = 2**scale_index
    coarse_rows, coarse_cols = TH // factor, TW // factor
    count = coarse_rows * coarse_cols
    row, col = place(count_up((1, ROWS * pitch), 1), pitch)
    target = count_up((count, 1), 0)
    target_row = jnp.floor((target + 0.5) * (1.0 / coarse_cols))
    target_col = target - coarse_cols * target_row
    row0 = (row_index * TH).astype(jnp.float32)
    col0 = (col_index * TW).astype(jnp.float32)
    at_row = jnp.clip((row + row0 + 0.5) * (1.0 / factor) - 0.5, 0.0, height // factor - 1.0)
    at_col = jnp.clip((col + col0 + 0.5) * (1.0 / factor) - 0.5, 0.0, width // factor - 1.0)
    at_row = at_row - row0 * (1.0 / factor)
    at_col = at_col - col0 * (1.0 / factor)
    weight = jnp.maximum(1.0 - jnp.abs(at_row - target_row), 0.0) * jnp.maximum(
        1.0 - jnp.abs(at_col - target_col), 0.0
    )
    return weight.astype(jnp.bfloat16)


def add_later(projection, linear, later):
    later = later.reshape(-1, D1).astype(jnp.float32)
    return (nt(projection, linear) + later).astype(jnp.bfloat16)


def own_kernel(
    height,
    width,
    joined_ref,
    block_ref,
    later_ref,
    top_ref,
    bottom_ref,
    join_ref,
    first_ref,
    reduce_ref,
    gain_ref,
    shift_ref,
    expand_ref,
    expand_bias_ref,
    feature2_ref,
    feature3_ref,
    feature4_ref,
    pooled_ref,
    side_matrix_ref,
    projection_ref,
    grad_ref,
    act_grad_ref,
    hidden_ref,
    normed_ref,
    standard_ref,
    scaling_ref,
    grouped2_ref,
    grouped3_ref,
    grouped4_ref,
    wide_ref,
):
    row_index = lax.axis_index("row")
    col_index = lax.axis_index("col")
    wide_ref[EDGE : EDGE + TH] = joined_ref[...]
    wide_ref[0:EDGE] = top_ref[:, :, 0:DEC]
    wide_ref[EDGE + TH :] = bottom_ref[:, :, 0:DEC]

    def matrix(pitch):
        return jnp.concatenate(
            [pool_matrix(k, pitch, row_index, col_index, height, width) for k in (1, 2, 3)], axis=0
        )

    pooled_ref[...] = nn(matrix(TW), wide_ref[...].reshape(ROWS * TW, DEC))
    side_matrix_ref[...] = matrix(PITCH - TW)
    projection = nt(wide_ref[3:21].reshape(18 * TW, DEC), join_ref[0:DEC, :]).astype(jnp.bfloat16)
    projection_ref[...] = projection[TW : 17 * TW]
    lanes = slice(DEC + D1, DEC + 2 * D1)
    later = jnp.concatenate(
        [top_ref[3:4, :, lanes], later_ref[...], bottom_ref[0:1, :, lanes]], axis=0
    )
    feature_grad = add_later(projection, first_ref[...], later)
    grad_ref[...] = feature_grad[TW : 17 * TW]
    act_grad_ref[...] = nn(feature_grad, reduce_ref[...]).reshape(18, TW, HID)

    values = jnp.concatenate(
        [top_ref[2:4, :, DEC : DEC + D1], block_ref[...], bottom_ref[0:2, :, DEC : DEC + D1]], axis=0
    )
    normed, standard, scaling = normalize(
        values.reshape(20 * TW, D1).astype(jnp.float32), gain_ref[...], shift_ref[...]
    )
    hidden = expand(normed, expand_ref[...], expand_bias_ref[...])
    hidden = hidden.reshape(20, TW, HID)
    for i, good in enumerate(rows_inside(2, height)):
        hidden_ref[i] = hidden[i] if good is None else hidden[i] * good
    own = slice(2 * TW, 18 * TW)
    normed_ref[...] = normed[own]
    standard_ref[...] = standard[own]
    scaling_ref[...] = jnp.broadcast_to(scaling[own], (TH * TW, D1))
    grouped2_ref[...] = regroup(feature2_ref[...])
    grouped3_ref[...] = regroup(feature3_ref[...])
    grouped4_ref[...] = regroup(feature4_ref[...])


def own_pass(height, width, *operands):
    sds = jax.ShapeDtypeStruct
    bf16, f32 = jnp.bfloat16, jnp.float32
    pixels = TH * TW
    return in_vmem(
        functools.partial(own_kernel, height, width),
        "own_pass",
        (
            sds((sum(COARSE), DEC), f32),
            sds((sum(COARSE), ROWS * (PITCH - TW)), bf16),
            sds((pixels, DEC), bf16),
            sds((pixels, D1), bf16),
            sds((18, TW, HID), f32),
            sds((20, TW, HID), f32),
            sds((pixels, D1), bf16),
            sds((pixels, D1), f32),
            sds((pixels, D1), f32),
            sds((COARSE[0], D2), bf16),
            sds((COARSE[1], D3), bf16),
            sds((COARSE[2], D4), bf16),
        ),
        *operands,
        scratch=[pltpu.VMEM((ROWS, TW, DEC), bf16)],
    )


def tile_kernel(
    height,
    width,
    pooled_ref,
    side_matrix_ref,
    own_projection_ref,
    own_grad_ref,
    own_act_grad_ref,
    own_hidden_ref,
    normed_ref,
    standard_ref,
    scaling_ref,
    feature2_ref,
    feature3_ref,
    feature4_ref,
    block_ref,
    side_ref,
    join_ref,
    first_ref,
    second_ref,
    third_ref,
    fourth_ref,
    gain_ref,
    shift_ref,
    expand_ref,
    expand_bias_ref,
    depth_ref,
    depth_bias_ref,
    reduce_ref,
    reduce_bias_ref,
    input_grad_ref,
    grad2_ref,
    grad3_ref,
    grad4_ref,
    mine_ref,
    other_ref,
    hid_ref,
    slope_ref,
    act_ref,
    pre_ref,
    hgrad_ref,
    linear_ref,
    rest_ref,
):
    row_index = lax.axis_index("row")
    scale_base = 1.0 / math.sqrt(height * width)

    rest_ref[...] = jnp.zeros_like(rest_ref)

    def keep_row(row, value):
        for piece in range(value.shape[1] // 128):
            at = rest_row(row + piece)
            rest_ref[at : at + 1, :] = value[:, 128 * piece : 128 * piece + 128]

    side_joined = side_ref[:, :, 0:DEC].reshape(ROWS * (PITCH - TW), DEC)
    pooled = (pooled_ref[...] + nn(side_matrix_ref[...], side_joined)).astype(jnp.bfloat16)
    start = 0
    base = D1
    for k, linear, feature, grad in (
        (1, second_ref, feature2_ref, grad2_ref),
        (2, third_ref, feature3_ref, grad3_ref),
        (3, fourth_ref, feature4_ref, grad4_ref),
    ):
        count = COARSE[k - 1]
        channels = linear.shape[0]
        projection = nt(pooled[start : start + count], join_ref[k * DEC : (k + 1) * DEC, :]).astype(
            jnp.bfloat16
        )
        grad[...] = nt(projection, linear[...]).astype(jnp.bfloat16)
        linear_ref[base : base + channels, :] = tn(feature[...], projection) * (2**k * scale_base)
        keep_row(
            3 * k,
            jnp.sum(projection.astype(jnp.float32), 0, keepdims=True) * (2**k * scale_base),
        )
        start += count
        base += channels

    values = side_ref[2:22, :, DEC : DEC + D1].astype(jnp.float32)[:, 0 : 2 * EDGE]
    normed, _, _ = normalize(values.reshape(20 * 2 * EDGE, D1), gain_ref[...], shift_ref[...])
    hidden = expand(normed, expand_ref[...], expand_bias_ref[...])
    hid_ref[:, 0:TW] = own_hidden_ref[...]
    hidden = hidden.reshape(20, 2 * EDGE, HID)
    sides = sides_inside(width)
    for i, good in enumerate(rows_inside(2, height)):
        hid_ref[i, TW:] = hidden[i] * (sides if good is None else sides * good)

    def across(before, same, after):
        return pltpu.roll(before, 1, 0) + same + pltpu.roll(after, USED - 1, 0)

    def conv_row(i, carry):
        rows = [hid_ref[i + a] for a in range(3)]
        sums = [
            add3([depth_ref[3 * a + b : 3 * a + b + 1, :] * rows[a] for a in range(3)])
            for b in range(3)
        ]
        conv = across(*sums) + depth_bias_ref[...]
        cumulative = 0.5 * (1.0 + lax.erf(conv * inv_root_two))
        density = inv_root_tau * jnp.exp(-0.5 * conv * conv)
        act_ref[i] = (conv * cumulative)[0:TW].astype(jnp.bfloat16)
        slope_ref[i] = cumulative + conv * density
        return carry

    lax.fori_loop(0, 18, conv_row, 0)

    beside = slice(0, 2 * EDGE)
    projection = nt(
        side_ref[3:21, :, 0:DEC].reshape(18 * (PITCH - TW), DEC), join_ref[0:DEC, :]
    ).astype(jnp.bfloat16)
    feature_grad = add_later(
        projection, first_ref[...], side_ref[3:21, :, DEC + D1 : DEC + 2 * D1]
    )
    act_grad = nn(feature_grad, reduce_ref[...]).reshape(18, PITCH - TW, HID)[:, beside]
    for i, good in enumerate(rows_inside(1, height)):
        for cols, part in ((slice(0, TW), own_act_grad_ref[i]), (slice(TW, USED), act_grad[i])):
            pre_grad = (part * slope_ref[i, cols, :]).astype(jnp.bfloat16).astype(jnp.float32)
            if cols.start:
                pre_grad = pre_grad * sides
            pre_ref[i, cols, :] = pre_grad if good is None else pre_grad * good

    activated = act_ref[1:17].reshape(TH * TW, HID)
    own_projection = own_projection_ref[...]
    own_grad = own_grad_ref[...]
    own_block = block_ref[...].reshape(TH * TW, D1).astype(jnp.float32)
    features = (own_block + (nt(activated, reduce_ref[...]) + reduce_bias_ref[...])).astype(
        jnp.bfloat16
    )
    linear_ref[0:D1, :] = tn(regroup(features), own_projection) * scale_base
    keep_row(0, jnp.sum(own_projection.astype(jnp.float32), 0, keepdims=True) * scale_base)
    reduce_part = tn(own_grad, activated) * scale_base

    def fold(value):
        return jnp.sum(value.reshape(-1, 8, HID), 0)

    def grad_row(i, sums):
        center_row = pre_ref[i + 1, 0:TW, :]
        own_row = jnp.concatenate([center_row, jnp.zeros((USED - TW, HID), jnp.float32)], axis=0)
        rows = [pre_ref[i + 2 - a] for a in range(3)]
        sums_b = [
            add3([depth_ref[3 * a + b : 3 * a + b + 1, :] * rows[a] for a in range(3)])
            for b in range(3)
        ]
        total = across(sums_b[2], sums_b[1], sums_b[0])[0:TW]
        moved = [pltpu.roll(own_row, USED - 1, 0), own_row, pltpu.roll(own_row, 1, 0)]
        taps = []
        for a in range(3):
            hid_row = hid_ref[i + 1 + a]
            for b in range(3):
                taps.append(sums[3 * a + b] + fold(hid_row * moved[b]))
        rounded = total.astype(jnp.bfloat16)
        hgrad_ref[i] = rounded
        taps.append(sums[9] + fold(rounded.astype(jnp.float32)))
        taps.append(sums[10] + fold(center_row))
        return tuple(taps)

    sums = lax.fori_loop(0, TH, grad_row, (jnp.zeros((8, HID), jnp.float32),) * 11)
    for n in range(11):
        keep_row(12 + 2 * n, jnp.sum(sums[n], 0, keepdims=True) * scale_base)

    hidden_grad = hgrad_ref[...].reshape(TH * TW, HID)
    own_standard = standard_ref[...]
    expand_part = tn(normed_ref[...], hidden_grad) * scale_base
    normed_grad = nt(hidden_grad, expand_ref[...])
    fgrad = own_grad.astype(jnp.float32)
    for n, value in enumerate((fgrad, normed_grad * own_standard, normed_grad)):
        at = rest_row(34 + n)
        rest_ref[at : at + 1, 0:D1] = jnp.sum(value, 0, keepdims=True) * scale_base
    scaled = normed_grad * gain_ref[...]
    input_grad = fgrad + scaling_ref[...] * (
        scaled
        - jnp.mean(scaled, -1, keepdims=True)
        - own_standard * jnp.mean(scaled * own_standard, -1, keepdims=True)
    )
    input_grad_ref[...] = input_grad.astype(jnp.bfloat16).reshape(TH, TW, D1)

    even_core = row_index % 2 == 0

    def keep(part, pairs):
        for n in range(0, len(pairs), 2):
            mine = [jnp.where(even_core, even, odd) for even, odd in pairs[n : n + 2]]
            other = [jnp.where(even_core, odd, even) for even, odd in pairs[n : n + 2]]
            if n + 2 == len(pairs):
                other[1] = split_rest(other[1])
            at = slice(8 * n, 8 * n + 16)
            mine_ref[part, at, :] = jnp.concatenate(mine, axis=0)
            other_ref[part, at, :] = jnp.concatenate(other, axis=0).astype(jnp.bfloat16)

    upper = lax.broadcasted_iota(jnp.int32, (8, 128), 0) < 4
    for part in range(NEAR):
        zl, within = part // 8, 8 * (part % 8)
        pairs = []
        for zh in range(4):
            first = 128 * (2 * zh + zl) + within
            for j in range(3):
                lanes = slice(128 * j, 128 * j + 128)
                pairs.append(
                    (
                        linear_ref[first : first + 8, lanes],
                        linear_ref[first + 64 : first + 72, lanes],
                    )
                )
        lanes = slice(0, 128) if part < 8 else slice(128, 256)
        expands = expand_part[within : within + 8, lanes]
        reduces = reduce_part[within : within + 8, lanes]
        pairs.append(
            (
                jnp.where(upper, expands, pltpu.roll(reduces, 4, 0)),
                jnp.where(upper, pltpu.roll(expands, 4, 0), reduces),
            )
        )
        rest = rest_ref[8 * part : 8 * part + 8, :]
        pairs.append((rest, pltpu.roll(rest, 4, 0)))
        keep(part, pairs)


def row_kernel(
    joined_ref, block_ref, later_ref, far_ref, near_ref, joined_buf, block_buf, later_buf, sems
):
    copies = []
    for n, (source, target) in enumerate(
        ((joined_ref, joined_buf), (block_ref, block_buf), (later_ref, later_buf))
    ):
        for last in range(2):
            rows = slice(TH - EDGE, TH) if last else slice(0, EDGE)
            copy = pltpu.make_async_copy(source.at[rows], target.at[last], sems.at[2 * n + last])
            copy.start()
            copies.append(copy)
    for copy in copies:
        copy.wait()
    even = lax.axis_index("row") % 2 == 0
    for buf, lanes in (
        (joined_buf, slice(0, DEC)),
        (block_buf, slice(DEC, DEC + D1)),
        (later_buf, slice(DEC + D1, DEC + 2 * D1)),
    ):
        first = buf[0].astype(jnp.float32)
        last = buf[1].astype(jnp.float32)
        far_ref[:, :, lanes] = jnp.where(even, first, last).astype(jnp.bfloat16)
        near_ref[:, :, lanes] = jnp.where(even, last, first).astype(jnp.bfloat16)


def row_borders(joined, block, later):
    vmem = pl.BlockSpec(memory_space=pltpu.VMEM)
    out = jax.ShapeDtypeStruct((EDGE, TW, DEC + 2 * D1), jnp.bfloat16)
    return pl.pallas_call(
        row_kernel,
        out_shape=(out, out),
        in_specs=[pl.BlockSpec(memory_space=pltpu.HBM)] * 3,
        out_specs=(vmem, vmem),
        scratch_shapes=[pltpu.VMEM((2, EDGE) + a.shape[1:], a.dtype) for a in (joined, block, later)]
        + [pltpu.SemaphoreType.DMA((6,))],
        compiler_params=pltpu.CompilerParams(vmem_limit_bytes=56 * 2**20),
        name="row_borders",
    )(joined, block, later)


def column_kernel(joined_ref, block_ref, later_ref, top_ref, bottom_ref, far_ref, near_ref):
    even = lax.axis_index("col") % 2 == 0
    own_rows = slice(EDGE, EDGE + TH)
    for ref, rows, lanes in (
        (joined_ref, own_rows, slice(0, DEC)),
        (block_ref, own_rows, slice(DEC, DEC + D1)),
        (later_ref, own_rows, slice(DEC + D1, DEC + 2 * D1)),
        (top_ref, slice(0, EDGE), slice(0, DEC + 2 * D1)),
        (bottom_ref, slice(EDGE + TH, ROWS), slice(0, DEC + 2 * D1)),
    ):
        first = ref[:, 0:16].astype(jnp.float32)[:, 0:EDGE]
        last = ref[:, TW - 16 : TW].astype(jnp.float32)[:, 16 - EDGE : 16]
        far_ref[rows, :, lanes] = jnp.where(even, first, last).astype(jnp.bfloat16)
        near_ref[rows, :, lanes] = jnp.where(even, last, first).astype(jnp.bfloat16)


def tile_pass(height, width, *operands):
    sds = jax.ShapeDtypeStruct
    bf16, f32 = jnp.bfloat16, jnp.float32
    vmem = pltpu.VMEM
    return pl.pallas_call(
        functools.partial(tile_kernel, height, width),
        out_shape=(
            sds((TH, TW, D1), bf16),
            sds((COARSE[0], D2), bf16),
            sds((COARSE[1], D3), bf16),
            sds((COARSE[2], D4), bf16),
            sds((NEAR, PART_ROWS, 128), f32),
            sds((NEAR, PART_ROWS, 128), bf16),
        ),
        in_specs=[pl.BlockSpec(memory_space=vmem)] * len(operands),
        out_specs=(pl.BlockSpec(memory_space=vmem),) * 6,
        scratch_shapes=[
            vmem((20, USED, HID), f32),
            vmem((18, USED, HID), f32),
            vmem((18, TW, HID), bf16),
            vmem((18, USED, HID), f32),
            vmem((TH, TW, HID), bf16),
            vmem((D1 + D2 + D3 + D4, DEC), f32),
            vmem((128, 128), f32),
        ],
        compiler_params=pltpu.CompilerParams(vmem_limit_bytes=28 * 2**20),
        name="tile_pass",
    )(*operands)


def near_kernel(received_ref, out_ref):
    total = jnp.sum(received_ref[...].astype(jnp.float32), 0)
    share = total[LINEAR_ROWS : LINEAR_ROWS + 8]
    rest = total[LINEAR_ROWS + 8 :]
    rest = pltpu.roll(join_rest(rest), 6, 0)
    row = lax.broadcasted_iota(jnp.int32, (8, 128), 0)
    for zh in range(4):
        pieces = [total[24 * zh + 8 * j : 24 * zh + 8 * j + 8] for j in range(3)]
        for yh in range(4):
            part = rest
            for j in range(3):
                shift = (2 * j - 2 * yh) % 8
                moved = pltpu.roll(pieces[j], shift, 0) if shift else pieces[j]
                part = jnp.where((row >= 2 * j) & (row < 2 * j + 2), moved, part)
            out_ref[4 * zh + yh, 0:8, :] = part
            out_ref[4 * zh + yh, 8:16, :] = share


def final_kernel(received_ref, out_ref):
    total = jnp.sum(received_ref[...], 0)
    for n in range(out_ref.shape[0]):
        for i in range(4):
            out_ref[n, i] = total[8 + 2 * i : 10 + 2 * i]
        out_ref[n, 4] = total[6:8]


def result_kernel(
    all_ref,
    received_ref,
    input_grad,
    grad2,
    grad3,
    grad4,
    input_out,
    out2,
    out3,
    out4,
    linear_ref,
    biases_ref,
    expand_ref,
    reduce_ref,
    depth_ref,
    hidden_ref,
    channel_ref,
):
    input_out[...] = input_grad[...]
    out2[...] = grad2[...]
    out3[...] = grad3[...]
    last = grad4[...].astype(jnp.float32)
    for i in range(out4.shape[0]):
        out4[i] = last[4 * i : 4 * i + 4].astype(jnp.bfloat16)
    total = jnp.sum(received_ref[:, 0:8, :], 0)
    for p in range(2):
        for j in range(3):
            linear_ref[3 * p + j : 3 * p + j + 1, :] = total[2 * j + p : 2 * j + p + 1, :]

    for share in range(2 * NEAR):
        lanes = slice(0, 128) if share < NEAR else slice(128, 256)
        first = 4 * (share % NEAR)
        for i in range(2):
            rows = slice(first + 2 * i, first + 2 * i + 2)
            expand_ref[rows, lanes] = all_ref[share, i]
            reduce_ref[rows, lanes] = all_ref[share, 2 + i]

    def row(n):
        return all_ref[n // 2, 4, n % 2 : n % 2 + 1, :]

    for k in range(4):
        for j in range(3):
            biases_ref[k : k + 1, 128 * j : 128 * j + 128] = row(3 * k + j)
    for t in range(9):
        for j in range(2):
            depth_ref[t : t + 1, 128 * j : 128 * j + 128] = row(12 + 2 * t + j)
    for t in range(2):
        for j in range(2):
            hidden_ref[t : t + 1, 128 * j : 128 * j + 128] = row(30 + 2 * t + j)
    for t in range(3):
        channel_ref[t : t + 1, :] = row(34 + t)[:, 0:D1]


def in_vmem(kernel, name, out_shape, *operands, scratch=()):
    vmem = pl.BlockSpec(memory_space=pltpu.VMEM)
    return pl.pallas_call(
        kernel,
        out_shape=out_shape,
        in_specs=[vmem] * len(operands),
        out_specs=jax.tree.map(lambda _: vmem, out_shape),
        scratch_shapes=scratch,
        compiler_params=pltpu.CompilerParams(vmem_limit_bytes=16 * 2**20),
        name=name,
    )(*operands)


def chip_kernel(mine_ref, received_ref, out_ref):
    plain = LINEAR_ROWS + 8
    received = received_ref[...].astype(jnp.float32)
    total = mine_ref[:, 0:plain, :] + received[:, 0:plain]
    rest = split_rest(mine_ref[:, plain:, :] + join_rest(received[:, plain:]))
    out_ref[...] = jnp.concatenate([total, rest], axis=1).astype(jnp.bfloat16)


def device_groups(chips, cols):
    half_z, half_y = range(chips // 2), range(cols // XS // 2)
    two, xs = range(2), range(XS)

    def device(zh, zl, core, yh, yl, x):
        return (2 * (2 * zh + zl) + core) * cols + XS * (2 * yh + yl) + x

    near = [
        [device(zh, zl, core, yh, yl, x) for zl in two for yl in two for x in xs]
        for core in two
        for zh in half_z
        for yh in half_y
    ]
    far = [
        [device(zh, zl, core, yh, yl, x) for zh in half_z for yh in half_y]
        for core in two
        for zl in two
        for yl in two
        for x in xs
    ]
    both = [
        [device(zh, zl, core, yh, yl, x) for zl in two for yl in two for x in xs for core in two]
        for zh in half_z
        for yh in half_y
    ]
    return near, far, both


def sum_over_mesh(mine, other, grads):
    rows = lax.axis_size("row")
    cols = lax.axis_size("col")
    sds = jax.ShapeDtypeStruct
    f32 = jnp.float32
    near, far, both = device_groups(rows // 2, cols)

    def exchange(parts, groups):
        return lax.all_to_all(parts, ("row", "col"), 0, 0, tiled=True, axis_index_groups=groups)

    received = lax.ppermute(other, "row", [(i, i ^ 1) for i in range(rows)])
    chip = in_vmem(chip_kernel, "chip_sums", sds(other.shape, other.dtype), mine, received)
    parts = in_vmem(near_kernel, "near_sums", sds((16, 16, 128), f32), exchange(chip, near))
    received = exchange(parts, far)
    share = in_vmem(final_kernel, "final_sums", sds((2 * NEAR, 5, 2, 128), f32), received)
    everything = exchange(share, both)
    *tiles, linear, biases, expand, reduce, depth, hidden, channel = in_vmem(
        result_kernel,
        "results",
        (
            *(sds(grad.shape, grad.dtype) for grad in grads[:3]),
            sds((TH // 8, TW // 8, D4), jnp.bfloat16),
            sds((6, 128), f32),
            sds((4, DEC), f32),
            sds((D1, HID), f32),
            sds((D1, HID), f32),
            sds((9, HID), f32),
            sds((2, HID), f32),
            sds((3, D1), f32),
        ),
        everything,
        received,
        *grads,
    )
    return tiles, (linear.reshape(-1), biases, expand, reduce.T, depth, hidden, channel)


def swap_edges(to_far, to_near, axis):
    devices = lax.axis_size(axis)
    even = lax.axis_index(axis) % 2 == 0
    near = [(i, i ^ 1) for i in range(devices)]
    far = [(i, i + 1) for i in range(1, devices - 1, 2)]
    far = far + [(j, i) for i, j in far]
    from_far = lax.ppermute(to_far, axis, far)
    from_near = lax.ppermute(to_near, axis, near)
    return jnp.where(even, from_far, from_near), jnp.where(even, from_near, from_far)


def local(
    joined_grad,
    join_weight,
    linear_first,
    linear_second,
    linear_third,
    linear_fourth,
    feature_second,
    feature_third,
    feature_fourth,
    block_input,
    later_grad,
    norm_gain,
    norm_shift,
    expand_weight,
    expand_bias,
    depth_weight,
    depth_bias,
    reduce_weight,
    reduce_bias,
):
    height = TH * lax.axis_size("row")
    width = TW * lax.axis_size("col")
    top, bottom = swap_edges(*row_borders(joined_grad, block_input, later_grad), "row")
    column = jax.ShapeDtypeStruct((ROWS, EDGE, DEC + 2 * D1), jnp.bfloat16)
    left, right = swap_edges(
        *in_vmem(
            column_kernel,
            "column_borders",
            (column, column),
            joined_grad,
            block_input,
            later_grad,
            top,
            bottom,
        ),
        "col",
    )
    early = own_pass(
        height,
        width,
        joined_grad,
        block_input,
        later_grad,
        top,
        bottom,
        join_weight,
        linear_first,
        reduce_weight.T,
        norm_gain.reshape(1, -1),
        norm_shift.reshape(1, -1),
        expand_weight,
        expand_bias.reshape(1, -1),
        feature_second.reshape(-1, D2),
        feature_third.reshape(-1, D3),
        feature_fourth.reshape(-1, D4),
    )
    gap = jnp.zeros((ROWS, PITCH - TW - 2 * EDGE, left.shape[2]), left.dtype)
    side = jnp.concatenate([right, left, gap], axis=1)

    input_grad, grad2, grad3, grad4, mine, other = tile_pass(
        height,
        width,
        *early,
        block_input,
        side,
        join_weight,
        linear_first,
        linear_second,
        linear_third,
        linear_fourth,
        norm_gain.reshape(1, -1),
        norm_shift.reshape(1, -1),
        expand_weight,
        expand_bias.reshape(1, -1),
        depth_weight,
        depth_bias.reshape(1, -1),
        reduce_weight.T,
        reduce_bias.reshape(1, -1),
    )
    tiles, sums = sum_over_mesh(mine, other, (input_grad, grad2, grad3, grad4))
    input_grad, grad2, grad3, grad4 = tiles
    return (
        input_grad,
        grad2.reshape(TH // 2, TW // 2, D2),
        grad3.reshape(TH // 4, TW // 4, D3),
        grad4,
        *sums,
    )


def solution(mesh):
    tiles = P("row", "col", None)
    return jax.shard_map(
        local,
        mesh=mesh,
        in_specs=(tiles,) + (P(),) * 5 + (tiles,) * 5 + (P(),) * 8,
        out_specs=(tiles,) * 4 + (P(("row", "col")),) + (P(),) * 6,
        check_vma=False,
    )
```

```python
import functools
import math

import jax
import jax.numpy as jnp
from jax import lax
from jax.experimental import pallas as pl
from jax.experimental.pallas import tpu as pltpu
from jax.sharding import PartitionSpec as P

D1 = 64
D2 = 128
D3 = 320
D4 = 512
HID = 256
DEC = 384
TH = 16
TW = 32

EDGE = 4
ROWS = TH + 2 * EDGE
PITCH = 48
USED = 40
COARSE = (128, 32, 8)

XS = 4
NEAR = 16
LINEAR_ROWS = 96
PART_ROWS = LINEAR_ROWS + 16

norm_eps = 1e-06
inv_root_two = 0.7071067811865476
inv_root_tau = 0.3989422804014327


def nt(left, right):
    return lax.dot_general(left, right, (((1,), (1,)), ((), ())), preferred_element_type=jnp.float32)


def tn(left, right):
    return lax.dot_general(left, right, (((0,), (0,)), ((), ())), preferred_element_type=jnp.float32)


def add3(terms):
    return terms[0] + terms[1] + terms[2]


def nn(left, right):
    return jnp.dot(left, right, preferred_element_type=jnp.float32)


def rest_row(n):
    return 8 * (n // 4) + 4 * (n // 2 % 2) + n % 2


def place(position, pitch):
    row = jnp.floor((position + 0.5) * (1.0 / pitch))
    col = position - pitch * row
    if pitch < TW:
        col = jnp.where(col < EDGE, col + TW, col - 2 * EDGE)
    elif pitch > TW:
        col = jnp.where(col < TW + EDGE, col, col - USED)
    return row - EDGE, col


def count_up(shape, axis):
    return lax.broadcasted_iota(jnp.int32, shape, axis).astype(jnp.float32)


def rows_inside(halo, height):
    row_index = lax.axis_index("row")
    above = jnp.where(row_index > 0, 1.0, 0.0)
    below = jnp.where(row_index < height // TH - 1, 1.0, 0.0)
    return [above] * halo + [None] * TH + [below] * halo


def sides_inside(width):
    col_index = lax.axis_index("col")
    before = jnp.where(col_index > 0, 1.0, 0.0)
    after = jnp.where(col_index < width // TW - 1, 1.0, 0.0)
    right = lax.broadcasted_iota(jnp.int32, (2 * EDGE, HID), 0) < EDGE
    return jnp.where(right, after, before)


def normalize(values, gain, shift):
    center = jnp.mean(values, -1, keepdims=True)
    offset = values - center
    spread = jnp.mean(jnp.square(offset), -1, keepdims=True)
    scaling = lax.rsqrt(spread + norm_eps)
    standard = offset * scaling
    return (standard * gain + shift).astype(jnp.bfloat16), standard, scaling


def expand(normed, weight, bias):
    return (nn(normed, weight) + bias).astype(jnp.bfloat16).astype(jnp.float32)


def regroup(channels_last):
    source = lax.broadcasted_iota(jnp.int32, (128, 128), 0)
    target = lax.broadcasted_iota(jnp.int32, (128, 128), 1)
    wanted = (
        (target & 64)
        + 8 * (target & 6)
        + ((target & 32) >> 2)
        + ((target & 24) >> 2)
        + (target & 1)
    )
    moves = jnp.where(source == wanted, 1.0, 0.0).astype(jnp.bfloat16)
    pieces = []
    for first in range(0, channels_last.shape[1], 128):
        piece = channels_last[:, first : first + 128]
        size = piece.shape[1]
        pieces.append(nn(piece, moves[0:size, 0:size]))
    return jnp.concatenate(pieces, axis=1).astype(jnp.bfloat16)


def split_rest(rest):
    axis = rest.ndim - 2
    row = lax.broadcasted_iota(jnp.int32, rest.shape, axis)
    high = rest.astype(jnp.bfloat16).astype(jnp.float32)
    low = jnp.where(row < 2, rest - high, 0.0)
    return jnp.where(row < 2, high, pltpu.roll(low, 4, axis))


def join_rest(rest):
    return rest + pltpu.roll(rest, 4, rest.ndim - 2)


def pool_matrix(scale_index, pitch, row_index, col_index, height, width):
    factor = 2**scale_index
    coarse_rows, coarse_cols = TH // factor, TW // factor
    count = coarse_rows * coarse_cols
    row, col = place(count_up((1, ROWS * pitch), 1), pitch)
    target = count_up((count, 1), 0)
    target_row = jnp.floor((target + 0.5) * (1.0 / coarse_cols))
    target_col = target - coarse_cols * target_row
    row0 = (row_index * TH).astype(jnp.float32)
    col0 = (col_index * TW).astype(jnp.float32)
    at_row = jnp.clip((row + row0 + 0.5) * (1.0 / factor) - 0.5, 0.0, height // factor - 1.0)
    at_col = jnp.clip((col + col0 + 0.5) * (1.0 / factor) - 0.5, 0.0, width // factor - 1.0)
    at_row = at_row - row0 * (1.0 / factor)
    at_col = at_col - col0 * (1.0 / factor)
    weight = jnp.maximum(1.0 - jnp.abs(at_row - target_row), 0.0) * jnp.maximum(
        1.0 - jnp.abs(at_col - target_col), 0.0
    )
    return weight.astype(jnp.bfloat16)


def add_later(projection, linear, later):
    later = later.reshape(-1, D1).astype(jnp.float32)
    return (nt(projection, linear) + later).astype(jnp.bfloat16)


def own_kernel(
    height,
    width,
    joined_ref,
    block_ref,
    later_ref,
    top_ref,
    bottom_ref,
    join_ref,
    first_ref,
    reduce_ref,
    gain_ref,
    shift_ref,
    expand_ref,
    expand_bias_ref,
    feature2_ref,
    feature3_ref,
    feature4_ref,
    pooled_ref,
    side_matrix_ref,
    projection_ref,
    grad_ref,
    act_grad_ref,
    hidden_ref,
    normed_ref,
    standard_ref,
    scaling_ref,
    grouped2_ref,
    grouped3_ref,
    grouped4_ref,
    wide_ref,
):
    row_index = lax.axis_index("row")
    col_index = lax.axis_index("col")
    wide_ref[EDGE : EDGE + TH] = joined_ref[...]
    wide_ref[0:EDGE] = top_ref[:, :, 0:DEC]
    wide_ref[EDGE + TH :] = bottom_ref[:, :, 0:DEC]

    def matrix(pitch):
        return jnp.concatenate(
            [pool_matrix(k, pitch, row_index, col_index, height, width) for k in (1, 2, 3)], axis=0
        )

    pooled_ref[...] = nn(matrix(TW), wide_ref[...].reshape(ROWS * TW, DEC))
    side_matrix_ref[...] = matrix(PITCH - TW)
    projection = nt(wide_ref[3:21].reshape(18 * TW, DEC), join_ref[0:DEC, :]).astype(jnp.bfloat16)
    projection_ref[...] = projection[TW : 17 * TW]
    lanes = slice(DEC + D1, DEC + 2 * D1)
    later = jnp.concatenate(
        [top_ref[3:4, :, lanes], later_ref[...], bottom_ref[0:1, :, lanes]], axis=0
    )
    feature_grad = add_later(projection, first_ref[...], later)
    grad_ref[...] = feature_grad[TW : 17 * TW]
    act_grad_ref[...] = nn(feature_grad, reduce_ref[...]).reshape(18, TW, HID)

    values = jnp.concatenate(
        [top_ref[2:4, :, DEC : DEC + D1], block_ref[...], bottom_ref[0:2, :, DEC : DEC + D1]], axis=0
    )
    normed, standard, scaling = normalize(
        values.reshape(20 * TW, D1).astype(jnp.float32), gain_ref[...], shift_ref[...]
    )
    hidden = expand(normed, expand_ref[...], expand_bias_ref[...])
    hidden = hidden.reshape(20, TW, HID)
    for i, good in enumerate(rows_inside(2, height)):
        hidden_ref[i] = hidden[i] if good is None else hidden[i] * good
    own = slice(2 * TW, 18 * TW)
    normed_ref[...] = normed[own]
    standard_ref[...] = standard[own]
    scaling_ref[...] = jnp.broadcast_to(scaling[own], (TH * TW, D1))
    grouped2_ref[...] = regroup(feature2_ref[...])
    grouped3_ref[...] = regroup(feature3_ref[...])
    grouped4_ref[...] = regroup(feature4_ref[...])


def own_pass(height, width, *operands):
    sds = jax.ShapeDtypeStruct
    bf16, f32 = jnp.bfloat16, jnp.float32
    pixels = TH * TW
    return in_vmem(
        functools.partial(own_kernel, height, width),
        "own_pass",
        (
            sds((sum(COARSE), DEC), f32),
            sds((sum(COARSE), ROWS * (PITCH - TW)), bf16),
            sds((pixels, DEC), bf16),
            sds((pixels, D1), bf16),
            sds((18, TW, HID), f32),
            sds((20, TW, HID), f32),
            sds((pixels, D1), bf16),
            sds((pixels, D1), f32),
            sds((pixels, D1), f32),
            sds((COARSE[0], D2), bf16),
            sds((COARSE[1], D3), bf16),
            sds((COARSE[2], D4), bf16),
        ),
        *operands,
        scratch=[pltpu.VMEM((ROWS, TW, DEC), bf16)],
    )


def tile_kernel(
    height,
    width,
    pooled_ref,
    side_matrix_ref,
    own_projection_ref,
    own_grad_ref,
    own_act_grad_ref,
    own_hidden_ref,
    normed_ref,
    standard_ref,
    scaling_ref,
    feature2_ref,
    feature3_ref,
    feature4_ref,
    block_ref,
    side_ref,
    join_ref,
    first_ref,
    second_ref,
    third_ref,
    fourth_ref,
    gain_ref,
    shift_ref,
    expand_ref,
    expand_bias_ref,
    depth_ref,
    depth_bias_ref,
    reduce_ref,
    reduce_bias_ref,
    input_grad_ref,
    grad2_ref,
    grad3_ref,
    grad4_ref,
    mine_ref,
    other_ref,
    hid_ref,
    slope_ref,
    act_ref,
    pre_ref,
    hgrad_ref,
    linear_ref,
    rest_ref,
):
    row_index = lax.axis_index("row")
    scale_base = 1.0 / math.sqrt(height * width)

    rest_ref[...] = jnp.zeros_like(rest_ref)

    def keep_row(row, value):
        for piece in range(value.shape[1] // 128):
            at = rest_row(row + piece)
            rest_ref[at : at + 1, :] = value[:, 128 * piece : 128 * piece + 128]

    side_joined = side_ref[:, :, 0:DEC].reshape(ROWS * (PITCH - TW), DEC)
    pooled = (pooled_ref[...] + nn(side_matrix_ref[...], side_joined)).astype(jnp.bfloat16)
    start = 0
    base = D1
    for k, linear, feature, grad in (
        (1, second_ref, feature2_ref, grad2_ref),
        (2, third_ref, feature3_ref, grad3_ref),
        (3, fourth_ref, feature4_ref, grad4_ref),
    ):
        count = COARSE[k - 1]
        channels = linear.shape[0]
        projection = nt(pooled[start : start + count], join_ref[k * DEC : (k + 1) * DEC, :]).astype(
            jnp.bfloat16
        )
        grad[...] = nt(projection, linear[...]).astype(jnp.bfloat16)
        linear_ref[base : base + channels, :] = tn(feature[...], projection) * (2**k * scale_base)
        keep_row(
            3 * k,
            jnp.sum(projection.astype(jnp.float32), 0, keepdims=True) * (2**k * scale_base),
        )
        start += count
        base += channels

    values = side_ref[2:22, :, DEC : DEC + D1].astype(jnp.float32)[:, 0 : 2 * EDGE]
    normed, _, _ = normalize(values.reshape(20 * 2 * EDGE, D1), gain_ref[...], shift_ref[...])
    hidden = expand(normed, expand_ref[...], expand_bias_ref[...])
    hid_ref[:, 0:TW] = own_hidden_ref[...]
    hidden = hidden.reshape(20, 2 * EDGE, HID)
    sides = sides_inside(width)
    for i, good in enumerate(rows_inside(2, height)):
        hid_ref[i, TW:] = hidden[i] * (sides if good is None else sides * good)

    def across(before, same, after):
        return pltpu.roll(before, 1, 0) + same + pltpu.roll(after, USED - 1, 0)

    def conv_row(i, carry):
        rows = [hid_ref[i + a] for a in range(3)]
        sums = [
            add3([depth_ref[3 * a + b : 3 * a + b + 1, :] * rows[a] for a in range(3)])
            for b in range(3)
        ]
        conv = across(*sums) + depth_bias_ref[...]
        cumulative = 0.5 * (1.0 + lax.erf(conv * inv_root_two))
        density = inv_root_tau * jnp.exp(-0.5 * conv * conv)
        act_ref[i] = (conv * cumulative)[0:TW].astype(jnp.bfloat16)
        slope_ref[i] = cumulative + conv * density
        return carry

    lax.fori_loop(0, 18, conv_row, 0, unroll=True)

    beside = slice(0, 2 * EDGE)
    projection = nt(
        side_ref[3:21, :, 0:DEC].reshape(18 * (PITCH - TW), DEC), join_ref[0:DEC, :]
    ).astype(jnp.bfloat16)
    feature_grad = add_later(
        projection, first_ref[...], side_ref[3:21, :, DEC + D1 : DEC + 2 * D1]
    )
    act_grad = nn(feature_grad, reduce_ref[...]).reshape(18, PITCH - TW, HID)[:, beside]
    for i, good in enumerate(rows_inside(1, height)):
        for cols, part in ((slice(0, TW), own_act_grad_ref[i]), (slice(TW, USED), act_grad[i])):
            pre_grad = (part * slope_ref[i, cols, :]).astype(jnp.bfloat16).astype(jnp.float32)
            if cols.start:
                pre_grad = pre_grad * sides
            pre_ref[i, cols, :] = pre_grad if good is None else pre_grad * good

    activated = act_ref[1:17].reshape(TH * TW, HID)
    own_projection = own_projection_ref[...]
    own_grad = own_grad_ref[...]
    own_block = block_ref[...].reshape(TH * TW, D1).astype(jnp.float32)
    features = (own_block + (nt(activated, reduce_ref[...]) + reduce_bias_ref[...])).astype(
        jnp.bfloat16
    )
    linear_ref[0:D1, :] = tn(regroup(features), own_projection) * scale_base
    keep_row(0, jnp.sum(own_projection.astype(jnp.float32), 0, keepdims=True) * scale_base)
    reduce_part = tn(own_grad, activated) * scale_base

    def fold(value):
        return jnp.sum(value.reshape(-1, 8, HID), 0)

    def grad_row(i, sums):
        center_row = pre_ref[i + 1, 0:TW, :]
        own_row = jnp.concatenate([center_row, jnp.zeros((USED - TW, HID), jnp.float32)], axis=0)
        rows = [pre_ref[i + 2 - a] for a in range(3)]
        sums_b = [
            add3([depth_ref[3 * a + b : 3 * a + b + 1, :] * rows[a] for a in range(3)])
            for b in range(3)
        ]
        total = across(sums_b[2], sums_b[1], sums_b[0])[0:TW]
        moved = [pltpu.roll(own_row, USED - 1, 0), own_row, pltpu.roll(own_row, 1, 0)]
        taps = []
        for a in range(3):
            hid_row = hid_ref[i + 1 + a]
            for b in range(3):
                taps.append(sums[3 * a + b] + fold(hid_row * moved[b]))
        rounded = total.astype(jnp.bfloat16)
        hgrad_ref[i] = rounded
        taps.append(sums[9] + fold(rounded.astype(jnp.float32)))
        taps.append(sums[10] + fold(center_row))
        return tuple(taps)

    sums = lax.fori_loop(0, TH, grad_row, (jnp.zeros((8, HID), jnp.float32),) * 11, unroll=True)
    for n in range(11):
        keep_row(12 + 2 * n, jnp.sum(sums[n], 0, keepdims=True) * scale_base)

    hidden_grad = hgrad_ref[...].reshape(TH * TW, HID)
    own_standard = standard_ref[...]
    expand_part = tn(normed_ref[...], hidden_grad) * scale_base
    normed_grad = nt(hidden_grad, expand_ref[...])
    fgrad = own_grad.astype(jnp.float32)
    for n, value in enumerate((fgrad, normed_grad * own_standard, normed_grad)):
        at = rest_row(34 + n)
        rest_ref[at : at + 1, 0:D1] = jnp.sum(value, 0, keepdims=True) * scale_base
    scaled = normed_grad * gain_ref[...]
    input_grad = fgrad + scaling_ref[...] * (
        scaled
        - jnp.mean(scaled, -1, keepdims=True)
        - own_standard * jnp.mean(scaled * own_standard, -1, keepdims=True)
    )
    input_grad_ref[...] = input_grad.astype(jnp.bfloat16).reshape(TH, TW, D1)

    even_core = row_index % 2 == 0

    def keep(part, pairs):
        for n in range(0, len(pairs), 2):
            mine = [jnp.where(even_core, even, odd) for even, odd in pairs[n : n + 2]]
            other = [jnp.where(even_core, odd, even) for even, odd in pairs[n : n + 2]]
            if n + 2 == len(pairs):
                other[1] = split_rest(other[1])
            at = slice(8 * n, 8 * n + 16)
            mine_ref[part, at, :] = jnp.concatenate(mine, axis=0)
            other_ref[part, at, :] = jnp.concatenate(other, axis=0).astype(jnp.bfloat16)

    upper = lax.broadcasted_iota(jnp.int32, (8, 128), 0) < 4
    for part in range(NEAR):
        zl, within = part // 8, 8 * (part % 8)
        pairs = []
        for zh in range(4):
            first = 128 * (2 * zh + zl) + within
            for j in range(3):
                lanes = slice(128 * j, 128 * j + 128)
                pairs.append(
                    (
                        linear_ref[first : first + 8, lanes],
                        linear_ref[first + 64 : first + 72, lanes],
                    )
                )
        lanes = slice(0, 128) if part < 8 else slice(128, 256)
        expands = expand_part[within : within + 8, lanes]
        reduces = reduce_part[within : within + 8, lanes]
        pairs.append(
            (
                jnp.where(upper, expands, pltpu.roll(reduces, 4, 0)),
                jnp.where(upper, pltpu.roll(expands, 4, 0), reduces),
            )
        )
        rest = rest_ref[8 * part : 8 * part + 8, :]
        pairs.append((rest, pltpu.roll(rest, 4, 0)))
        keep(part, pairs)


def row_kernel(
    joined_ref, block_ref, later_ref, far_ref, near_ref, joined_buf, block_buf, later_buf, sems
):
    copies = []
    for n, (source, target) in enumerate(
        ((joined_ref, joined_buf), (block_ref, block_buf), (later_ref, later_buf))
    ):
        for last in range(2):
            rows = slice(TH - EDGE, TH) if last else slice(0, EDGE)
            copy = pltpu.make_async_copy(source.at[rows], target.at[last], sems.at[2 * n + last])
            copy.start()
            copies.append(copy)
    for copy in copies:
        copy.wait()
    even = lax.axis_index("row") % 2 == 0
    for buf, lanes in (
        (joined_buf, slice(0, DEC)),
        (block_buf, slice(DEC, DEC + D1)),
        (later_buf, slice(DEC + D1, DEC + 2 * D1)),
    ):
        first = buf[0].astype(jnp.float32)
        last = buf[1].astype(jnp.float32)
        far_ref[:, :, lanes] = jnp.where(even, first, last).astype(jnp.bfloat16)
        near_ref[:, :, lanes] = jnp.where(even, last, first).astype(jnp.bfloat16)


def row_borders(joined, block, later):
    vmem = pl.BlockSpec(memory_space=pltpu.VMEM)
    out = jax.ShapeDtypeStruct((EDGE, TW, DEC + 2 * D1), jnp.bfloat16)
    return pl.pallas_call(
        row_kernel,
        out_shape=(out, out),
        in_specs=[pl.BlockSpec(memory_space=pltpu.HBM)] * 3,
        out_specs=(vmem, vmem),
        scratch_shapes=[pltpu.VMEM((2, EDGE) + a.shape[1:], a.dtype) for a in (joined, block, later)]
        + [pltpu.SemaphoreType.DMA((6,))],
        compiler_params=pltpu.CompilerParams(vmem_limit_bytes=56 * 2**20),
        name="row_borders",
    )(joined, block, later)


def column_kernel(joined_ref, block_ref, later_ref, top_ref, bottom_ref, far_ref, near_ref):
    even = lax.axis_index("col") % 2 == 0
    own_rows = slice(EDGE, EDGE + TH)
    for ref, rows, lanes in (
        (joined_ref, own_rows, slice(0, DEC)),
        (block_ref, own_rows, slice(DEC, DEC + D1)),
        (later_ref, own_rows, slice(DEC + D1, DEC + 2 * D1)),
        (top_ref, slice(0, EDGE), slice(0, DEC + 2 * D1)),
        (bottom_ref, slice(EDGE + TH, ROWS), slice(0, DEC + 2 * D1)),
    ):
        first = ref[:, 0:16].astype(jnp.float32)[:, 0:EDGE]
        last = ref[:, TW - 16 : TW].astype(jnp.float32)[:, 16 - EDGE : 16]
        far_ref[rows, :, lanes] = jnp.where(even, first, last).astype(jnp.bfloat16)
        near_ref[rows, :, lanes] = jnp.where(even, last, first).astype(jnp.bfloat16)


def tile_pass(height, width, *operands):
    sds = jax.ShapeDtypeStruct
    bf16, f32 = jnp.bfloat16, jnp.float32
    vmem = pltpu.VMEM
    return pl.pallas_call(
        functools.partial(tile_kernel, height, width),
        out_shape=(
            sds((TH, TW, D1), bf16),
            sds((COARSE[0], D2), bf16),
            sds((COARSE[1], D3), bf16),
            sds((COARSE[2], D4), bf16),
            sds((NEAR, PART_ROWS, 128), f32),
            sds((NEAR, PART_ROWS, 128), bf16),
        ),
        in_specs=[pl.BlockSpec(memory_space=vmem)] * len(operands),
        out_specs=(pl.BlockSpec(memory_space=vmem),) * 6,
        scratch_shapes=[
            vmem((20, USED, HID), f32),
            vmem((18, USED, HID), f32),
            vmem((18, TW, HID), bf16),
            vmem((18, USED, HID), f32),
            vmem((TH, TW, HID), bf16),
            vmem((D1 + D2 + D3 + D4, DEC), f32),
            vmem((128, 128), f32),
        ],
        compiler_params=pltpu.CompilerParams(vmem_limit_bytes=28 * 2**20),
        name="tile_pass",
    )(*operands)


def near_kernel(received_ref, out_ref):
    total = jnp.sum(received_ref[...].astype(jnp.float32), 0)
    share = total[LINEAR_ROWS : LINEAR_ROWS + 8]
    rest = total[LINEAR_ROWS + 8 :]
    rest = pltpu.roll(join_rest(rest), 6, 0)
    row = lax.broadcasted_iota(jnp.int32, (8, 128), 0)
    for zh in range(4):
        pieces = [total[24 * zh + 8 * j : 24 * zh + 8 * j + 8] for j in range(3)]
        for yh in range(4):
            part = rest
            for j in range(3):
                shift = (2 * j - 2 * yh) % 8
                moved = pltpu.roll(pieces[j], shift, 0) if shift else pieces[j]
                part = jnp.where((row >= 2 * j) & (row < 2 * j + 2), moved, part)
            out_ref[4 * zh + yh, 0:8, :] = part
            out_ref[4 * zh + yh, 8:16, :] = share


def final_kernel(received_ref, out_ref):
    total = jnp.sum(received_ref[...], 0)
    for n in range(out_ref.shape[0]):
        for i in range(4):
            out_ref[n, i] = total[8 + 2 * i : 10 + 2 * i]
        out_ref[n, 4] = total[6:8]


def result_kernel(
    all_ref,
    received_ref,
    input_grad,
    grad2,
    grad3,
    grad4,
    input_out,
    out2,
    out3,
    out4,
    linear_ref,
    biases_ref,
    expand_ref,
    reduce_ref,
    depth_ref,
    hidden_ref,
    channel_ref,
):
    input_out[...] = input_grad[...]
    out2[...] = grad2[...]
    out3[...] = grad3[...]
    last = grad4[...].astype(jnp.float32)
    for i in range(out4.shape[0]):
        out4[i] = last[4 * i : 4 * i + 4].astype(jnp.bfloat16)
    total = jnp.sum(received_ref[:, 0:8, :], 0)
    for p in range(2):
        for j in range(3):
            linear_ref[3 * p + j : 3 * p + j + 1, :] = total[2 * j + p : 2 * j + p + 1, :]

    for share in range(2 * NEAR):
        lanes = slice(0, 128) if share < NEAR else slice(128, 256)
        first = 4 * (share % NEAR)
        for i in range(2):
            rows = slice(first + 2 * i, first + 2 * i + 2)
            expand_ref[rows, lanes] = all_ref[share, i]
            reduce_ref[rows, lanes] = all_ref[share, 2 + i]

    def row(n):
        return all_ref[n // 2, 4, n % 2 : n % 2 + 1, :]

    for k in range(4):
        for j in range(3):
            biases_ref[k : k + 1, 128 * j : 128 * j + 128] = row(3 * k + j)
    for t in range(9):
        for j in range(2):
            depth_ref[t : t + 1, 128 * j : 128 * j + 128] = row(12 + 2 * t + j)
    for t in range(2):
        for j in range(2):
            hidden_ref[t : t + 1, 128 * j : 128 * j + 128] = row(30 + 2 * t + j)
    for t in range(3):
        channel_ref[t : t + 1, :] = row(34 + t)[:, 0:D1]


def in_vmem(kernel, name, out_shape, *operands, scratch=()):
    vmem = pl.BlockSpec(memory_space=pltpu.VMEM)
    return pl.pallas_call(
        kernel,
        out_shape=out_shape,
        in_specs=[vmem] * len(operands),
        out_specs=jax.tree.map(lambda _: vmem, out_shape),
        scratch_shapes=scratch,
        compiler_params=pltpu.CompilerParams(vmem_limit_bytes=16 * 2**20),
        name=name,
    )(*operands)


def chip_kernel(mine_ref, received_ref, out_ref):
    plain = LINEAR_ROWS + 8
    received = received_ref[...].astype(jnp.float32)
    total = mine_ref[:, 0:plain, :] + received[:, 0:plain]
    rest = split_rest(mine_ref[:, plain:, :] + join_rest(received[:, plain:]))
    out_ref[...] = jnp.concatenate([total, rest], axis=1).astype(jnp.bfloat16)


def device_groups(chips, cols):
    half_z, half_y = range(chips // 2), range(cols // XS // 2)
    two, xs = range(2), range(XS)

    def device(zh, zl, core, yh, yl, x):
        return (2 * (2 * zh + zl) + core) * cols + XS * (2 * yh + yl) + x

    near = [
        [device(zh, zl, core, yh, yl, x) for zl in two for yl in two for x in xs]
        for core in two
        for zh in half_z
        for yh in half_y
    ]
    far = [
        [device(zh, zl, core, yh, yl, x) for zh in half_z for yh in half_y]
        for core in two
        for zl in two
        for yl in two
        for x in xs
    ]
    both = [
        [device(zh, zl, core, yh, yl, x) for zl in two for yl in two for x in xs for core in two]
        for zh in half_z
        for yh in half_y
    ]
    return near, far, both


def sum_over_mesh(mine, other, grads):
    rows = lax.axis_size("row")
    cols = lax.axis_size("col")
    sds = jax.ShapeDtypeStruct
    f32 = jnp.float32
    near, far, both = device_groups(rows // 2, cols)

    def exchange(parts, groups):
        return lax.all_to_all(parts, ("row", "col"), 0, 0, tiled=True, axis_index_groups=groups)

    received = lax.ppermute(other, "row", [(i, i ^ 1) for i in range(rows)])
    chip = in_vmem(chip_kernel, "chip_sums", sds(other.shape, other.dtype), mine, received)
    parts = in_vmem(near_kernel, "near_sums", sds((16, 16, 128), f32), exchange(chip, near))
    received = exchange(parts, far)
    share = in_vmem(final_kernel, "final_sums", sds((2 * NEAR, 5, 2, 128), f32), received)
    everything = exchange(share, both)
    *tiles, linear, biases, expand, reduce, depth, hidden, channel = in_vmem(
        result_kernel,
        "results",
        (
            *(sds(grad.shape, grad.dtype) for grad in grads[:3]),
            sds((TH // 8, TW // 8, D4), jnp.bfloat16),
            sds((6, 128), f32),
            sds((4, DEC), f32),
            sds((D1, HID), f32),
            sds((D1, HID), f32),
            sds((9, HID), f32),
            sds((2, HID), f32),
            sds((3, D1), f32),
        ),
        everything,
        received,
        *grads,
    )
    return tiles, (linear.reshape(-1), biases, expand, reduce.T, depth, hidden, channel)


def swap_edges(to_far, to_near, axis):
    devices = lax.axis_size(axis)
    even = lax.axis_index(axis) % 2 == 0
    near = [(i, i ^ 1) for i in range(devices)]
    far = [(i, i + 1) for i in range(1, devices - 1, 2)]
    far = far + [(j, i) for i, j in far]
    from_far = lax.ppermute(to_far, axis, far)
    from_near = lax.ppermute(to_near, axis, near)
    return jnp.where(even, from_far, from_near), jnp.where(even, from_near, from_far)


def local(
    joined_grad,
    join_weight,
    linear_first,
    linear_second,
    linear_third,
    linear_fourth,
    feature_second,
    feature_third,
    feature_fourth,
    block_input,
    later_grad,
    norm_gain,
    norm_shift,
    expand_weight,
    expand_bias,
    depth_weight,
    depth_bias,
    reduce_weight,
    reduce_bias,
):
    height = TH * lax.axis_size("row")
    width = TW * lax.axis_size("col")
    top, bottom = swap_edges(*row_borders(joined_grad, block_input, later_grad), "row")
    column = jax.ShapeDtypeStruct((ROWS, EDGE, DEC + 2 * D1), jnp.bfloat16)
    left, right = swap_edges(
        *in_vmem(
            column_kernel,
            "column_borders",
            (column, column),
            joined_grad,
            block_input,
            later_grad,
            top,
            bottom,
        ),
        "col",
    )
    early = own_pass(
        height,
        width,
        joined_grad,
        block_input,
        later_grad,
        top,
        bottom,
        join_weight,
        linear_first,
        reduce_weight.T,
        norm_gain.reshape(1, -1),
        norm_shift.reshape(1, -1),
        expand_weight,
        expand_bias.reshape(1, -1),
        feature_second.reshape(-1, D2),
        feature_third.reshape(-1, D3),
        feature_fourth.reshape(-1, D4),
    )
    gap = jnp.zeros((ROWS, PITCH - TW - 2 * EDGE, left.shape[2]), left.dtype)
    side = jnp.concatenate([right, left, gap], axis=1)

    input_grad, grad2, grad3, grad4, mine, other = tile_pass(
        height,
        width,
        *early,
        block_input,
        side,
        join_weight,
        linear_first,
        linear_second,
        linear_third,
        linear_fourth,
        norm_gain.reshape(1, -1),
        norm_shift.reshape(1, -1),
        expand_weight,
        expand_bias.reshape(1, -1),
        depth_weight,
        depth_bias.reshape(1, -1),
        reduce_weight.T,
        reduce_bias.reshape(1, -1),
    )
    tiles, sums = sum_over_mesh(mine, other, (input_grad, grad2, grad3, grad4))
    input_grad, grad2, grad3, grad4 = tiles
    return (
        input_grad,
        grad2.reshape(TH // 2, TW // 2, D2),
        grad3.reshape(TH // 4, TW // 4, D3),
        grad4,
        *sums,
    )


def solution(mesh):
    tiles = P("row", "col", None)
    return jax.shard_map(
        local,
        mesh=mesh,
        in_specs=(tiles,) + (P(),) * 5 + (tiles,) * 5 + (P(),) * 8,
        out_specs=(tiles,) * 4 + (P(("row", "col")),) + (P(),) * 6,
        check_vma=False,
    )
```
